32 devices in a mesh: seq: 8 (over y, x, core), ch: 4 (over z).
Axes of the slice: x: 2, y: 2, z: 4, core: 2. Of those that a mesh axis runs over, the one named last changes fastest.
Arguments:
- inputs: bfloat16 [4, 2048, 1536], P(None, 'seq'), may hold values from -6 to 6
- lengths: int32 [4], replicated, may hold values from 512 to 2048, as said below
- norm1_gain: bfloat16 [1536], P('seq'), may hold values from 0.5 to 1.5
- w_in_x: bfloat16 [1536, 3072], P('seq', 'ch'), may hold values from -0.15625 to 0.15625
- w_in_z: bfloat16 [1536, 3072], P('seq', 'ch'), may hold values from -0.15625 to 0.15625
- conv_w: float32 [4, 3072], P(None, 'ch'), may hold values from -3 to 3
- conv_b: float32 [3072], P('ch'), may hold values from -3 to 3
- w_xproj: bfloat16 [3072, 128], P('ch'), may hold values from -0.109375 to 0.109375
- dt_gain: float32 [96], replicated, may hold values from 0.5 to 1.5
- b_gain: float32 [16], replicated, may hold values from 0.5 to 1.5
- c_gain: float32 [16], replicated, may hold values from 0.5 to 1.5
- w_dt: bfloat16 [96, 3072], P(None, 'ch'), may hold values from -0.625 to 0.625
- dt_bias: float32 [3072], P('ch'), may hold values from -3 to -1
- decay_log: float32 [16, 3072], P(None, 'ch'), may hold values from -7 to -1
- skip_d: float32 [3072], P('ch'), may hold values from -5 to 5
- w_out: bfloat16 [3072, 1536], P('ch', 'seq'), may hold values from -0.109375 to 0.109375
- norm2_gain: bfloat16 [1536], P('seq'), may hold values from 0.5 to 1.5
- w_gate: bfloat16 [1536, 4096], P('seq', 'ch'), may hold values from -0.15625 to 0.15625
- w_up: bfloat16 [1536, 4096], P('seq', 'ch'), may hold values from -0.15625 to 0.15625
- w_down: bfloat16 [4096, 1536], P('ch', 'seq'), may hold values from -0.09375 to 0.09375
- cotangent: bfloat16 [4, 2048, 1536], P(None, 'seq'), may hold values from -6 to 6
Outputs:
- block_out: float32 [4, 2048, 1536], P(None, 'seq')
- grad_inputs: float32 [4, 2048, 1536], P(None, 'seq')
- grad_norm1_gain: float32 [1536], P('seq')
- grad_w_in_x: float32 [1536, 3072], P('seq', 'ch')
- grad_w_in_z: float32 [1536, 3072], P('seq', 'ch')
- grad_conv_w: float32 [4, 3072], P(None, 'ch')
- grad_conv_b: float32 [3072], P('ch')
- grad_w_xproj: float32 [3072, 128], P('ch')
- grad_dt_gain: float32 [96], replicated
- grad_b_gain: float32 [16], replicated
- grad_c_gain: float32 [16], replicated
- grad_w_dt: float32 [96, 3072], P(None, 'ch')
- grad_dt_bias: float32 [3072], P('ch')
- grad_decay_log: float32 [16, 3072], P(None, 'ch')
- grad_skip_d: float32 [3072], P('ch')
- grad_w_out: float32 [3072, 1536], P('ch', 'seq')
- grad_norm2_gain: float32 [1536], P('seq')
- grad_w_gate: float32 [1536, 4096], P('seq', 'ch')
- grad_w_up: float32 [1536, 4096], P('seq', 'ch')
- grad_w_down: float32 [4096, 1536], P('ch', 'seq')
The draws below stay inside these ranges and needn't reach their ends.
Inputs may be any that keep to these rules, and one draw needn't show every extreme that they name: `lengths`: each micro-batch's length lies in the stated range and at least one micro-batch fills all 2048 slots.
All inputs are finite; a program needn't handle non-finite values.
Results may differ from the reference program's by a relative error of at most 0.028.
Values may be sent and summed in bfloat16 or wider, within the bound.
No kernel may reach another device: no remote copies, remote signals or barrier semaphores. Data moves between devices by JAX's collectives and lax.ppermute only.
A program may use at most 320 MiB of HBM per device.

```python
import jax
import jax.numpy as jnp
from jax import lax

D = 1536
INNER = 3072
NST = 16
CONV = 4
RANK = 96
FF = 4096
MB = 4
TOK = 256
SEQ_LEN = 2048
PROJ = 128


def draw_lengths(key, part):
    first_key, second_key = jax.random.split(jax.random.fold_in(key, 17))
    drawn = jax.random.randint(first_key, (MB,), SEQ_LEN // 4, SEQ_LEN + 1)
    filled = jax.random.randint(second_key, (), 0, MB)
    return jnp.where(jnp.arange(MB) == filled, SEQ_LEN, drawn).astype(jnp.int32)


def draw_skip_d(key, part):
    key = jax.random.fold_in(key, 29)
    size_key = jax.random.fold_in(key, 0)
    return jax.random.uniform(size_key, (INNER,), jnp.float32, -1.0, 3.0)


def levels(own_key, dims, pieces, smallest, top_value):
    loudness, own = 1.0, jax.random.fold_in(own_key, 6)
    for position, shards_of in pieces:
        draws = jnp.exp(jax.random.uniform(jax.random.fold_in(own, position), (shards_of,), jnp.float32, smallest / len(pieces), top_value / len(pieces)))
        loudness = loudness * jnp.repeat(draws, dims[position] // shards_of).reshape([-1 if axis == position else 1 for axis in range(len(dims))])
    return loudness


def noise(own_key, dims, spread, bound, cuts=(), held_as=jnp.bfloat16):
    values = jax.random.normal(own_key, dims, jnp.float32) * spread
    if len(cuts) > 0:
        values = levels(own_key, dims, cuts, -0.22, 0.18) * values
    return jnp.clip(values, min=-bound, max=bound).astype(held_as)


def setup_inputs(seed: int = 0) -> dict:
    streams_of = jax.random.split(jax.random.key(seed), 22)
    inputs = noise(streams_of[0], (MB, SEQ_LEN, D), 1.0, 6.0, ((1, 8),))
    lengths = draw_lengths(jax.random.fold_in(streams_of[21], 71), 0)
    norm1_gain = jnp.clip(1.0 + 0.1 * jax.random.normal(streams_of[2], (D,), jnp.float32), 0.5, 1.5).astype(jnp.bfloat16)
    w_in_x = noise(streams_of[3], (D, INNER), D ** -0.5, 0.15625, ((0, 8), (1, 4)))
    w_in_z = noise(streams_of[4], (D, INNER), D ** -0.5, 0.15625, ((0, 8), (1, 4)))
    conv_w = noise(streams_of[5], (CONV, INNER), CONV ** -0.5, 3.0, ((1, 4),), jnp.float32)
    conv_b = noise(streams_of[6], (INNER,), 0.5, 3.0, ((0, 4),), jnp.float32)
    w_xproj = noise(streams_of[7], (INNER, PROJ), INNER ** -0.5, 0.109375, ((0, 4),))
    dt_gain = jnp.clip(1.0 + 0.1 * jax.random.normal(streams_of[8], (RANK,), jnp.float32), 0.5, 1.5)
    b_gain = jnp.clip(1.0 + 0.1 * jax.random.normal(streams_of[9], (NST,), jnp.float32), 0.5, 1.5)
    c_gain = jnp.clip(1.0 + 0.1 * jax.random.normal(streams_of[10], (NST,), jnp.float32), 0.5, 1.5)
    w_dt = noise(streams_of[11], (RANK, INNER), RANK ** -0.5, 0.625, ((1, 4),))
    dt_bias = jnp.clip(-3.0 + 2.0 * jax.random.uniform(streams_of[12], (INNER,), jnp.float32) ** levels(streams_of[12], (INNER,), ((0, 4),), -0.2, 0.2), -3.0, -1.0)
    decay_log = jnp.clip(-7.0 + 6.0 * jax.random.uniform(streams_of[13], (NST, INNER), jnp.float32) ** levels(streams_of[13], (NST, INNER), ((1, 4),), -0.2, 0.2), -7.0, -1.0)
    skip_d = draw_skip_d(jax.random.fold_in(streams_of[21], 71), 0)
    w_out = noise(streams_of[15], (INNER, D), INNER ** -0.5, 0.109375, ((0, 4), (1, 8)))
    norm2_gain = jnp.clip(1.0 + 0.1 * jax.random.normal(streams_of[16], (D,), jnp.float32), 0.5, 1.5).astype(jnp.bfloat16)
    w_gate = noise(streams_of[17], (D, FF), D ** -0.5, 0.15625, ((0, 8), (1, 4)))
    w_up = noise(streams_of[18], (D, FF), D ** -0.5, 0.15625, ((0, 8), (1, 4)))
    w_down = noise(streams_of[19], (FF, D), FF ** -0.5, 0.09375, ((0, 4), (1, 8)))
    cotangent = noise(streams_of[20], (MB, SEQ_LEN, D), 1.0, 6.0, ((1, 8),))
    return dict(inputs=inputs, lengths=lengths, norm1_gain=norm1_gain, w_in_x=w_in_x, w_in_z=w_in_z, conv_w=conv_w, conv_b=conv_b, w_xproj=w_xproj, dt_gain=dt_gain, b_gain=b_gain, c_gain=c_gain, w_dt=w_dt, dt_bias=dt_bias, decay_log=decay_log, skip_d=skip_d, w_out=w_out, norm2_gain=norm2_gain, w_gate=w_gate, w_up=w_up, w_down=w_down, cotangent=cotangent)


EPS = 1e-05

@jax.custom_vjp
def low(v):
    return lax.optimization_barrier(v.astype(jnp.bfloat16)).astype(jnp.float32)

@jax.custom_vjp
def low_back(v):
    return v

def low_keep(v):
    return (low(v), None)

def low_pass(kept, grad):
    return (grad,)

def back_keep(v):
    return (v, None)

def back_low(kept, grad):
    return (low(grad),)
low.defvjp(low_keep, low_pass)
low_back.defvjp(back_keep, back_low)

def norm_rows(value, gain):
    return value * lax.rsqrt(lax.optimization_barrier(jnp.mean(value * value, axis=-1, keepdims=True)) + EPS) * gain

def matmul(left, right):
    return jnp.dot(left, right, precision=lax.Precision.HIGHEST, preferred_element_type=jnp.float32)

def linear_pair(first, second):
    return (first[0] * second[0], second[0] * first[1] + second[1])

def selective(step_size, b_norm, c_norm, mixed, decay_rate):
    blocks = SEQ_LEN // TOK

    def block_step(state, member):
        step_blk, b_blk, c_blk, u_blk = member
        factor = jnp.exp(step_blk[:, None, :] * decay_rate[None])
        drive_term = step_blk[:, None, :] * b_blk[:, :, None] * u_blk[:, None, :]
        cum_factor, local_state = lax.associative_scan(linear_pair, (factor, drive_term), axis=0)
        states = local_state + cum_factor * state[None]
        return (states[-1], lax.optimization_barrier(jnp.sum(c_blk[:, :, None] * states, axis=1)))
    members = (step_size.reshape(blocks, TOK, INNER), b_norm.reshape(blocks, TOK, NST), c_norm.reshape(blocks, TOK, NST), mixed.reshape(blocks, TOK, INNER))
    unused, outputs = lax.scan(jax.checkpoint(block_step), jnp.zeros((NST, INNER), jnp.float32), members)
    return outputs.reshape(SEQ_LEN, INNER)

def sequence(source, live_mask, params):
    gain_one, w_in_x, w_in_z, conv_w, conv_b, w_xproj, dt_gain, b_gain, c_gain, w_dt, dt_bias, decay_log, skip_d, w_out, gain_two, w_gate, w_up, w_down = params
    normed_one = low(norm_rows(source, gain_one))
    xs_val = low(low_back(matmul(normed_one, w_in_x)))
    z_gate = low_back(matmul(normed_one, w_in_z))
    padded = jnp.concatenate([jnp.zeros((CONV - 1, INNER), jnp.float32), xs_val], axis=0)
    conv_out = conv_b + jnp.zeros((SEQ_LEN, INNER), jnp.float32)
    for offset in range(CONV):
        conv_out = conv_out + conv_w[offset] * padded[offset:offset + SEQ_LEN]
    mixed = low(jax.nn.silu(conv_out))
    projected = low_back(matmul(mixed, w_xproj))
    step_norm = low(norm_rows(projected[:, :RANK], dt_gain))
    b_norm = norm_rows(projected[:, RANK:RANK + NST], b_gain)
    c_norm = norm_rows(projected[:, RANK + NST:], c_gain)
    step_pre = low_back(matmul(step_norm, w_dt) + dt_bias)
    step_size = jax.nn.softplus(step_pre) * live_mask[:, None]
    decay_rate = -jnp.exp(decay_log)
    inner_out = selective(step_size, b_norm, c_norm, mixed, decay_rate) + skip_d * mixed
    gated_val = low(inner_out * jax.nn.silu(z_gate))
    middle = source + low_back(matmul(gated_val, w_out))
    normed_two = low(norm_rows(middle, gain_two))
    gate_pre = low_back(matmul(normed_two, w_gate))
    up_pre = low_back(matmul(normed_two, w_up))
    hidden = low(jax.nn.silu(gate_pre) * up_pre)
    return middle + low_back(matmul(hidden, w_down))

def reference(inputs, lengths, norm1_gain, w_in_x, w_in_z, conv_w, conv_b, w_xproj, dt_gain, b_gain, c_gain, w_dt, dt_bias, decay_log, skip_d, w_out, norm2_gain, w_gate, w_up, w_down, cotangent):
    params = tuple((value.astype(jnp.float32) for value in (norm1_gain, w_in_x, w_in_z, conv_w, conv_b, w_xproj, dt_gain, b_gain, c_gain, w_dt, dt_bias, decay_log, skip_d, w_out, norm2_gain, w_gate, w_up, w_down)))
    positions = jnp.arange(SEQ_LEN, dtype=jnp.int32)
    live_mask = (positions[None, :] < lengths[:, None].astype(jnp.int32)).astype(jnp.float32)
    source = inputs.astype(jnp.float32)

    def whole(source, params):

        def one_sequence(member):
            return sequence(member[0], member[1], params)
        return lax.map(jax.checkpoint(one_sequence), (source, live_mask))
    block_out, pull_back = jax.vjp(whole, source, params)
    grad_inputs, grad_params = pull_back(cotangent.astype(jnp.float32) * live_mask[:, :, None])
    return (block_out, grad_inputs) + tuple(grad_params)
```

```python
import functools

import jax
import jax.numpy as jnp
from jax import lax
from jax.experimental import pallas as pl
from jax.experimental.pallas import tpu as pltpu
from jax.sharding import PartitionSpec as P

EPS = 1e-05
LOG2E = 1.4426950408889634
LANE = 128
CHUNKS = 8
UNROLL = 4
GROUPS = 4
F32 = jnp.float32
BF16 = jnp.bfloat16
VMEM_LIMIT = 48 * 1024 * 1024


def tree_sum(parts):
    parts = list(parts)
    while len(parts) > 1:
        parts = [
            parts[i] + parts[i + 1] if i + 1 < len(parts) else parts[i]
            for i in range(0, len(parts), 2)
        ]
    return parts[0]


def dot(left, right):
    return jnp.dot(left, right, preferred_element_type=F32)


def dot_nt(left, right):
    return lax.dot_general(left, right, (((1,), (1,)), ((), ())), preferred_element_type=F32)


def dot_tn(left, right):
    return lax.dot_general(left, right, (((0,), (0,)), ((), ())), preferred_element_type=F32)


def sigmoid(value):
    return 1.0 / (1.0 + jnp.exp(-value))


def split_low(value):
    high = value.astype(BF16)
    rest = (value - high.astype(F32)).astype(BF16)
    return jnp.concatenate([high, rest], axis=1)


def segment_rows(value, rank, states):
    lane = lax.broadcasted_iota(jnp.int32, value.shape, 1)
    first = lane < rank
    last = lane >= rank + states
    middle = jnp.logical_not(jnp.logical_or(first, last))
    means = []
    for mask, count in ((first, rank), (middle, states), (last, states)):
        means.append(jnp.sum(jnp.where(mask, value, 0.0), axis=1, keepdims=True) / count)
    return jnp.where(first, means[0], jnp.where(last, means[2], means[1]))


def load_padded(pad_ref, edge_ref, xs_ref, tok):
    pad_ref[0:8, :] = edge_ref[0].astype(F32)
    pad_ref[8 : 8 + tok, :] = xs_ref[0].astype(F32)


def conv_of(pad_ref, conv_w, conv_b, tok, taps):
    out = conv_b
    for k in range(taps):
        start = 8 - (taps - 1) + k
        out = out + conv_w[k : k + 1, :] * pad_ref[start : start + tok, :]
    return out


def to_scan_order(value, tmp_ref, dst_ref):
    tok, chans = value.shape
    steps = tok // CHUNKS
    for j in range(chans // LANE):
        tmp_ref[j] = value[:, col(j)]
        for t in range(steps):
            dst_ref[8 * t : 8 * t + 8, col(j)] = tmp_ref[j, pl.ds(t, 8, stride=steps), :]


def to_natural_order(value, tmp_ref, dst_ref):
    tok, chans = value.shape
    steps = tok // CHUNKS
    for j in range(chans // LANE):
        tmp_ref[j] = value[:, col(j)]
        for k in range(CHUNKS):
            for t in range(0, steps, 8):
                dst_ref[k * steps + t : k * steps + t + 8, col(j)] = tmp_ref[
                    j, pl.ds(8 * t + k, 8, stride=8), :
                ]


def pre_kernel(xs_ref, edge_ref, cw_ref, cb_ref, wxp_ref, u_ref, proj_ref, pad, nat, per):
    tok, taps = xs_ref.shape[1], cw_ref.shape[0]
    load_padded(pad, edge_ref, xs_ref, tok)
    conv = conv_of(pad, cw_ref[...], cb_ref[...], tok, taps)
    to_scan_order(conv * sigmoid(conv), nat, per)
    u_low = per[...].astype(BF16)
    u_ref[0] = u_low
    proj_ref[0] = dot(u_low, wxp_ref[...])


def lanes_at(j):
    return pl.ds(pl.multiple_of(j * LANE, LANE), LANE)


def rows_at(t):
    return pl.ds(pl.multiple_of(t * 8, 8), 8)


def col(n):
    return slice(n * LANE, (n + 1) * LANE)


def chunk_prefix(prod, value, backwards):
    place = lax.broadcasted_iota(jnp.int32, value.shape, 0)
    for step in (1, 2, 4):
        shift = CHUNKS - step if backwards else step
        keep = place < CHUNKS - step if backwards else place >= step
        prod_far = jnp.where(keep, pltpu.roll(prod, shift, 0), 1.0)
        value_far = jnp.where(keep, pltpu.roll(value, shift, 0), 0.0)
        value = prod * value_far + value
        prod = prod * prod_far
    return value


def sum_prefix(value):
    place = lax.broadcasted_iota(jnp.int32, value.shape, 0)
    for step in (1, 2, 4):
        value = value + jnp.where(place >= step, pltpu.roll(value, step, 0), 0.0)
    return value


def state_kernel(
    cnt_ref, proj_ref, u_ref, wdt_ref, bias_ref, gain_ref, dec_ref, eb_ref,
    delta_ref, normed_ref, sn_ref, einc_ref, csd_ref, pay_ref, bb, du,
    *, rank, states,
):
    tok, chans = u_ref.shape[1], u_ref.shape[2]
    steps = tok // CHUNKS
    value = proj_ref[0]
    scale = lax.rsqrt(segment_rows(value * value, rank, states) + EPS)
    normed = value * scale * gain_ref[...]
    normed_ref[0] = normed
    lane = lax.broadcasted_iota(jnp.int32, value.shape, 1)
    step_low = jnp.where(lane < rank, normed, 0.0).astype(BF16)
    sn_ref[0] = step_low
    pre = dot(step_low, wdt_ref[...]) + bias_ref[...]
    row = lax.broadcasted_iota(jnp.int32, pre.shape, 0)
    place = (row & 7) * steps + (row >> 3)
    live = place < cnt_ref[pl.program_id(0)]
    soft = jnp.maximum(pre, 0.0) + jnp.log(1.0 + jnp.exp(-jnp.abs(pre)))
    delta = jnp.where(live, soft, 0.0)
    delta_ref[0] = delta
    du[...] = delta * u_ref[0].astype(F32)
    bb[...] = dot(split_low(normed), eb_ref[...])

    def tile(j, carry):
        lanes = lanes_at(j)
        dec = [dec_ref[8 * n : 8 * n + 8, lanes] for n in range(states)]

        def step(i, carry):
            ends, total = carry
            for q in range(UNROLL):
                rows = rows_at(i * UNROLL + q)
                d = delta_ref[0, rows, lanes]
                v = du[rows, lanes]
                ends = tuple(
                    jnp.exp2(d * dec[n]) * ends[n] + v * bb[rows, col(n)] for n in range(states)
                )
                total = total + d
            return ends, total

        zero = jnp.zeros((8, LANE), F32)
        ends, total = lax.fori_loop(0, steps // UNROLL, step, ((zero,) * states, zero))
        csd = sum_prefix(total)
        csd_ref[0, :, lanes] = csd
        for n in range(states):
            inc = chunk_prefix(jnp.exp2(dec[n] * total), ends[n], False)
            einc_ref[0, 8 * n : 8 * n + 8, lanes] = inc
            pay_ref[0, n : n + 1, lanes] = inc[7:8, :]
        pay_ref[0, states : states + 8, lanes] = jnp.broadcast_to(csd[7:8, :], (8, LANE))
        return carry

    lax.fori_loop(0, chans // LANE, tile, 0)


def start_states(dec, csd, einc_ref, enter_ref, lanes, states):
    place = lax.broadcasted_iota(jnp.int32, csd.shape, 0)
    before = jnp.where(place >= 1, pltpu.roll(csd, 1, 0), 0.0)
    out = []
    for n in range(states):
        own = jnp.where(place >= 1, pltpu.roll(einc_ref[0, 8 * n : 8 * n + 8, lanes], 1, 0), 0.0)
        out.append(own + jnp.exp2(dec[n] * before) * enter_ref[0, n : n + 1, lanes])
    return tuple(out)


def out_kernel(
    delta_ref, u_ref, normed_ref, dec_ref, einc_ref, csd_ref, enter_ref, z_ref, skip_ref, eb_ref,
    inner_ref, gated_ref, bc, du, per, tmp, *, states,
):
    tok, chans = u_ref.shape[1], u_ref.shape[2]
    steps = tok // CHUNKS
    bc[...] = dot(split_low(normed_ref[0]), eb_ref[...])
    u_val = u_ref[0].astype(F32)
    du[...] = delta_ref[0] * u_val
    per[...] = skip_ref[...] * u_val

    def tile(j, carry):
        lanes = lanes_at(j)
        dec = [dec_ref[8 * n : 8 * n + 8, lanes] for n in range(states)]

        def step(i, hs):
            for q in range(UNROLL):
                rows = rows_at(i * UNROLL + q)
                d = delta_ref[0, rows, lanes]
                v = du[rows, lanes]
                hs = tuple(
                    jnp.exp2(d * dec[n]) * hs[n] + v * bc[rows, col(n)] for n in range(states)
                )
                per[rows, lanes] += tree_sum(
                    hs[n] * bc[rows, col(states + n)] for n in range(states)
                )
            return hs

        first = start_states(dec, csd_ref[0, :, lanes], einc_ref, enter_ref, lanes, states)
        lax.fori_loop(0, steps // UNROLL, step, first)
        return carry

    lax.fori_loop(0, chans // LANE, tile, 0)
    to_natural_order(per[...], tmp, du)
    inner = du[...]
    inner_ref[0] = inner
    z_val = z_ref[0].astype(F32)
    gated_ref[0] = (inner * z_val * sigmoid(z_val)).astype(BF16)


def back_state_kernel(
    gg_ref, z_ref, inner_ref, delta_ref, u_ref, normed_ref, dec_ref, skip_ref, ec_ref,
    gin_ref, gz_ref, sinc_ref, pay_ref, gskip_ref, cb, nat, *, states,
):
    tok, chans = u_ref.shape[1], u_ref.shape[2]
    steps = tok // CHUNKS
    cb[...] = dot(split_low(normed_ref[0]), ec_ref[...])
    gg = gg_ref[0].astype(F32)
    z_val = z_ref[0].astype(F32)
    sig = sigmoid(z_val)
    gin = gin_ref.at[0]
    to_scan_order(gg * z_val * sig, nat, gin)
    gz_ref[0] = (gg * inner_ref[0] * sig * (1.0 + z_val * (1.0 - sig))).astype(BF16)

    @pl.when(pl.program_id(0) == 0)
    def _():
        gskip_ref[...] = jnp.zeros_like(gskip_ref)

    gskip_ref[0:1, :] += jnp.sum(gin[...] * u_ref[0].astype(F32), axis=0, keepdims=True)

    def tile(j, carry):
        lanes = lanes_at(j)
        dec = [dec_ref[8 * n : 8 * n + 8, lanes] for n in range(states)]

        def step(i, carry):
            flow, total = carry
            for q in range(UNROLL):
                rows = rows_at(steps - 1 - (i * UNROLL + q))
                d = delta_ref[0, rows, lanes]
                g = gin[rows, lanes]
                flow = tuple(
                    jnp.exp2(d * dec[n]) * (flow[n] + g * cb[rows, col(n)]) for n in range(states)
                )
                total = total + d
            return flow, total

        zero = jnp.zeros((8, LANE), F32)
        flow, total = lax.fori_loop(0, steps // UNROLL, step, ((zero,) * states, zero))
        for n in range(states):
            inc = chunk_prefix(jnp.exp2(dec[n] * total), flow[n], True)
            sinc_ref[0, 8 * n : 8 * n + 8, lanes] = inc
            pay_ref[0, n : n + 1, lanes] = inc[0:1, :]
        full = jnp.sum(total, axis=0, keepdims=True)
        pay_ref[0, states : states + 8, lanes] = jnp.broadcast_to(full, (8, LANE))
        return carry

    lax.fori_loop(0, chans // LANE, tile, 0)


def back_kernel(
    delta_ref, u_ref, normed_ref, dec_ref, einc_ref, csd_ref, enter_ref, gin_ref, sinc_ref,
    leave_ref, skip_ref, eb_ref, ebt_ref, wdt_ref,
    gpre_ref, gu_ref, gnorm_ref, gdec_ref, gbias_ref, bc, acc, du, fac, prev, gstep,
    *, states,
):
    tok, chans = u_ref.shape[1], u_ref.shape[2]
    steps = tok // CHUNKS
    bc[...] = dot(split_low(normed_ref[0]), eb_ref[...])
    du[...] = delta_ref[0] * u_ref[0].astype(F32)
    acc[...] = jnp.zeros_like(acc)

    @pl.when(pl.program_id(0) == 0)
    def _():
        gdec_ref[...] = jnp.zeros_like(gdec_ref)
        gbias_ref[...] = jnp.zeros_like(gbias_ref)

    def tile(j, carry):
        lanes = lanes_at(j)
        dec = [dec_ref[8 * n : 8 * n + 8, lanes] for n in range(states)]
        csd = csd_ref[0, :, lanes]

        def forward(i, hs):
            for q in range(UNROLL):
                rows = rows_at(i * UNROLL + q)
                d = delta_ref[0, rows, lanes]
                v = du[rows, lanes]
                new = []
                for n in range(states):
                    a = jnp.exp2(d * dec[n])
                    p = a * hs[n]
                    fac[rows, col(n)] = a
                    prev[rows, col(n)] = p
                    new.append(p + v * bc[rows, col(n)])
                hs = tuple(new)
            return hs

        first = start_states(dec, csd, einc_ref, enter_ref, lanes, states)
        lax.fori_loop(0, steps // UNROLL, forward, first)

        place = lax.broadcasted_iota(jnp.int32, csd.shape, 0)
        after = csd[7:8, :] - csd
        flow = []
        for n in range(states):
            own = jnp.where(
                place < 7, pltpu.roll(sinc_ref[0, 8 * n : 8 * n + 8, lanes], 7, 0), 0.0
            )
            flow.append(own + jnp.exp2(dec[n] * after) * leave_ref[0, n : n + 1, lanes])

        def backward(i, carry):
            flow, logs = carry
            for q in range(UNROLL // 2):
                rows = rows_at(steps - 1 - (i * (UNROLL // 2) + q))
                d = delta_ref[0, rows, lanes]
                v = du[rows, lanes]
                g = gin_ref[0, rows, lanes]
                new_flow, new_logs, by_b, by_dec = [], [], [], []
                for n in range(states):
                    b = bc[rows, col(n)]
                    p = prev[rows, col(n)]
                    grad = flow[n] + g * bc[rows, col(states + n)]
                    gp = grad * p
                    new_flow.append(fac[rows, col(n)] * grad)
                    new_logs.append(logs[n] + gp * d)
                    by_dec.append(gp * dec[n])
                    by_b.append(grad * b)
                    acc[rows, col(n)] += grad * v
                    acc[rows, col(states + n)] += (p + v * b) * g
                flow, logs = tuple(new_flow), tuple(new_logs)
                drive = tree_sum(by_b)
                gu_ref[0, rows, lanes] = drive
                gstep[rows, lanes] = tree_sum(by_dec)
            return flow, logs

        zero = jnp.zeros((8, LANE), F32)
        unused, logs = lax.fori_loop(
            0, 2 * steps // UNROLL, backward, (tuple(flow), (zero,) * states)
        )
        for n in range(states):
            gdec_ref[n : n + 1, lanes] += jnp.sum(logs[n], axis=0, keepdims=True)
        return carry

    lax.fori_loop(0, chans // LANE, tile, 0)
    delta = delta_ref[0]
    drive = gu_ref[0]
    gdelta = gstep[...] * (1.0 / LOG2E) + drive * u_ref[0].astype(F32)
    gu_ref[0] = drive * delta + skip_ref[...] * gin_ref[0]
    small = delta * (1.0 - delta * (0.5 - delta * (1.0 / 6.0)))
    slope = jnp.where(delta < 0.01, small, 1.0 - jnp.exp(-delta))
    gpre = (gdelta * slope).astype(BF16)
    gpre_ref[0] = gpre
    gbias_ref[0:1, :] += jnp.sum(gpre.astype(F32), axis=0, keepdims=True)
    gnorm = dot_nt(gpre, wdt_ref[...]) + dot(acc[...].astype(BF16), ebt_ref[...])
    gnorm_ref[0] = gnorm


def conv_back_kernel(
    gn_ref, proj_ref, gain_ref, gu_ref, wxp_ref, xs_ref, edge_ref, cw_ref, cb_ref,
    gproj_ref, gxs_ref, head_ref, ggain_ref, gcw_ref, pad, per, nat, *, rank, states,
):
    tok, taps = xs_ref.shape[1], cw_ref.shape[0]

    @pl.when(pl.program_id(0) == 0)
    def _():
        ggain_ref[...] = jnp.zeros_like(ggain_ref)
        gcw_ref[...] = jnp.zeros_like(gcw_ref)

    grad = gn_ref[0]
    value = proj_ref[0]
    scale = lax.rsqrt(segment_rows(value * value, rank, states) + EPS)
    by_gain = gain_ref[...] * grad
    mean = segment_rows(value * by_gain, rank, states)
    gproj = (scale * by_gain - scale * scale * scale * value * mean).astype(BF16)
    gproj_ref[0] = gproj
    ggain_ref[0:1, :] += jnp.sum(grad * value * scale, axis=0, keepdims=True)
    to_natural_order(gu_ref[0] + dot_nt(gproj, wxp_ref[...]), per, nat)
    load_padded(pad, edge_ref, xs_ref, tok)
    conv = conv_of(pad, cw_ref[...], cb_ref[...], tok, taps)
    sig = sigmoid(conv)
    gconv = nat[...] * sig * (1.0 + conv * (1.0 - sig))
    for k in range(taps):
        start = 8 - (taps - 1) + k
        gcw_ref[k : k + 1, :] += jnp.sum(
            gconv * pad[start : start + tok, :], axis=0, keepdims=True
        )
    gcw_ref[taps : taps + 1, :] += jnp.sum(gconv, axis=0, keepdims=True)
    head_ref[0] = gconv[0:8, :]
    pad[0:tok, :] = gconv
    pad[tok : tok + 8, :] = jnp.zeros((8, gconv.shape[1]), F32)
    gxs = cw_ref[taps - 1 : taps, :] * gconv
    for k in range(taps - 1):
        ahead = taps - 1 - k
        gxs = gxs + cw_ref[k : k + 1, :] * pad[ahead : ahead + tok, :]
    gxs_ref[0] = gxs


def part(*shape):
    return pl.BlockSpec((1,) + shape, lambda i: (i,) + (0,) * len(shape))


def same(*shape):
    return pl.BlockSpec(shape, lambda i: (0,) * len(shape))


def call(body, count, in_specs, outs, scratch, args, cost):
    out_specs = [spec for spec, kind in outs]
    out_shape = []
    for spec, kind in outs:
        shape = tuple(spec.block_shape)
        probe = spec.index_map(1)
        out_shape.append(
            jax.ShapeDtypeStruct(((count,) + shape[1:]) if probe[0] == 1 else shape, kind)
        )
    flops, exps = cost
    moved = sum(a.size * a.dtype.itemsize for a in args)
    return pl.pallas_call(
        body,
        grid=(count,),
        in_specs=in_specs,
        out_specs=out_specs,
        out_shape=out_shape,
        scratch_shapes=scratch,
        compiler_params=pltpu.CompilerParams(vmem_limit_bytes=VMEM_LIMIT),
        cost_estimate=pl.CostEstimate(
            flops=flops, bytes_accessed=2 * moved, transcendentals=exps
        ),
    )(*args)


def sum_over(value, axis):
    if lax.axis_size(axis) != 4:
        return lax.psum(value, axis)
    place = lax.axis_index(axis)
    at_end = jnp.logical_or(place == 0, place == 3)
    half = value + lax.ppermute(value, axis, [(0, 1), (3, 2)])
    full = half + lax.ppermute(half, axis, [(1, 2), (2, 1)])
    back = lax.ppermute(full, axis, [(1, 0), (2, 3)])
    return jnp.where(at_end, back, full)


def shifted(value, distance):
    size = lax.axis_size("seq")
    route = [(i, i + distance) for i in range(size) if 0 <= i + distance < size]
    return lax.ppermute(value, "seq", route)


def from_before(payload, decay, states, sign):
    def join(far, near):
        keep = jnp.exp2(decay[None] * near[:, states : states + 1])
        value = keep * far[:, :states] + near[:, :states]
        rest = far[:, states:] + near[:, states:]
        return jnp.concatenate([value, rest], axis=1)

    size = lax.axis_size("seq")
    reach = min(4, size - 1)
    parts = [shifted(payload, sign * k) for k in range(1, reach + 1)]
    total = parts[-1]
    for near in parts[-2::-1]:
        total = join(total, near)
    while reach < size - 1:
        total = join(shifted(total, sign * reach), total)
        reach *= 2
    return total[:, :states]


def on_device(
    inputs, lengths, norm1_gain, w_in_x, w_in_z, conv_w, conv_b, w_xproj, dt_gain, b_gain, c_gain,
    w_dt, dt_bias, decay_log, skip_d, w_out, norm2_gain, w_gate, w_up, w_down, cotangent,
):
    batch, tok, width = inputs.shape
    chans = conv_w.shape[1]
    taps = conv_w.shape[0]
    rank, states = dt_gain.shape[0], b_gain.shape[0]
    cols = w_xproj.shape[1]
    per = batch // GROUPS
    rows = per * tok
    groups = range(GROUPS)

    def gather(weight):
        return lax.all_gather(weight, "seq", axis=0, tiled=True)

    gain_one = norm1_gain.astype(F32)[:, None]
    gain_two = norm2_gain.astype(F32)[:, None]
    full_in_x = gather((w_in_x.astype(F32) * gain_one).astype(BF16))
    full_in_z = gather((w_in_z.astype(F32) * gain_one).astype(BF16))
    full_out = gather(w_out.T)
    full_gate = gather((w_gate.astype(F32) * gain_two).astype(BF16))
    full_up = gather((w_up.astype(F32) * gain_two).astype(BF16))
    full_down = gather(w_down.T)

    first_place = lax.axis_index("seq") * tok
    counts = jnp.clip(lengths - first_place, 0, tok)
    live = (jnp.arange(tok, dtype=jnp.int32)[None, :] < counts[:, None])[:, :, None]
    decay = -jnp.exp(decay_log)
    decay2 = decay * LOG2E
    dec8 = jnp.repeat(decay2, 8, axis=0)
    k_of = lax.broadcasted_iota(jnp.int32, (2 * cols, 2 * states * LANE), 0) % cols
    c_of = lax.broadcasted_iota(jnp.int32, (2 * cols, 2 * states * LANE), 1) // LANE
    spread = (k_of == c_of + rank).astype(BF16)
    k_of = lax.broadcasted_iota(jnp.int32, (2 * states * LANE, cols), 1)
    c_of = lax.broadcasted_iota(jnp.int32, (2 * states * LANE, cols), 0) // LANE
    gathering = (k_of == c_of + rank).astype(BF16)
    gains = jnp.concatenate([dt_gain, b_gain, c_gain])[None]
    wdt = jnp.pad(w_dt, ((0, cols - rank), (0, 0)))
    cb_row, bias_row, skip_row = conv_b[None], dt_bias[None], skip_d[None]

    def unit(value):
        return value * lax.rsqrt(jnp.mean(value * value, axis=-1, keepdims=True) + EPS)

    edge_in = shifted(inputs[:, tok - 8 :, :], 1)
    edge_low = unit(edge_in.astype(F32)).astype(BF16)
    edge_xs = dot(edge_low.reshape(batch * 8, width), full_in_x).astype(BF16)
    edge_xs = edge_xs.reshape(batch, 8, chans)

    big = (per, tok, chans)
    scan_flops = per * tok * chans * states
    f32_blk = lambda *s: pltpu.VMEM(s, F32)
    wide = states * LANE
    tmp_blk = pltpu.VMEM((chans // LANE, tok, LANE), F32)

    src, low1, xs, z, edges, u, proj_part = [], [], [], [], [], [], []
    for g in groups:
        sl = slice(g * per, (g + 1) * per)
        x = inputs[sl].astype(F32).reshape(rows, width)
        n1 = unit(x).astype(BF16)
        src.append(x)
        low1.append(n1)
        xs.append(dot(n1, full_in_x).astype(BF16).reshape(big))
        edges.append(edge_xs[sl])
        uu, pp = call(
            pre_kernel, per,
            [part(tok, chans), part(8, chans), same(taps, chans), same(1, chans), same(chans, cols)],
            [(part(tok, chans), BF16), (part(tok, cols), F32)],
            [f32_blk(tok + 8, chans), tmp_blk, f32_blk(tok, chans)],
            (xs[g], edges[g], conv_w, cb_row, w_xproj),
            (2 * rows * chans * cols, rows * chans),
        )
        u.append(uu)
        proj_part.append(pp)
    for g in groups:
        z.append(dot(low1[g], full_in_z).reshape(big))

    proj = [sum_over(p, "ch") for p in proj_part]
    delta, normed, sn, einc, csd, enter = [], [], [], [], [], []
    for g in groups:
        sl = slice(g * per, (g + 1) * per)
        out = call(
            functools.partial(state_kernel, rank=rank, states=states), per,
            [pl.BlockSpec(memory_space=pltpu.SMEM), part(tok, cols), part(tok, chans),
             same(cols, chans), same(1, chans), same(1, cols), same(8 * states, chans),
             same(2 * cols, wide)],
            [(part(tok, chans), F32), (part(tok, cols), F32), (part(tok, cols), BF16),
             (part(8 * states, chans), F32), (part(8, chans), F32), (part(states + 8, chans), F32)],
            [f32_blk(tok, wide), f32_blk(tok, chans)],
            (counts[sl], proj[g], u[g], wdt, bias_row, gains, dec8, spread[:, :wide]),
            (5 * scan_flops, scan_flops),
        )
        delta.append(out[0]), normed.append(out[1]), sn.append(out[2])
        einc.append(out[3]), csd.append(out[4])
        enter.append(from_before(out[5], decay2, states, 1))

    inner, gated, branch = [], [], []
    for g in groups:
        i_, g_ = call(
            functools.partial(out_kernel, states=states), per,
            [part(tok, chans), part(tok, chans), part(tok, cols), same(8 * states, chans),
             part(8 * states, chans), part(8, chans), part(states, chans), part(tok, chans),
             same(1, chans), same(2 * cols, 2 * wide)],
            [(part(tok, chans), F32), (part(tok, chans), BF16)],
            [f32_blk(tok, 2 * wide), f32_blk(tok, chans), f32_blk(tok, chans), tmp_blk],
            (delta[g], u[g], normed[g], dec8, einc[g], csd[g], enter[g], z[g], skip_row, spread),
            (7 * scan_flops, scan_flops),
        )
        inner.append(i_), gated.append(g_)
        part_out = dot_nt(g_.reshape(rows, chans), full_out).astype(BF16)
        branch.append(sum_over(part_out, "ch"))

    middle, low2, hidden, ctl, upstream, ggate, gup, block, gmid, gml = ([] for _ in range(10))
    gain2_part = 0.0
    for g in groups:
        sl = slice(g * per, (g + 1) * per)
        mid = src[g] + branch[g].astype(F32)
        n2 = unit(mid).astype(BF16)
        gate_pre = dot(n2, full_gate)
        up_pre = dot(n2, full_up)
        sig = jax.nn.sigmoid(gate_pre)
        act = gate_pre * sig
        hid = (act * up_pre).astype(BF16)
        ffn = sum_over(dot_nt(hid, full_down).astype(BF16), "ch")
        block.append(mid + ffn.astype(F32))
        ct = jnp.where(live[sl], cotangent[sl].astype(F32), 0.0).reshape(rows, width)
        low_ct = ct.astype(BF16)
        ghid = dot(low_ct, full_down)
        gg = (ghid * up_pre * sig * (1.0 + gate_pre * (1.0 - sig))).astype(BF16)
        gu = (ghid * act).astype(BF16)
        gn2_part = dot_nt(gg, full_gate) + dot_nt(gu, full_up)
        scale = lax.rsqrt(jnp.mean(mid * mid, axis=-1, keepdims=True) + EPS)
        gn2 = sum_over(gn2_part.astype(BF16), "ch").astype(F32)
        gain2_part = gain2_part + jnp.sum(gn2 * mid * scale, axis=0)
        gm = ct + scale * gn2 - scale**3 * mid * jnp.mean(mid * gn2, axis=-1, keepdims=True)
        middle.append(mid), low2.append(n2), hidden.append(hid), ctl.append(low_ct)
        ggate.append(gg), gup.append(gu), gmid.append(gm), gml.append(gm.astype(BF16))

    def joined(parts):
        return jnp.concatenate([p.reshape(-1, p.shape[-1]) for p in parts], axis=0)

    def scattered(grad):
        return lax.psum_scatter(grad.astype(BF16), "seq", scatter_dimension=0, tiled=True).astype(F32)

    low2_all, ctl_all = joined(low2), joined(ctl)
    own_down = scattered(dot_tn(ctl_all, joined(hidden))).T
    own_gate = scattered(dot_tn(low2_all, joined(ggate))) * gain_two
    own_up = scattered(dot_tn(low2_all, joined(gup))) * gain_two
    own_out = scattered(dot_tn(joined(gml), joined(gated))).T

    gin, gz, sinc, leave = [], [], [], []
    gskip = 0.0
    for g in groups:
        ggated = dot(gml[g], full_out).reshape(big)
        out = call(
            functools.partial(back_state_kernel, states=states), per,
            [part(tok, chans)] * 5 + [part(tok, cols), same(8 * states, chans), same(1, chans),
             same(2 * cols, wide)],
            [(part(tok, chans), F32), (part(tok, chans), BF16), (part(8 * states, chans), F32),
             (part(states + 8, chans), F32), (same(8, chans), F32)],
            [f32_blk(tok, wide), tmp_blk],
            (ggated, z[g], inner[g], delta[g], u[g], normed[g], dec8, skip_row, spread[:, wide:]),
            (6 * scan_flops, scan_flops),
        )
        gin.append(out[0]), gz.append(out[1]), sinc.append(out[2])
        leave.append(from_before(out[3], decay2, states, -1))
        gskip = gskip + out[4][0]
    low1_all = joined(low1)
    own_in_z = scattered(dot_tn(low1_all, joined(gz))) * gain_one

    gpre, gu1, gnorm = [], [], []
    gdec, gbias = 0.0, 0.0
    for g in groups:
        out = call(
            functools.partial(back_kernel, states=states), per,
            [part(tok, chans), part(tok, chans), part(tok, cols), same(8 * states, chans),
             part(8 * states, chans), part(8, chans), part(states, chans), part(tok, chans),
             part(8 * states, chans), part(states, chans), same(1, chans),
             same(2 * cols, 2 * wide), same(2 * wide, cols), same(cols, chans)],
            [(part(tok, chans), BF16), (part(tok, chans), F32), (part(tok, cols), F32),
             (same(states, chans), F32), (same(8, chans), F32)],
            [f32_blk(tok, 2 * wide), f32_blk(tok, 2 * wide), f32_blk(tok, chans),
             f32_blk(tok, wide), f32_blk(tok, wide), f32_blk(tok, chans)],
            (delta[g], u[g], normed[g], dec8, einc[g], csd[g], enter[g], gin[g], sinc[g],
             leave[g], skip_row, spread, gathering, wdt),
            (22 * scan_flops, scan_flops),
        )
        gpre.append(out[0]), gu1.append(out[1])
        gnorm.append(sum_over(out[2].astype(BF16), "ch").astype(F32))
        gdec, gbias = gdec + out[3], gbias + out[4][0]

    gxs, gproj, grad_in = [], [], []
    ggain, gcw, gain1_part = 0.0, 0.0, 0.0
    for g in groups:
        out = call(
            functools.partial(conv_back_kernel, rank=rank, states=states), per,
            [part(tok, cols), part(tok, cols), same(1, cols), part(tok, chans), same(chans, cols),
             part(tok, chans), part(8, chans), same(taps, chans), same(1, chans)],
            [(part(tok, cols), BF16), (part(tok, chans), F32), (part(8, chans), F32),
             (same(8, cols), F32), (same(8, chans), F32)],
            [f32_blk(tok + 8, chans), tmp_blk, f32_blk(tok, chans)],
            (gnorm[g], proj[g], gains, gu1[g], w_xproj, xs[g], edges[g], conv_w, cb_row),
            (4 * rows * chans * cols, rows * chans),
        )
        gproj.append(out[0])
        ggain, gcw = ggain + out[3], gcw + out[4]
        ahead = shifted(out[2], -1)
        fix = jnp.zeros((per, 8, chans), F32)
        for k in range(taps - 1):
            dist = taps - 1 - k
            fix = fix.at[:, 8 - dist :, :].add(conv_w[k] * ahead[:, :dist, :])
        tail = out[1][:, tok - 8 :, :] + fix
        low_xs = jnp.concatenate([out[1][:, : tok - 8, :], tail], axis=1).astype(BF16)
        low_xs = low_xs.reshape(rows, chans)
        gxs.append(low_xs)
        gn1_part = dot_nt(low_xs, full_in_x) + dot_nt(gz[g].reshape(rows, chans), full_in_z)
        gn1 = sum_over(gn1_part.astype(BF16), "ch").astype(F32)
        x = src[g]
        scale = lax.rsqrt(jnp.mean(x * x, axis=-1, keepdims=True) + EPS)
        gain1_part = gain1_part + jnp.sum(gn1 * x * scale, axis=0)
        gx = scale * gn1 - scale**3 * x * jnp.mean(x * gn1, axis=-1, keepdims=True)
        grad_in.append(gx + gmid[g])
    own_in_x = scattered(dot_tn(low1_all, joined(gxs))) * gain_one
    gxproj = dot_tn(joined(gproj), joined(u))
    gwdt = dot_tn(joined(sn), joined(gpre))[:rank]

    rows_of = [gxproj, gwdt, gdec * decay * 1.0, gcw[: taps + 1], gbias[None], gskip[None]]
    stacked = jnp.concatenate(rows_of, axis=0).astype(BF16)
    stacked = lax.psum(stacked, "seq").astype(F32)
    marks = [0]
    for r in rows_of:
        marks.append(marks[-1] + r.shape[0])
    cut = [stacked[a:b] for a, b in zip(marks[:-1], marks[1:])]
    narrow = jnp.concatenate([gain1_part, gain2_part, ggain[0]]).astype(BF16)
    narrow = lax.psum(narrow, "seq").astype(F32)
    own = norm1_gain.shape[0]
    at = lax.axis_index("seq") * own
    own_one = lax.dynamic_slice(narrow, (at,), (own,)) / gain_one[:, 0]
    own_two = lax.dynamic_slice(narrow, (width + at,), (own,)) / gain_two[:, 0]
    ggain = narrow[2 * width :]
    return (
        jnp.stack(block).reshape(inputs.shape),
        jnp.stack(grad_in).reshape(inputs.shape),
        own_one,
        own_in_x,
        own_in_z,
        cut[3][:taps],
        cut[3][taps],
        cut[0].T,
        ggain[:rank],
        ggain[rank : rank + states],
        ggain[rank + states :],
        cut[1],
        cut[4][0],
        cut[2],
        cut[5][0],
        own_out,
        own_two,
        own_gate,
        own_up,
        own_down,
    )


def solution(mesh):
    return jax.shard_map(
        on_device,
        mesh=mesh,
        in_specs=(
            P(None, "seq", None),
            P(),
            P("seq"),
            P("seq", "ch"),
            P("seq", "ch"),
            P(None, "ch"),
            P("ch"),
            P("ch", None),
            P(),
            P(),
            P(),
            P(None, "ch"),
            P("ch"),
            P(None, "ch"),
            P("ch"),
            P("ch", "seq"),
            P("seq"),
            P("seq", "ch"),
            P("seq", "ch"),
            P("ch", "seq"),
            P(None, "seq", None),
        ),
        out_specs=(
            P(None, "seq", None),
            P(None, "seq", None),
            P("seq"),
            P("seq", "ch"),
            P("seq", "ch"),
            P(None, "ch"),
            P("ch"),
            P("ch", None),
            P(),
            P(),
            P(),
            P(None, "ch"),
            P("ch"),
            P(None, "ch"),
            P("ch"),
            P("ch", "seq"),
            P("seq"),
            P("seq", "ch"),
            P("seq", "ch"),
            P("ch", "seq"),
        ),
        check_vma=False,
    )
```

```python
import functools

import jax
import jax.numpy as jnp
from jax import lax
from jax.experimental import pallas as pl
from jax.experimental.pallas import tpu as pltpu
from jax.sharding import PartitionSpec as P

EPS = 1e-05
LOG2E = 1.4426950408889634
LANE = 128
CHUNKS = 8
UNROLL = 8
FORWARD_UNROLL = 4
BACK_UNROLL = 4
STATE_BLOCK = 2
WEIGHT_STEPS = 3
GROUPS = 1
ORDER = (
    "A0", "p0", "H0", "p0", "S0", "Z0", "e0", "O0", "O1", "O2", "o0", "O3", "o1", "o0", "o2", "o1",
    "F0", "o3", "o2", "F1", "f0", "o3", "F2", "f1", "f0", "F3", "f2", "f1", "B0", "f3", "f2", "D0",
    "B1", "Wdown", "f3", "D1", "B2", "Wffn", "B3", "d0", "Wout", "l0", "Win_z", "M0", "d1", "M1",
    "Rdown", "d0", "M2", "Q0", "Q1", "m0", "M3", "m0", "C0", "m1", "X0", "m1", "X1", "Rffn", "C1",
    "d1", "X2", "X3", "x0", "G0", "Win_x", "x1", "Q2", "Q3", "x0", "g0", "x2", "x1", "g0", "E0",
    "Rout", "N0", "x3", "x2", "n0", "E1", "x3", "n0", "E2", "Rin_z", "E3",
)
F32 = jnp.float32
BF16 = jnp.bfloat16
VMEM_LIMIT = 48 * 1024 * 1024


def tree_sum(parts):
    parts = list(parts)
    while len(parts) > 1:
        parts = [
            parts[i] + parts[i + 1] if i + 1 < len(parts) else parts[i]
            for i in range(0, len(parts), 2)
        ]
    return parts[0]


def dot(left, right):
    return jnp.dot(left, right, preferred_element_type=F32)


def dot_nt(left, right):
    return lax.dot_general(left, right, (((1,), (1,)), ((), ())), preferred_element_type=F32)


def dot_tn(left, right):
    return lax.dot_general(left, right, (((0,), (0,)), ((), ())), preferred_element_type=F32)


def sigmoid(value):
    return 1.0 / (1.0 + jnp.exp(-value))


def split_low(value):
    high = value.astype(BF16)
    rest = (value - high.astype(F32)).astype(BF16)
    return jnp.concatenate([high, rest], axis=1)


def segment_rows(value, rank, states):
    lane = lax.broadcasted_iota(jnp.int32, value.shape, 1)
    first = lane < rank
    last = lane >= rank + states
    middle = jnp.logical_not(jnp.logical_or(first, last))
    means = []
    for mask, count in ((first, rank), (middle, states), (last, states)):
        means.append(jnp.sum(jnp.where(mask, value, 0.0), axis=1, keepdims=True) / count)
    return jnp.where(first, means[0], jnp.where(last, means[2], means[1]))


def load_padded(pad_ref, edge_ref, xs_ref, tok):
    pad_ref[0:8, :] = edge_ref[0].astype(F32)
    pad_ref[8 : 8 + tok, :] = xs_ref[0].astype(F32)


def conv_of(pad_ref, conv_w, conv_b, tok, taps):
    out = conv_b
    for k in range(taps):
        start = 8 - (taps - 1) + k
        out = out + conv_w[k : k + 1, :] * pad_ref[start : start + tok, :]
    return out


def picked(end_ref, kept_ref, coming_ref):
    kept, coming = kept_ref[...], coming_ref[...]
    return jnp.where(end_ref[0] == 1, coming, kept).astype(F32)


def partial_rows(value):
    return jnp.sum(value.reshape(value.shape[0] // 8, 8, value.shape[1]), axis=0)


def to_scan_order(value, tmp_ref, dst_ref):
    tok, chans = value.shape
    steps = tok // CHUNKS
    for j in range(chans // LANE):
        tmp_ref[j] = value[:, col(j)]
        for t in range(steps):
            dst_ref[8 * t : 8 * t + 8, col(j)] = tmp_ref[j, pl.ds(t, 8, stride=steps), :]


def to_natural_order(value, tmp_ref, dst_ref):
    tok, chans = value.shape
    steps = tok // CHUNKS
    for j in range(chans // LANE):
        tmp_ref[j] = value[:, col(j)]
        for k in range(CHUNKS):
            for t in range(0, steps, 8):
                dst_ref[k * steps + t : k * steps + t + 8, col(j)] = tmp_ref[
                    j, pl.ds(8 * t + k, 8, stride=8), :
                ]


def pre_kernel(xs_ref, edge_ref, cw_ref, cb_ref, wxp_ref, u_ref, proj_ref, pad, nat, per):
    tok, taps = xs_ref.shape[1], cw_ref.shape[0]
    load_padded(pad, edge_ref, xs_ref, tok)
    conv = conv_of(pad, cw_ref[...], cb_ref[...], tok, taps)
    to_scan_order(conv * sigmoid(conv), nat, per)
    u_low = per[...].astype(BF16)
    u_ref[0] = u_low
    proj_ref[0] = dot(u_low, wxp_ref[...]).astype(BF16)


def lanes_at(j):
    return pl.ds(pl.multiple_of(j * LANE, LANE), LANE)


def rows_at(t):
    return pl.ds(pl.multiple_of(t * 8, 8), 8)


def col(n):
    return slice(n * LANE, (n + 1) * LANE)


def chunk_prefix(prod, value, backwards):
    place = lax.broadcasted_iota(jnp.int32, value.shape, 0)
    for step in (1, 2, 4):
        shift = CHUNKS - step if backwards else step
        keep = place < CHUNKS - step if backwards else place >= step
        prod_far = jnp.where(keep, pltpu.roll(prod, shift, 0), 1.0)
        value_far = jnp.where(keep, pltpu.roll(value, shift, 0), 0.0)
        value = prod * value_far + value
        prod = prod * prod_far
    return value


def sum_prefix(value):
    place = lax.broadcasted_iota(jnp.int32, value.shape, 0)
    for step in (1, 2, 4):
        value = value + jnp.where(place >= step, pltpu.roll(value, step, 0), 0.0)
    return value


def state_kernel(
    cnt_ref, proj_ref, u_ref, wdt_ref, bias_ref, gain_ref, dec_ref, eb_ref,
    delta_ref, normed_ref, sn_ref, einc_ref, csd_ref, pay_ref, bb, du,
    *, rank, states,
):
    tok, chans = u_ref.shape[1], u_ref.shape[2]
    steps = tok // CHUNKS
    value = proj_ref[0]
    scale = lax.rsqrt(segment_rows(value * value, rank, states) + EPS)
    normed = value * scale * gain_ref[...]
    normed_ref[0] = normed
    lane = lax.broadcasted_iota(jnp.int32, value.shape, 1)
    step_low = jnp.where(lane < rank, normed, 0.0).astype(BF16)
    sn_ref[0] = step_low
    pre = dot(step_low, wdt_ref[...]) + bias_ref[...]
    row = lax.broadcasted_iota(jnp.int32, pre.shape, 0)
    place = (row & 7) * steps + (row >> 3)
    live = place < cnt_ref[pl.program_id(0)]
    soft = jnp.maximum(pre, 0.0) + jnp.log(1.0 + jnp.exp(-jnp.abs(pre)))
    delta = jnp.where(live, soft, 0.0)
    delta_ref[0] = delta
    du[...] = delta * u_ref[0].astype(F32)
    bb[...] = dot(split_low(normed), eb_ref[...])

    def tile(j, carry):
        lanes = lanes_at(j)
        dec = [dec_ref[8 * n : 8 * n + 8, lanes] for n in range(states)]

        def step(i, carry):
            ends, total = carry
            for q in range(UNROLL):
                rows = rows_at(i * UNROLL + q)
                d = delta_ref[0, rows, lanes]
                v = du[rows, lanes]
                ends = tuple(
                    jnp.exp2(d * dec[n]) * ends[n] + v * bb[rows, col(n)] for n in range(states)
                )
                total = total + d
            return ends, total

        zero = jnp.zeros((8, LANE), F32)
        ends, total = lax.fori_loop(0, steps // UNROLL, step, ((zero,) * states, zero))
        csd = sum_prefix(total)
        csd_ref[0, :, lanes] = csd
        for n in range(states):
            inc = chunk_prefix(jnp.exp2(dec[n] * total), ends[n], False)
            einc_ref[0, 8 * n : 8 * n + 8, lanes] = inc
            pay_ref[0, n : n + 1, lanes] = inc[7:8, :]
        pay_ref[0, states : states + 8, lanes] = jnp.broadcast_to(csd[7:8, :], (8, LANE))
        return carry

    lax.fori_loop(0, chans // LANE, tile, 0)


def start_states(dec, csd, einc_ref, enter_ref, lanes, states):
    place = lax.broadcasted_iota(jnp.int32, csd.shape, 0)
    before = jnp.where(place >= 1, pltpu.roll(csd, 1, 0), 0.0)
    out = []
    for n in range(states):
        own = jnp.where(place >= 1, pltpu.roll(einc_ref[0, 8 * n : 8 * n + 8, lanes], 1, 0), 0.0)
        out.append(own + jnp.exp2(dec[n] * before) * enter_ref[0, n : n + 1, lanes])
    return tuple(out)


def out_kernel(
    delta_ref, u_ref, normed_ref, dec_ref, einc_ref, csd_ref, enter_ref, z_ref, skip_ref, eb_ref,
    wout_ref, inner_ref, gated_ref, branch_ref, bc, du, per, tmp, *, states,
):
    tok, chans = u_ref.shape[1], u_ref.shape[2]
    steps = tok // CHUNKS
    bc[...] = dot(split_low(normed_ref[0]), eb_ref[...])
    u_val = u_ref[0].astype(F32)
    du[...] = delta_ref[0] * u_val
    per[...] = skip_ref[...] * u_val

    def tile(j, carry):
        lanes = lanes_at(j)
        dec = [dec_ref[8 * n : 8 * n + 8, lanes] for n in range(states)]

        def step(i, hs):
            for q in range(UNROLL):
                rows = rows_at(i * UNROLL + q)
                d = delta_ref[0, rows, lanes]
                v = du[rows, lanes]
                hs = tuple(
                    jnp.exp2(d * dec[n]) * hs[n] + v * bc[rows, col(n)] for n in range(states)
                )
                per[rows, lanes] += tree_sum(
                    hs[n] * bc[rows, col(states + n)] for n in range(states)
                )
            return hs

        first = start_states(dec, csd_ref[0, :, lanes], einc_ref, enter_ref, lanes, states)
        lax.fori_loop(0, steps // UNROLL, step, first)
        return carry

    lax.fori_loop(0, chans // LANE, tile, 0)
    to_natural_order(per[...], tmp, du)
    inner = du[...]
    inner_ref[0] = inner
    z_val = z_ref[0].astype(F32)
    gated = (inner * z_val * sigmoid(z_val)).astype(BF16)
    gated_ref[0] = gated
    branch_ref[...] = dot_nt(gated, wout_ref[...]).astype(BF16)


def back_state_kernel(
    edge_ref, mid_ref, kept_ref, coming_ref, ctl_ref, wout_ref, z_ref, inner_ref, delta_ref, u_ref,
    normed_ref, dec_ref, skip_ref, ec_ref, gskip_in, gain_in,
    gm_ref, gml_ref, gin_ref, gz_ref, sinc_ref, pay_ref, gskip_ref, gain_ref, cb, nat, *, states,
):
    tok, chans = u_ref.shape[1], u_ref.shape[2]
    steps = tok // CHUNKS
    mid = mid_ref[0]
    grad = picked(edge_ref, kept_ref, coming_ref)
    scale = lax.rsqrt(jnp.mean(mid * mid, axis=-1, keepdims=True) + EPS)
    by_mid = mid * grad
    mean = jnp.mean(by_mid, axis=-1, keepdims=True)
    gain_ref[...] = gain_in[...] + partial_rows(by_mid * scale)
    gm = ctl_ref[0].astype(F32) + scale * grad - (scale * scale * scale * mean) * mid
    gm_ref[0] = gm
    gml_ref[0] = gm.astype(BF16)
    gg = dot(gml_ref[0], wout_ref[...])
    cb[...] = dot(split_low(normed_ref[0]), ec_ref[...])
    z_val = z_ref[0].astype(F32)
    sig = sigmoid(z_val)
    gin = gin_ref.at[0]
    to_scan_order(gg * z_val * sig, nat, gin)
    gz_ref[0] = (gg * inner_ref[0] * sig * (1.0 + z_val * (1.0 - sig))).astype(BF16)

    gskip_ref[...] = gskip_in[...] + partial_rows(gin[...] * u_ref[0].astype(F32))

    def tile(j, carry):
        lanes = lanes_at(j)
        dec = [dec_ref[8 * n : 8 * n + 8, lanes] for n in range(states)]

        def step(i, carry):
            flow, total = carry
            for q in range(UNROLL):
                rows = rows_at(steps - 1 - (i * UNROLL + q))
                d = delta_ref[0, rows, lanes]
                g = gin[rows, lanes]
                flow = tuple(
                    jnp.exp2(d * dec[n]) * (flow[n] + g * cb[rows, col(n)]) for n in range(states)
                )
                total = total + d
            return flow, total

        zero = jnp.zeros((8, LANE), F32)
        flow, total = lax.fori_loop(0, steps // UNROLL, step, ((zero,) * states, zero))
        for n in range(states):
            inc = chunk_prefix(jnp.exp2(dec[n] * total), flow[n], True)
            sinc_ref[0, 8 * n : 8 * n + 8, lanes] = inc
            pay_ref[0, n : n + 1, lanes] = inc[0:1, :]
        full = jnp.sum(total, axis=0, keepdims=True)
        pay_ref[0, states : states + 8, lanes] = jnp.broadcast_to(full, (8, LANE))
        return carry

    lax.fori_loop(0, chans // LANE, tile, 0)


def back_kernel(
    delta_ref, u_ref, normed_ref, dec_ref, einc_ref, csd_ref, enter_ref, gin_ref, sinc_ref,
    leave_ref, skip_ref, eb_ref, ebt_ref, wdt_ref, gdec_in, gbias_in,
    gpre_ref, gu_ref, gnorm_ref, gdec_ref, gbias_ref, bc, acc, du, fac, prev, gstep,
    enter8, leave8, logs8,
    *, states,
):
    tok, chans = u_ref.shape[1], u_ref.shape[2]
    steps, tiles = tok // CHUNKS, chans // LANE
    bc[...] = dot(split_low(normed_ref[0]), eb_ref[...])
    du[...] = delta_ref[0] * u_ref[0].astype(F32)
    gu_ref[0] = jnp.zeros((tok, chans), F32)
    gstep[...] = jnp.zeros((tok, chans), F32)
    for n in range(states):
        rows = slice(8 * n, 8 * n + 8)
        enter8[rows, :] = jnp.broadcast_to(enter_ref[0, n : n + 1, :], (8, chans))
        leave8[rows, :] = jnp.broadcast_to(leave_ref[0, n : n + 1, :], (8, chans))
    place = lax.broadcasted_iota(jnp.int32, (8, LANE), 0)
    pairs = [(q, j) for q in range(STATE_BLOCK) for j in range(tiles)]

    def block(i, carry):
        ns = [i * STATE_BLOCK + q for q in range(STATE_BLOCK)]
        rows_of = [rows_at(n) for n in ns]
        at_b = [lanes_at(n) for n in ns]
        at_c = [lanes_at(n + states) for n in ns]
        dec = {(q, j): dec_ref[rows_of[q], col(j)] for q, j in pairs}
        first, last = [], []
        for q, j in pairs:
            csd = csd_ref[0, :, col(j)]
            before = jnp.where(place >= 1, pltpu.roll(csd, 1, 0), 0.0)
            own = jnp.where(place >= 1, pltpu.roll(einc_ref[0, rows_of[q], col(j)], 1, 0), 0.0)
            first.append(own + jnp.exp2(dec[q, j] * before) * enter8[rows_of[q], col(j)])
            after = csd[7:8, :] - csd
            own = jnp.where(place < 7, pltpu.roll(sinc_ref[0, rows_of[q], col(j)], 7, 0), 0.0)
            last.append(own + jnp.exp2(dec[q, j] * after) * leave8[rows_of[q], col(j)])

        def forward(t, hs):
            for r in range(FORWARD_UNROLL):
                rows = rows_at(t * FORWARD_UNROLL + r)
                d = [delta_ref[0, rows, col(j)] for j in range(tiles)]
                v = [du[rows, col(j)] for j in range(tiles)]
                g = [gin_ref[0, rows, col(j)] for j in range(tiles)]
                b = [bc[rows, at] for at in at_b]
                new = []
                for k, (q, j) in enumerate(pairs):
                    a = jnp.exp2(d[j] * dec[q, j])
                    p = a * hs[k]
                    fac[rows, col(k)] = a
                    prev[rows, col(k)] = p
                    new.append(p + v[j] * b[q])
                hs = tuple(new)
                for q in range(STATE_BLOCK):
                    acc[rows, at_c[q]] = tree_sum(hs[q * tiles + j] * g[j] for j in range(tiles))
            return hs

        lax.fori_loop(0, steps // FORWARD_UNROLL, forward, tuple(first))

        def backward(t, carry):
            flow, logs = carry
            for r in range(BACK_UNROLL):
                rows = rows_at(steps - 1 - (t * BACK_UNROLL + r))
                d = [delta_ref[0, rows, col(j)] for j in range(tiles)]
                v = [du[rows, col(j)] for j in range(tiles)]
                g = [gin_ref[0, rows, col(j)] for j in range(tiles)]
                b = [bc[rows, at] for at in at_b]
                c = [bc[rows, at] for at in at_c]
                new_flow, new_logs, grads, scaled = [], [], [], []
                for k, (q, j) in enumerate(pairs):
                    grad = flow[k] + g[j] * c[q]
                    gp = grad * prev[rows, col(k)]
                    new_flow.append(fac[rows, col(k)] * grad)
                    new_logs.append(logs[k] + gp * d[j])
                    scaled.append(gp * dec[q, j])
                    grads.append(grad)
                flow, logs = tuple(new_flow), tuple(new_logs)
                for j in range(tiles):
                    gu_ref[0, rows, col(j)] += tree_sum(
                        grads[q * tiles + j] * b[q] for q in range(STATE_BLOCK)
                    )
                    gstep[rows, col(j)] += tree_sum(
                        scaled[q * tiles + j] for q in range(STATE_BLOCK)
                    )
                for q in range(STATE_BLOCK):
                    acc[rows, at_b[q]] = tree_sum(grads[q * tiles + j] * v[j] for j in range(tiles))
            return flow, logs

        zero = jnp.zeros((8, LANE), F32)
        unused, logs = lax.fori_loop(
            0, steps // BACK_UNROLL, backward, (tuple(last), (zero,) * len(pairs))
        )
        for k, (q, j) in enumerate(pairs):
            logs8[rows_of[q], col(j)] = logs[k]
        return carry

    lax.fori_loop(0, states // STATE_BLOCK, block, 0)
    for n in range(states):
        total = jnp.sum(logs8[8 * n : 8 * n + 8, :], axis=0, keepdims=True)
        gdec_ref[n : n + 1, :] = gdec_in[n : n + 1, :] + total
    delta = delta_ref[0]
    drive = gu_ref[0]
    gdelta = gstep[...] * (1.0 / LOG2E) + drive * u_ref[0].astype(F32)
    gu_ref[0] = drive * delta + skip_ref[...] * gin_ref[0]
    small = delta * (1.0 - delta * (0.5 - delta * (1.0 / 6.0)))
    slope = jnp.where(delta < 0.01, small, 1.0 - jnp.exp(-delta))
    gpre = (gdelta * slope).astype(BF16)
    gpre_ref[0] = gpre
    gbias_ref[...] = gbias_in[...] + partial_rows(gpre.astype(F32))
    gnorm = dot_nt(gpre, wdt_ref[...]) + dot(acc[...].astype(BF16), ebt_ref[...])
    gnorm_ref[0] = gnorm.astype(BF16)


def conv_back_kernel(
    end_ref, kept_ref, coming_ref, proj_ref, gain_ref, gu_ref, wxp_ref, xs_ref, edge_ref, cw_ref,
    cb_ref, ggain_in, gcw_in, gproj_ref, gxs_ref, head_ref, ggain_ref, gcw_ref, pad, per, nat,
    *, rank, states,
):
    tok, taps = xs_ref.shape[1], cw_ref.shape[0]
    grad = picked(end_ref, kept_ref, coming_ref)[0]
    value = proj_ref[0]
    scale = lax.rsqrt(segment_rows(value * value, rank, states) + EPS)
    by_gain = gain_ref[...] * grad
    mean = segment_rows(value * by_gain, rank, states)
    gproj = (scale * by_gain - scale * scale * scale * value * mean).astype(BF16)
    gproj_ref[0] = gproj
    ggain_ref[...] = ggain_in[...] + partial_rows(grad * value * scale)
    to_natural_order(gu_ref[0] + dot_nt(gproj, wxp_ref[...]), per, nat)
    load_padded(pad, edge_ref, xs_ref, tok)
    conv = conv_of(pad, cw_ref[...], cb_ref[...], tok, taps)
    sig = sigmoid(conv)
    gconv = nat[...] * sig * (1.0 + conv * (1.0 - sig))
    for k in range(taps):
        start = 8 - (taps - 1) + k
        gcw_ref[8 * k : 8 * k + 8, :] = gcw_in[8 * k : 8 * k + 8, :] + partial_rows(
            gconv * pad[start : start + tok, :]
        )
    gcw_ref[8 * taps :, :] = gcw_in[8 * taps :, :] + partial_rows(gconv)
    head_ref[0] = gconv[0:8, :]
    pad[0:tok, :] = gconv
    pad[tok : tok + 8, :] = jnp.zeros((8, gconv.shape[1]), F32)
    gxs = cw_ref[taps - 1 : taps, :] * gconv
    for k in range(taps - 1):
        ahead = taps - 1 - k
        gxs = gxs + cw_ref[k : k + 1, :] * pad[ahead : ahead + tok, :]
    gxs_ref[0] = gxs


def ffn_kernel(
    end_ref, x_ref, kept_ref, coming_ref, ctl_ref, w_ref, wd_ref,
    mid_ref, low_ref, hid_ref, gffn_ref, gn_ref, down_ref, gn_acc, down_acc,
):
    step = pl.program_id(0)

    @pl.when(step == 0)
    def _():
        mid = x_ref[0].astype(F32) + picked(end_ref, kept_ref, coming_ref)
        mid_ref[0] = mid
        scale = lax.rsqrt(jnp.mean(mid * mid, axis=-1, keepdims=True) + EPS)
        low_ref[0] = (mid * scale).astype(BF16)

    weight = w_ref[...]
    units = weight.shape[1] // 2
    both = dot(low_ref[0], weight)
    back = dot(ctl_ref[0], wd_ref[...])
    gate, up = both[:, :units], both[:, units:]
    sig = sigmoid(gate)
    act = gate * sig
    hid = (act * up).astype(BF16)
    hid_ref[0] = hid
    ggate = (back * up * (sig * (1.0 + gate - act))).astype(BF16)
    gffn = jnp.concatenate([ggate, (back * act).astype(BF16)], axis=1)
    gffn_ref[0] = gffn
    gn = dot_nt(gffn, weight)
    down = dot_nt(hid, wd_ref[...])

    @pl.when(step == 0)
    def _():
        gn_acc[...] = gn
        down_acc[...] = down

    @pl.when(step > 0)
    def _():
        gn_acc[...] += gn
        down_acc[...] += down

    @pl.when(step == pl.num_programs(0) - 1)
    def _():
        gn_ref[...] = gn_acc[...].astype(BF16)
        down_ref[...] = down_acc[...].astype(BF16)


def add_kernel(end_ref, mid_ref, kept_ref, coming_ref, out_ref):
    out_ref[0] = mid_ref[0] + picked(end_ref, kept_ref, coming_ref)


def in_grad_kernel(
    gxs_ref, ahead_ref, cw_ref, gz_ref, wx_ref, wz_ref, x_ref, gain_in,
    low_ref, gn_ref, gain_ref, *, taps,
):
    tok = gxs_ref.shape[1]
    row = lax.broadcasted_iota(jnp.int32, (8, gxs_ref.shape[2]), 0)
    ahead = ahead_ref[0]
    fix = jnp.zeros((8, gxs_ref.shape[2]), F32)
    for k in range(taps - 1):
        start = 8 - (taps - 1 - k)
        moved = pltpu.roll(ahead, start, 0)
        fix = fix + jnp.where(row >= start, cw_ref[k : k + 1, :] * moved, 0.0)
    main = gxs_ref[0]
    low = jnp.concatenate([main[: tok - 8], main[tok - 8 :] + fix], axis=0).astype(BF16)
    low_ref[0] = low
    gn = dot_nt(low, wx_ref[...]) + dot_nt(gz_ref[0], wz_ref[...])
    x = x_ref[0].astype(F32)
    scale = lax.rsqrt(jnp.mean(x * x, axis=-1, keepdims=True) + EPS)
    gain_ref[...] = gain_in[...] + partial_rows(gn * x * scale)
    gn_ref[...] = gn.astype(BF16)


def end_kernel(end_ref, x_ref, kept_ref, coming_ref, gm_ref, out_ref):
    x = x_ref[0].astype(F32)
    grad = picked(end_ref, kept_ref, coming_ref)
    scale = lax.rsqrt(jnp.mean(x * x, axis=-1, keepdims=True) + EPS)
    mean = jnp.mean(x * grad, axis=-1, keepdims=True)
    out_ref[0] = gm_ref[0] + scale * grad - (scale * scale * scale * mean) * x


def weight_kernel(left_ref, right_ref, out_ref):
    out_ref[...] = dot_tn(left_ref[...], right_ref[...]).astype(BF16)


def part(*shape, at=0):
    return pl.BlockSpec((1,) + shape, lambda i: (i + at,) + (0,) * len(shape))


def slot(*shape, at):
    return pl.BlockSpec((1,) + shape, lambda i: (at,) + (0,) * len(shape))


def same(*shape, at=0):
    return pl.BlockSpec(shape, lambda i: (at,) + (0,) * (len(shape) - 1))


def call(body, count, in_specs, outs, scratch, args, into=None, carry=None):
    into, carry = into or {}, carry or {}
    fixed = len(args)
    kept = sorted(k for k in into if into[k] is not None)
    args = tuple(args) + tuple(into[k] for k in kept)
    in_specs = list(in_specs) + [pl.BlockSpec(memory_space=pl.ANY)] * len(kept)
    aliases = {fixed + i: k for i, k in enumerate(kept)}
    aliases.update({arg: out for out, arg in carry.items()})

    def run(*refs):
        body(*refs[:fixed], *refs[fixed + len(kept) :])

    return pl.pallas_call(
        run,
        grid=(count,),
        in_specs=in_specs,
        out_specs=[spec for spec, kind, shape in outs],
        out_shape=[jax.ShapeDtypeStruct(shape, kind) for spec, kind, shape in outs],
        scratch_shapes=scratch,
        input_output_aliases=aliases,
        compiler_params=pltpu.CompilerParams(vmem_limit_bytes=VMEM_LIMIT),
        cost_estimate=pl.CostEstimate(flops=0, bytes_accessed=0, transcendentals=0),
    )(*args)


class Sum:
    def __init__(self, value, axis):
        self.axis, self.hops, self.kept = axis, 0, value
        if lax.axis_size(axis) != 4:
            self.hops, self.kept = 3, lax.psum(value, axis)
            return
        self.coming = lax.ppermute(value, axis, [(0, 1), (3, 2)])

    def advance(self, tie, mark):
        if self.hops >= 2:
            return
        self.kept = self.kept + tie(self.coming)
        mark(self.kept)
        route = [(1, 0), (2, 3)] if self.hops else [(1, 2), (2, 1)]
        self.coming = lax.ppermute(self.kept, self.axis, route)
        self.hops += 1

    def result(self):
        while self.hops < 2:
            self.advance(lambda v: v, lambda v: None)
        if self.hops == 2:
            place = lax.axis_index(self.axis)
            at_end = jnp.logical_or(place == 0, place == 3)
            self.kept, self.hops = jnp.where(at_end, self.coming, self.kept), 3
        return self.kept

    def pair(self):
        while self.hops < 2:
            self.advance(lambda v: v, lambda v: None)
        return (self.kept, self.coming if self.hops == 2 else self.kept)


def shifted(value, distance):
    size = lax.axis_size("seq")
    route = [(i, i + distance) for i in range(size) if 0 <= i + distance < size]
    return lax.ppermute(value, "seq", route)


class Cube:
    def __init__(self, value, axis):
        self.value, self.axis, self.size, self.bit = value, axis, lax.axis_size(axis), 1
        if self.size & (self.size - 1):
            self.value, self.bit = lax.psum(value, axis), self.size
        self.send()

    def send(self):
        if self.bit < self.size:
            route = [(i, i ^ self.bit) for i in range(self.size)]
            self.coming = lax.ppermute(self.value, self.axis, route)

    def advance(self, tie, mark):
        if self.bit < self.size:
            self.value = self.value + tie(self.coming)
            mark(self.value)
            self.bit *= 2
            self.send()

    def result(self):
        while self.bit < self.size:
            self.advance(lambda v: v, lambda v: None)
        return self.value


class Entering:
    def __init__(self, payload, decay, states, sign):
        self.decay, self.states, self.sign = decay, states, sign
        self.size = lax.axis_size("seq")
        self.reach = min(4, self.size - 1)
        packed = self.pack((payload[:, :states], payload[:, states : states + 1]))
        self.parts = [shifted(packed, sign * k) for k in range(1, self.reach + 1)]
        self.total = None

    def pack(self, pair):
        value, length = pair
        high = lax.optimization_barrier(length.astype(BF16))
        low = (length - high.astype(F32)).astype(BF16)
        return jnp.concatenate([value.astype(BF16), high, low], axis=1)

    def unpack(self, packed):
        whole = packed.astype(F32)
        value, high = whole[:, : self.states], whole[:, self.states : self.states + 1]
        return value, high + whole[:, self.states + 1 :]

    def join(self, far, near):
        return jnp.exp2(self.decay[None] * near[1]) * far[0] + near[0], far[1] + near[1]

    def advance(self, tie, mark):
        total = self.unpack(tie(self.parts[-1]))
        for near in self.parts[-2::-1]:
            total = self.join(total, self.unpack(near))
        self.total = total
        mark(total[0])
        if self.reach < self.size - 1:
            self.coming = shifted(self.pack(total), self.sign * self.reach)

    def result(self):
        if self.total is None:
            self.advance(lambda v: v, lambda v: None)
        while self.reach < self.size - 1:
            self.total = self.join(self.unpack(self.coming), self.total)
            self.reach *= 2
            if self.reach < self.size - 1:
                self.coming = shifted(self.pack(self.total), self.sign * self.reach)
        return self.total[0]


def on_device(
    inputs, lengths, norm1_gain, w_in_x, w_in_z, conv_w, conv_b, w_xproj, dt_gain, b_gain, c_gain,
    w_dt, dt_bias, decay_log, skip_d, w_out, norm2_gain, w_gate, w_up, w_down, cotangent,
):
    batch, tok, width = inputs.shape
    chans = conv_w.shape[1]
    taps = conv_w.shape[0]
    rank, states = dt_gain.shape[0], b_gain.shape[0]
    cols = w_xproj.shape[1]
    per = batch // GROUPS
    rows = per * tok
    groups = range(GROUPS)

    def gather(weight):
        return lax.all_gather(weight, "seq", axis=0, tiled=True)

    gain_one = norm1_gain.astype(F32)[:, None]
    gain_two = norm2_gain.astype(F32)[:, None]
    full_in_x = gather((w_in_x.astype(F32) * gain_one).astype(BF16))
    full_in_z = gather((w_in_z.astype(F32) * gain_one).astype(BF16))
    full_out = gather(w_out.T)
    full_down = gather(w_down.T)
    low_gate = (w_gate.astype(F32) * gain_two).astype(BF16)
    low_up = (w_up.astype(F32) * gain_two).astype(BF16)
    units, tile = w_gate.shape[1], w_gate.shape[1]
    own_rows = w_gate.shape[0]
    both_ffn = jnp.stack([low_gate.reshape(own_rows, -1, tile), low_up.reshape(own_rows, -1, tile)], 2)
    full_ffn = gather(both_ffn.reshape(own_rows, 2 * units))

    first_place = lax.axis_index("seq") * tok
    counts = jnp.clip(lengths - first_place, 0, tok)
    live = (jnp.arange(tok, dtype=jnp.int32)[None, :] < counts[:, None])[:, :, None]
    decay = -jnp.exp(decay_log)
    decay2 = decay * LOG2E
    dec8 = jnp.repeat(decay2, 8, axis=0)
    k_of = lax.broadcasted_iota(jnp.int32, (2 * cols, 2 * states * LANE), 0) % cols
    c_of = lax.broadcasted_iota(jnp.int32, (2 * cols, 2 * states * LANE), 1) // LANE
    spread = (k_of == c_of + rank).astype(BF16)
    k_of = lax.broadcasted_iota(jnp.int32, (2 * states * LANE, cols), 1)
    c_of = lax.broadcasted_iota(jnp.int32, (2 * states * LANE, cols), 0) // LANE
    gathering = (k_of == c_of + rank).astype(BF16)
    gains = jnp.concatenate([dt_gain, b_gain, c_gain])[None]
    wdt = jnp.pad(w_dt, ((0, cols - rank), (0, 0)))
    cb_row, bias_row, skip_row = conv_b[None], dt_bias[None], skip_d[None]

    def unit(value):
        return value * lax.rsqrt(jnp.mean(value * value, axis=-1, keepdims=True) + EPS)

    edge_in = shifted(inputs[:, tok - 8 :, :], 1)
    edge_low = unit(edge_in.astype(F32)).astype(BF16)
    edge_xs = dot(edge_low.reshape(batch * 8, width), full_in_x).astype(BF16)
    edge_xs = edge_xs.reshape(batch, 8, chans)

    big = (per, tok, chans)
    f32_blk = lambda *s: pltpu.VMEM(s, F32)
    wide = states * LANE
    tmp_blk = pltpu.VMEM((chans // LANE, tok, LANE), F32)

    state = {"last": None}

    def tie(value):
        if state["last"] is None:
            return value
        return lax.optimization_barrier((value, state["last"]))[0]

    def mark(value):
        state["last"] = value

    low1, xs, z, edges, u, proj = {}, {}, {}, {}, {}, {}
    delta, normed, sn, einc, csd, enter, ctl, own = {}, {}, {}, {}, {}, {}, {}, {}
    live_sums = {}

    def scattered(grad):
        return lax.psum_scatter(grad, "seq", scatter_dimension=0, tiled=True).astype(F32)

    ch_place = lax.axis_index("ch")
    at_end = jnp.logical_or(ch_place == 0, ch_place == lax.axis_size("ch") - 1)
    at_end = at_end.astype(jnp.int32).reshape(1)
    smem = pl.BlockSpec(memory_space=pltpu.SMEM)
    whole = lambda *shape: (batch,) + shape
    acc = lambda rows_, width_: jnp.zeros((rows_, width_), F32)
    buf = dict.fromkeys(
        ("inner", "gated", "mid", "low2", "hidden", "gffn", "gm", "gml", "gin", "gz", "sinc", "pay",
         "gpre", "gu1", "gnorm", "gproj", "gxs", "head", "low_xs", "block", "grad_in")
    )
    buf.update(gskip=acc(8, chans), gain2=acc(8, width), gdec=acc(states, chans),
               gbias=acc(8, chans), ggain=acc(8, cols), gcw=acc(8 * (taps + 1), chans),
               gain1=acc(8, width))

    def at_block(b, *shape):
        return slot(*shape, at=b)

    def run(body, b, specs, args, outs, scratch=(), count=1, carry=()):
        specs, args = list(specs), list(args)
        shapes, into, carried = [], {}, {}
        for i, (name, block, kind) in enumerate(outs):
            if name in buf:
                shapes.append((at_block(b, *block), kind, whole(*block)))
                into[i] = buf[name]
            else:
                shapes.append((same(*block), kind, block))
        for name in carry:
            shape = buf[name].shape
            carried[len(shapes)] = len(args)
            specs.append(same(*shape))
            args.append(buf[name])
            shapes.append((same(*shape), F32, shape))
        out = call(body, count, specs, shapes, list(scratch), args, into, carried)
        names = [name for name, block, kind in outs] + list(carry)
        for name, value in zip(names, out):
            buf[name] = value
        return dict(zip(names, out))

    def stage_a(g):
        x = tie(inputs).astype(F32).reshape(rows, width)
        low1[g] = unit(x).astype(BF16)
        xs[g] = dot(low1[g], full_in_x).astype(BF16).reshape(big)
        edges[g] = edge_xs
        u[g], proj_part = call(
            pre_kernel, per,
            [part(tok, chans), part(8, chans), same(taps, chans), same(1, chans), same(chans, cols)],
            [(part(tok, chans), BF16, big), (part(tok, cols), BF16, whole(tok, cols))],
            [f32_blk(tok + 8, chans), tmp_blk, f32_blk(tok, chans)],
            (xs[g], edges[g], conv_w, cb_row, w_xproj),
        )
        mark(proj_part)
        live_sums["p", g] = Sum(proj_part.reshape(rows, cols), "ch")

    def stage_z(g):
        z[g] = dot(tie(low1[g]), full_in_z).astype(BF16).reshape(big)
        mark(z[g])

    def stage_s(g):
        proj[g] = live_sums["p", g].result().astype(F32).reshape(per, tok, cols)
        out = call(
            functools.partial(state_kernel, rank=rank, states=states), per,
            [smem, part(tok, cols), part(tok, chans),
             same(cols, chans), same(1, chans), same(1, cols), same(8 * states, chans),
             same(2 * cols, wide)],
            [(part(tok, chans), F32, big), (part(tok, cols), F32, whole(tok, cols)),
             (part(tok, cols), BF16, whole(tok, cols)),
             (part(8 * states, chans), F32, whole(8 * states, chans)),
             (part(8, chans), F32, whole(8, chans)),
             (part(states + 8, chans), F32, whole(states + 8, chans))],
            [f32_blk(tok, wide), f32_blk(tok, chans)],
            (counts, proj[g], tie(u[g]), wdt, bias_row, gains, dec8, spread[:, :wide]),
        )
        delta[g], normed[g], sn[g], einc[g], csd[g] = out[:5]
        mark(out[5])
        live_sums["e", g] = Entering(out[5], decay2, states, 1)

    def stage_h(g):
        ctl[0] = jnp.where(live, tie(cotangent), 0)
        mark(ctl[0])

    def stage_o(b):
        if 0 not in enter:
            enter[0] = live_sums["e", 0].result()
        out = run(
            functools.partial(out_kernel, states=states), b,
            [at_block(b, tok, chans), at_block(b, tok, chans), at_block(b, tok, cols),
             same(8 * states, chans), at_block(b, 8 * states, chans), at_block(b, 8, chans),
             at_block(b, states, chans), at_block(b, tok, chans), same(1, chans),
             same(2 * cols, 2 * wide), same(width, chans)],
            (delta[0], u[0], normed[0], dec8, einc[0], csd[0], enter[0], tie(z[0]), skip_row, spread,
             full_out),
            [("inner", (tok, chans), F32), ("gated", (tok, chans), BF16), ("branch", (tok, width), BF16)],
            [f32_blk(tok, 2 * wide), f32_blk(tok, chans), f32_blk(tok, chans), tmp_blk],
        )
        del buf["branch"]
        mark(out["branch"])
        live_sums["o", b] = Sum(out["branch"], "ch")

    def stage_f(b):
        kept, coming = live_sums["o", b].pair()
        deep = lambda *shape: pl.BlockSpec((1,) + shape, lambda i: (b, 0, i))
        outs = [
            (at_block(b, tok, width), F32, whole(tok, width)),
            (at_block(b, tok, width), BF16, whole(tok, width)),
            (deep(tok, tile), BF16, whole(tok, units)),
            (deep(tok, 2 * tile), BF16, whole(tok, 2 * units)),
            (same(tok, width), BF16, (tok, width)),
            (same(tok, width, at=b % 2), BF16, (2 * tok, width)),
        ]
        names = ["mid", "low2", "hidden", "gffn"]
        into = {i: buf[name] for i, name in enumerate(names)}
        if b % 2:
            into[5] = live_sums["down", b // 2]
        out = call(
            ffn_kernel, units // tile,
            [smem, at_block(b, tok, width), same(tok, width), same(tok, width),
             at_block(b, tok, width),
             pl.BlockSpec((width, 2 * tile), lambda i: (0, i)),
             pl.BlockSpec((width, tile), lambda i: (0, i))],
            outs, [f32_blk(tok, width), f32_blk(tok, width)],
            (at_end, tie(inputs), kept, coming, ctl[0], full_ffn, full_down),
            into,
        )
        for name, value in zip(names, out):
            buf[name] = value
        mark(out[4])
        live_sums["f", b] = Sum(out[4], "ch")
        live_sums["down", b // 2] = out[5]

    def stage_d(pair):
        live_sums["d", pair] = Sum(tie(live_sums["down", pair]), "ch")

    def row_part(b):
        return pl.BlockSpec((1, tok // 2, width), lambda i: (b, i, 0))

    def stage_q(b):
        kept, coming = live_sums["d", b // 2].pair()
        moved = pl.BlockSpec((tok // 2, width), lambda i: (2 * (b % 2) + i, 0))
        (buf["block"],) = call(
            add_kernel, 2, [smem, row_part(b), moved, moved],
            [(row_part(b), F32, whole(tok, width))], [],
            (at_end, tie(buf["mid"]), kept, coming), {0: buf["block"]},
        )
        mark(buf["block"])

    def flat(value):
        return value.reshape(-1, value.shape[-1])

    def stage_w(name):
        left, right = dict(
            down=lambda: (ctl[0], buf["hidden"]), ffn=lambda: (buf["low2"], buf["gffn"]),
            out=lambda: (buf["gml"], buf["gated"]), in_z=lambda: (low1[0], buf["gz"]),
            in_x=lambda: (low1[0], buf["low_xs"]),
        )[name]()
        left, right = flat(left), flat(right)
        deep, cut, wide_ = left.shape[0], width // WEIGHT_STEPS, right.shape[1]
        (grad,) = call(
            weight_kernel, WEIGHT_STEPS,
            [pl.BlockSpec((deep, cut), lambda i: (0, i)), same(deep, wide_)],
            [(pl.BlockSpec((cut, wide_), lambda i: (i, 0)), BF16, (width, wide_))], [],
            (left, tie(right)),
        )
        mark(grad)
        own[name] = scattered(grad)

    def stage_r(name):
        own[name] = tie(own[name])
        mark(own[name])

    def stage_b(b):
        kept, coming = live_sums["f", b].pair()
        out = run(
            functools.partial(back_state_kernel, states=states), b,
            [smem, at_block(b, tok, width), same(tok, width), same(tok, width),
             at_block(b, tok, width), same(width, chans)]
            + [at_block(b, tok, chans)] * 4
            + [at_block(b, tok, cols), same(8 * states, chans), same(1, chans), same(2 * cols, wide)],
            (at_end, buf["mid"], kept, coming, ctl[0], full_out, z[0], buf["inner"], delta[0],
             tie(u[0]), normed[0], dec8, skip_row, spread[:, wide:]),
            [("gm", (tok, width), F32), ("gml", (tok, width), BF16), ("gin", (tok, chans), F32),
             ("gz", (tok, chans), BF16), ("sinc", (8 * states, chans), F32),
             ("pay", (states + 8, chans), F32)],
            [f32_blk(tok, wide), tmp_blk],
            carry=("gskip", "gain2"),
        )
        mark(out["pay"])
        if b == batch - 1:
            live_sums["l", 0] = Entering(out["pay"], decay2, states, -1)

    def stage_m(b):
        if b == 0:
            live_sums["leave"] = live_sums["l", 0].result()
        out = run(
            functools.partial(back_kernel, states=states), b,
            [at_block(b, tok, chans), at_block(b, tok, chans), at_block(b, tok, cols),
             same(8 * states, chans), at_block(b, 8 * states, chans), at_block(b, 8, chans),
             at_block(b, states, chans), at_block(b, tok, chans), at_block(b, 8 * states, chans),
             at_block(b, states, chans), same(1, chans),
             same(2 * cols, 2 * wide), same(2 * wide, cols), same(cols, chans)],
            (delta[0], tie(u[0]), normed[0], dec8, einc[0], csd[0], enter[0], buf["gin"],
             buf["sinc"], live_sums["leave"], skip_row, spread, gathering, wdt),
            [("gpre", (tok, chans), BF16), ("gu1", (tok, chans), F32), ("gnorm", (tok, cols), BF16)],
            [f32_blk(tok, 2 * wide), f32_blk(tok, 2 * wide), f32_blk(tok, chans),
             f32_blk(tok, STATE_BLOCK * chans), f32_blk(tok, STATE_BLOCK * chans), f32_blk(tok, chans)]
            + [f32_blk(8 * states, chans)] * 3,
            carry=("gdec", "gbias"),
        )
        mark(out["gnorm"])
        if b % 2 == 1:
            live_sums["m", b // 2] = Sum(out["gnorm"][b - 1 : b + 1].reshape(2 * tok, cols), "ch")

    def stage_c(pair):
        kept, coming = live_sums["m", pair].pair()
        kept, coming = kept.reshape(2, tok, cols), coming.reshape(2, tok, cols)
        for b in (2 * pair, 2 * pair + 1):
            out = run(
                functools.partial(conv_back_kernel, rank=rank, states=states), b,
                [smem, at_block(b % 2, tok, cols), at_block(b % 2, tok, cols),
                 at_block(b, tok, cols), same(1, cols), at_block(b, tok, chans),
                 same(chans, cols), at_block(b, tok, chans), at_block(b, 8, chans),
                 same(taps, chans), same(1, chans)],
                (at_end, kept, coming, proj[0], gains, buf["gu1"], w_xproj, tie(xs[0]), edges[0],
                 conv_w, cb_row),
                [("gproj", (tok, cols), BF16), ("gxs", (tok, chans), F32), ("head", (8, chans), F32)],
                [f32_blk(tok + 8, chans), tmp_blk, f32_blk(tok, chans)],
                carry=("ggain", "gcw"),
            )
            mark(out["head"])
        live_sums["fix", pair] = shifted(out["head"][2 * pair : 2 * pair + 2], -1)

    def stage_x(b):
        out = run(
            functools.partial(in_grad_kernel, taps=taps), b,
            [at_block(b, tok, chans), at_block(b % 2, 8, chans), same(taps, chans),
             at_block(b, tok, chans), same(width, chans), same(width, chans),
             at_block(b, tok, width)],
            (buf["gxs"], live_sums["fix", b // 2], conv_w, buf["gz"], full_in_x, full_in_z,
             tie(inputs)),
            [("low_xs", (tok, chans), BF16), ("gn1", (tok, width), BF16)],
            carry=("gain1",),
        )
        del buf["gn1"]
        mark(out["gn1"])
        live_sums["x", b] = Sum(out["gn1"], "ch")

    def stage_e(b):
        kept, coming = live_sums["x", b].pair()
        moved = pl.BlockSpec((tok // 2, width), lambda i: (i, 0))
        (buf["grad_in"],) = call(
            end_kernel, 2, [smem, row_part(b), moved, moved, row_part(b)],
            [(row_part(b), F32, whole(tok, width))], [],
            (at_end, tie(inputs), kept, coming, buf["gm"]), {0: buf["grad_in"]},
        )
        mark(buf["grad_in"])

    def stage_g(name):
        total = jnp.sum(tie(buf["gain1"]), axis=0).reshape(8, width // 8)
        live_sums["g", 0] = Sum(total, "ch")

    def stage_n(name):
        gxproj = dot_tn(flat(buf["gproj"]), tie(flat(u[0])))
        gwdt = dot_tn(flat(sn[0]), flat(buf["gpre"]))[:rank]
        one = lambda v: jnp.sum(v, axis=0, keepdims=True)
        narrow = [live_sums["g", 0].result().reshape(width), one(buf["gain2"])[0], one(buf["ggain"])[0]]
        narrow = jnp.concatenate(narrow)
        narrow = jnp.pad(narrow, (0, -narrow.shape[0] % chans)).reshape(-1, chans)
        gcw = jnp.sum(buf["gcw"].reshape(taps + 1, 8, chans), axis=1)
        rows_of = [gxproj, gwdt, buf["gdec"] * decay, gcw, one(buf["gbias"]), one(buf["gskip"]), narrow]
        stacked = jnp.concatenate(rows_of, axis=0).astype(BF16)
        mark(stacked)
        live_sums["n", 0] = Cube(stacked, "seq")
        own["marks"] = [r.shape[0] for r in rows_of]

    stages = dict(
        A=stage_a, Z=stage_z, S=stage_s, O=stage_o, H=stage_h, F=stage_f, D=stage_d, W=stage_w,
        B=stage_b, M=stage_m, C=stage_c, X=stage_x, E=stage_e, Q=stage_q, R=stage_r, N=stage_n, G=stage_g,
    )
    for step in ORDER:
        rest = step[1:]
        rest = int(rest) if rest.isdigit() else rest
        if step[0].islower():
            live_sums[step[0], rest].advance(tie, mark)
        else:
            stages[step[0]](rest)

    split_ffn = own["ffn"].reshape(own_rows, units // tile, 2, tile)
    own["stacked"] = live_sums["n", 0].result().astype(F32)
    marks = [0]
    for count in own["marks"]:
        marks.append(marks[-1] + count)
    cut = [own["stacked"][a:b] for a, b in zip(marks[:-1], marks[1:])]
    narrow = cut[6].reshape(-1)
    local = norm1_gain.shape[0]
    at = lax.axis_index("seq") * local
    own_one = lax.dynamic_slice(narrow, (at,), (local,)) / gain_one[:, 0]
    own_two = lax.dynamic_slice(narrow, (width + at,), (local,)) / gain_two[:, 0]
    ggain = narrow[2 * width : 2 * width + cols]
    return (
        buf["block"],
        buf["grad_in"],
        own_one,
        own["in_x"] * gain_one,
        own["in_z"] * gain_one,
        cut[3][:taps],
        cut[3][taps],
        cut[0].T,
        ggain[:rank],
        ggain[rank : rank + states],
        ggain[rank + states :],
        cut[1],
        cut[4][0],
        cut[2],
        cut[5][0],
        own["out"].T,
        own_two,
        split_ffn[:, :, 0].reshape(own_rows, units) * gain_two,
        split_ffn[:, :, 1].reshape(own_rows, units) * gain_two,
        own["down"].T,
    )


def solution(mesh):
    return jax.shard_map(
        on_device,
        mesh=mesh,
        in_specs=(
            P(None, "seq", None),
            P(),
            P("seq"),
            P("seq", "ch"),
            P("seq", "ch"),
            P(None, "ch"),
            P("ch"),
            P("ch", None),
            P(),
            P(),
            P(),
            P(None, "ch"),
            P("ch"),
            P(None, "ch"),
            P("ch"),
            P("ch", "seq"),
            P("seq"),
            P("seq", "ch"),
            P("seq", "ch"),
            P("ch", "seq"),
            P(None, "seq", None),
        ),
        out_specs=(
            P(None, "seq", None),
            P(None, "seq", None),
            P("seq"),
            P("seq", "ch"),
            P("seq", "ch"),
            P(None, "ch"),
            P("ch"),
            P("ch", None),
            P(),
            P(),
            P(),
            P(None, "ch"),
            P("ch"),
            P(None, "ch"),
            P("ch"),
            P("ch", "seq"),
            P("seq"),
            P("seq", "ch"),
            P("seq", "ch"),
            P("ch", "seq"),
        ),
        check_vma=False,
    )
```

```python
import functools

import jax
import jax.numpy as jnp
from jax import lax
from jax.experimental import pallas as pl
from jax.experimental.pallas import tpu as pltpu
from jax.sharding import PartitionSpec as P

EPS = 1e-05
LOG2E = 1.4426950408889634
LANE = 128
CHUNKS = 8
UNROLL = 8
FORWARD_UNROLL = 4
BACK_UNROLL = 4
STATE_BLOCK = 2
WEIGHT_STEPS = 3
GROUPS = 1
ORDER = (
    "A0", "p0", "H0", "p0", "S0", "Z0", "e0", "O0", "O1", "O2", "o0", "O3", "o1", "o0", "o2", "o1",
    "F0", "o3", "o2", "F1", "f0", "o3", "F2", "f1", "f0", "F3", "Wdown", "Tdown", "f2", "f1", "B0",
    "f3", "f2", "D0", "B1", "f3", "B2", "d0", "B3", "D1", "Wffn", "l0", "Wout", "Win_z", "M0",
    "d0", "d1", "Tffn", "Tout", "Tin_z", "M1", "M2", "m0", "M3", "Q0", "Q1", "m0", "Rdown", "C0",
    "m1", "X0", "m1", "C1", "d1", "X1", "x0", "X2", "x1", "x0", "X3", "x2", "x1", "Q2", "Q3", "G0",
    "E0", "Win_x", "Tin_x", "N0", "x3", "x2", "Rffn", "E1", "n0", "x3", "n0", "E2", "Rout",
    "Rin_z", "E3",
)
F32 = jnp.float32
BF16 = jnp.bfloat16
VMEM_LIMIT = 48 * 1024 * 1024


def tree_sum(parts):
    parts = list(parts)
    while len(parts) > 1:
        parts = [
            parts[i] + parts[i + 1] if i + 1 < len(parts) else parts[i]
            for i in range(0, len(parts), 2)
        ]
    return parts[0]


def dot(left, right):
    return jnp.dot(left, right, preferred_element_type=F32)


def dot_nt(left, right):
    return lax.dot_general(left, right, (((1,), (1,)), ((), ())), preferred_element_type=F32)


def dot_tn(left, right):
    return lax.dot_general(left, right, (((0,), (0,)), ((), ())), preferred_element_type=F32)


def sigmoid(value):
    return 1.0 / (1.0 + jnp.exp(-value))


def split_low(value):
    high = value.astype(BF16)
    rest = (value - high.astype(F32)).astype(BF16)
    return jnp.concatenate([high, rest], axis=1)


def segment_rows(value, rank, states):
    lane = lax.broadcasted_iota(jnp.int32, value.shape, 1)
    first = lane < rank
    last = lane >= rank + states
    middle = jnp.logical_not(jnp.logical_or(first, last))
    means = []
    for mask, count in ((first, rank), (middle, states), (last, states)):
        means.append(jnp.sum(jnp.where(mask, value, 0.0), axis=1, keepdims=True) / count)
    return jnp.where(first, means[0], jnp.where(last, means[2], means[1]))


def load_padded(pad_ref, edge_ref, xs_ref, tok):
    pad_ref[0:8, :] = edge_ref[0].astype(F32)
    pad_ref[8 : 8 + tok, :] = xs_ref[0].astype(F32)


def conv_of(pad_ref, conv_w, conv_b, tok, taps):
    out = conv_b
    for k in range(taps):
        start = 8 - (taps - 1) + k
        out = out + conv_w[k : k + 1, :] * pad_ref[start : start + tok, :]
    return out


def picked(end_ref, kept_ref, coming_ref):
    kept, coming = kept_ref[...], coming_ref[...]
    return jnp.where(end_ref[0] == 1, coming, kept).astype(F32)


def partial_rows(value):
    return jnp.sum(value.reshape(value.shape[0] // 8, 8, value.shape[1]), axis=0)


def to_scan_order(value, tmp_ref, dst_ref):
    tok, chans = value.shape
    steps = tok // CHUNKS
    for j in range(chans // LANE):
        tmp_ref[j] = value[:, col(j)]
        for t in range(steps):
            dst_ref[8 * t : 8 * t + 8, col(j)] = tmp_ref[j, pl.ds(t, 8, stride=steps), :]


def to_natural_order(value, tmp_ref, dst_ref):
    tok, chans = value.shape
    steps = tok // CHUNKS
    for j in range(chans // LANE):
        tmp_ref[j] = value[:, col(j)]
        for k in range(CHUNKS):
            for t in range(0, steps, 8):
                dst_ref[k * steps + t : k * steps + t + 8, col(j)] = tmp_ref[
                    j, pl.ds(8 * t + k, 8, stride=8), :
                ]


def pre_kernel(xs_ref, edge_ref, cw_ref, cb_ref, wxp_ref, u_ref, proj_ref, pad, nat, per):
    tok, taps = xs_ref.shape[1], cw_ref.shape[0]
    load_padded(pad, edge_ref, xs_ref, tok)
    conv = conv_of(pad, cw_ref[...], cb_ref[...], tok, taps)
    to_scan_order(conv * sigmoid(conv), nat, per)
    u_low = per[...].astype(BF16)
    u_ref[0] = u_low
    proj_ref[0] = dot(u_low, wxp_ref[...]).astype(BF16)


def lanes_at(j):
    return pl.ds(pl.multiple_of(j * LANE, LANE), LANE)


def rows_at(t):
    return pl.ds(pl.multiple_of(t * 8, 8), 8)


def col(n):
    return slice(n * LANE, (n + 1) * LANE)


def chunk_prefix(prod, value, backwards):
    place = lax.broadcasted_iota(jnp.int32, value.shape, 0)
    for step in (1, 2, 4):
        shift = CHUNKS - step if backwards else step
        keep = place < CHUNKS - step if backwards else place >= step
        prod_far = jnp.where(keep, pltpu.roll(prod, shift, 0), 1.0)
        value_far = jnp.where(keep, pltpu.roll(value, shift, 0), 0.0)
        value = prod * value_far + value
        prod = prod * prod_far
    return value


def sum_prefix(value):
    place = lax.broadcasted_iota(jnp.int32, value.shape, 0)
    for step in (1, 2, 4):
        value = value + jnp.where(place >= step, pltpu.roll(value, step, 0), 0.0)
    return value


def state_kernel(
    cnt_ref, proj_ref, u_ref, wdt_ref, bias_ref, gain_ref, dec_ref, eb_ref,
    delta_ref, normed_ref, sn_ref, einc_ref, csd_ref, pay_ref, bb, du,
    *, rank, states,
):
    tok, chans = u_ref.shape[1], u_ref.shape[2]
    steps = tok // CHUNKS
    value = proj_ref[0]
    scale = lax.rsqrt(segment_rows(value * value, rank, states) + EPS)
    normed = value * scale * gain_ref[...]
    normed_ref[0] = normed
    lane = lax.broadcasted_iota(jnp.int32, value.shape, 1)
    step_low = jnp.where(lane < rank, normed, 0.0).astype(BF16)
    sn_ref[0] = step_low
    pre = dot(step_low, wdt_ref[...]) + bias_ref[...]
    row = lax.broadcasted_iota(jnp.int32, pre.shape, 0)
    place = (row & 7) * steps + (row >> 3)
    live = place < cnt_ref[pl.program_id(0)]
    soft = jnp.maximum(pre, 0.0) + jnp.log(1.0 + jnp.exp(-jnp.abs(pre)))
    delta = jnp.where(live, soft, 0.0)
    delta_ref[0] = delta
    du[...] = delta * u_ref[0].astype(F32)
    bb[...] = dot(split_low(normed), eb_ref[...])

    def tile(j, carry):
        lanes = lanes_at(j)
        dec = [dec_ref[8 * n : 8 * n + 8, lanes] for n in range(states)]

        def step(i, carry):
            ends, total = carry
            for q in range(UNROLL):
                rows = rows_at(i * UNROLL + q)
                d = delta_ref[0, rows, lanes]
                v = du[rows, lanes]
                ends = tuple(
                    jnp.exp2(d * dec[n]) * ends[n] + v * bb[rows, col(n)] for n in range(states)
                )
                total = total + d
            return ends, total

        zero = jnp.zeros((8, LANE), F32)
        ends, total = lax.fori_loop(0, steps // UNROLL, step, ((zero,) * states, zero))
        csd = sum_prefix(total)
        csd_ref[0, :, lanes] = csd
        for n in range(states):
            inc = chunk_prefix(jnp.exp2(dec[n] * total), ends[n], False)
            einc_ref[0, 8 * n : 8 * n + 8, lanes] = inc
            pay_ref[0, n : n + 1, lanes] = inc[7:8, :]
        pay_ref[0, states : states + 8, lanes] = jnp.broadcast_to(csd[7:8, :], (8, LANE))
        return carry

    lax.fori_loop(0, chans // LANE, tile, 0)


def start_states(dec, csd, einc_ref, enter_ref, lanes, states):
    place = lax.broadcasted_iota(jnp.int32, csd.shape, 0)
    before = jnp.where(place >= 1, pltpu.roll(csd, 1, 0), 0.0)
    out = []
    for n in range(states):
        own = jnp.where(place >= 1, pltpu.roll(einc_ref[0, 8 * n : 8 * n + 8, lanes], 1, 0), 0.0)
        out.append(own + jnp.exp2(dec[n] * before) * enter_ref[0, n : n + 1, lanes])
    return tuple(out)


def out_kernel(
    delta_ref, u_ref, normed_ref, dec_ref, einc_ref, csd_ref, enter_ref, z_ref, skip_ref, eb_ref,
    wout_ref, inner_ref, gated_ref, branch_ref, bc, du, per, tmp, *, states,
):
    tok, chans = u_ref.shape[1], u_ref.shape[2]
    steps = tok // CHUNKS
    bc[...] = dot(split_low(normed_ref[0]), eb_ref[...])
    u_val = u_ref[0].astype(F32)
    du[...] = delta_ref[0] * u_val
    per[...] = skip_ref[...] * u_val

    def tile(j, carry):
        lanes = lanes_at(j)
        dec = [dec_ref[8 * n : 8 * n + 8, lanes] for n in range(states)]

        def step(i, hs):
            for q in range(UNROLL):
                rows = rows_at(i * UNROLL + q)
                d = delta_ref[0, rows, lanes]
                v = du[rows, lanes]
                hs = tuple(
                    jnp.exp2(d * dec[n]) * hs[n] + v * bc[rows, col(n)] for n in range(states)
                )
                per[rows, lanes] += tree_sum(
                    hs[n] * bc[rows, col(states + n)] for n in range(states)
                )
            return hs

        first = start_states(dec, csd_ref[0, :, lanes], einc_ref, enter_ref, lanes, states)
        lax.fori_loop(0, steps // UNROLL, step, first)
        return carry

    lax.fori_loop(0, chans // LANE, tile, 0)
    to_natural_order(per[...], tmp, du)
    inner = du[...]
    inner_ref[0] = inner
    z_val = z_ref[0].astype(F32)
    gated = (inner * z_val * sigmoid(z_val)).astype(BF16)
    gated_ref[0] = gated
    branch_ref[...] = dot_nt(gated, wout_ref[...]).astype(BF16)


def back_state_kernel(
    edge_ref, mid_ref, kept_ref, coming_ref, ctl_ref, wout_ref, z_ref, inner_ref, delta_ref, u_ref,
    normed_ref, dec_ref, skip_ref, ec_ref, gskip_in, gain_in,
    gm_ref, gml_ref, gin_ref, gz_ref, sinc_ref, pay_ref, gskip_ref, gain_ref, cb, nat, *, states,
):
    tok, chans = u_ref.shape[1], u_ref.shape[2]
    steps = tok // CHUNKS
    mid = mid_ref[0]
    grad = picked(edge_ref, kept_ref, coming_ref)
    scale = lax.rsqrt(jnp.mean(mid * mid, axis=-1, keepdims=True) + EPS)
    by_mid = mid * grad
    mean = jnp.mean(by_mid, axis=-1, keepdims=True)
    gain_ref[...] = gain_in[...] + partial_rows(by_mid * scale)
    gm = ctl_ref[0].astype(F32) + scale * grad - (scale * scale * scale * mean) * mid
    gm_ref[0] = gm
    gml_ref[0] = gm.astype(BF16)
    gg = dot(gml_ref[0], wout_ref[...])
    cb[...] = dot(split_low(normed_ref[0]), ec_ref[...])
    z_val = z_ref[0].astype(F32)
    sig = sigmoid(z_val)
    gin = gin_ref.at[0]
    to_scan_order(gg * z_val * sig, nat, gin)
    gz_ref[0] = (gg * inner_ref[0] * sig * (1.0 + z_val * (1.0 - sig))).astype(BF16)

    gskip_ref[...] = gskip_in[...] + partial_rows(gin[...] * u_ref[0].astype(F32))

    def tile(j, carry):
        lanes = lanes_at(j)
        dec = [dec_ref[8 * n : 8 * n + 8, lanes] for n in range(states)]

        def step(i, carry):
            flow, total = carry
            for q in range(UNROLL):
                rows = rows_at(steps - 1 - (i * UNROLL + q))
                d = delta_ref[0, rows, lanes]
                g = gin[rows, lanes]
                flow = tuple(
                    jnp.exp2(d * dec[n]) * (flow[n] + g * cb[rows, col(n)]) for n in range(states)
                )
                total = total + d
            return flow, total

        zero = jnp.zeros((8, LANE), F32)
        flow, total = lax.fori_loop(0, steps // UNROLL, step, ((zero,) * states, zero))
        for n in range(states):
            inc = chunk_prefix(jnp.exp2(dec[n] * total), flow[n], True)
            sinc_ref[0, 8 * n : 8 * n + 8, lanes] = inc
            pay_ref[0, n : n + 1, lanes] = inc[0:1, :]
        full = jnp.sum(total, axis=0, keepdims=True)
        pay_ref[0, states : states + 8, lanes] = jnp.broadcast_to(full, (8, LANE))
        return carry

    lax.fori_loop(0, chans // LANE, tile, 0)


def back_kernel(
    delta_ref, u_ref, normed_ref, dec_ref, einc_ref, csd_ref, enter_ref, gin_ref, sinc_ref,
    leave_ref, skip_ref, eb_ref, ebt_ref, wdt_ref, gdec_in, gbias_in,
    gpre_ref, gu_ref, gnorm_ref, gdec_ref, gbias_ref, bc, acc, du, fac, prev, gstep,
    enter8, leave8, logs8,
    *, states,
):
    tok, chans = u_ref.shape[1], u_ref.shape[2]
    steps, tiles = tok // CHUNKS, chans // LANE
    bc[...] = dot(split_low(normed_ref[0]), eb_ref[...])
    du[...] = delta_ref[0] * u_ref[0].astype(F32)
    gu_ref[0] = jnp.zeros((tok, chans), F32)
    gstep[...] = jnp.zeros((tok, chans), F32)
    for n in range(states):
        rows = slice(8 * n, 8 * n + 8)
        enter8[rows, :] = jnp.broadcast_to(enter_ref[0, n : n + 1, :], (8, chans))
        leave8[rows, :] = jnp.broadcast_to(leave_ref[0, n : n + 1, :], (8, chans))
    place = lax.broadcasted_iota(jnp.int32, (8, LANE), 0)
    pairs = [(q, j) for q in range(STATE_BLOCK) for j in range(tiles)]

    def block(i, carry):
        ns = [i * STATE_BLOCK + q for q in range(STATE_BLOCK)]
        rows_of = [rows_at(n) for n in ns]
        at_b = [lanes_at(n) for n in ns]
        at_c = [lanes_at(n + states) for n in ns]
        dec = {(q, j): dec_ref[rows_of[q], col(j)] for q, j in pairs}
        first, last = [], []
        for q, j in pairs:
            csd = csd_ref[0, :, col(j)]
            before = jnp.where(place >= 1, pltpu.roll(csd, 1, 0), 0.0)
            own = jnp.where(place >= 1, pltpu.roll(einc_ref[0, rows_of[q], col(j)], 1, 0), 0.0)
            first.append(own + jnp.exp2(dec[q, j] * before) * enter8[rows_of[q], col(j)])
            after = csd[7:8, :] - csd
            own = jnp.where(place < 7, pltpu.roll(sinc_ref[0, rows_of[q], col(j)], 7, 0), 0.0)
            last.append(own + jnp.exp2(dec[q, j] * after) * leave8[rows_of[q], col(j)])

        def forward(t, hs):
            for r in range(FORWARD_UNROLL):
                rows = rows_at(t * FORWARD_UNROLL + r)
                d = [delta_ref[0, rows, col(j)] for j in range(tiles)]
                v = [du[rows, col(j)] for j in range(tiles)]
                g = [gin_ref[0, rows, col(j)] for j in range(tiles)]
                b = [bc[rows, at] for at in at_b]
                new = []
                for k, (q, j) in enumerate(pairs):
                    a = jnp.exp2(d[j] * dec[q, j])
                    p = a * hs[k]
                    fac[rows, col(k)] = a
                    prev[rows, col(k)] = p
                    new.append(p + v[j] * b[q])
                hs = tuple(new)
                for q in range(STATE_BLOCK):
                    acc[rows, at_c[q]] = tree_sum(hs[q * tiles + j] * g[j] for j in range(tiles))
            return hs

        lax.fori_loop(0, steps // FORWARD_UNROLL, forward, tuple(first))

        def backward(t, carry):
            flow, logs = carry
            for r in range(BACK_UNROLL):
                rows = rows_at(steps - 1 - (t * BACK_UNROLL + r))
                d = [delta_ref[0, rows, col(j)] for j in range(tiles)]
                v = [du[rows, col(j)] for j in range(tiles)]
                g = [gin_ref[0, rows, col(j)] for j in range(tiles)]
                b = [bc[rows, at] for at in at_b]
                c = [bc[rows, at] for at in at_c]
                new_flow, new_logs, grads, scaled = [], [], [], []
                for k, (q, j) in enumerate(pairs):
                    grad = flow[k] + g[j] * c[q]
                    gp = grad * prev[rows, col(k)]
                    new_flow.append(fac[rows, col(k)] * grad)
                    new_logs.append(logs[k] + gp * d[j])
                    scaled.append(gp * dec[q, j])
                    grads.append(grad)
                flow, logs = tuple(new_flow), tuple(new_logs)
                for j in range(tiles):
                    gu_ref[0, rows, col(j)] += tree_sum(
                        grads[q * tiles + j] * b[q] for q in range(STATE_BLOCK)
                    )
                    gstep[rows, col(j)] += tree_sum(
                        scaled[q * tiles + j] for q in range(STATE_BLOCK)
                    )
                for q in range(STATE_BLOCK):
                    acc[rows, at_b[q]] = tree_sum(grads[q * tiles + j] * v[j] for j in range(tiles))
            return flow, logs

        zero = jnp.zeros((8, LANE), F32)
        unused, logs = lax.fori_loop(
            0, steps // BACK_UNROLL, backward, (tuple(last), (zero,) * len(pairs))
        )
        for k, (q, j) in enumerate(pairs):
            logs8[rows_of[q], col(j)] = logs[k]
        return carry

    lax.fori_loop(0, states // STATE_BLOCK, block, 0)
    for n in range(states):
        total = jnp.sum(logs8[8 * n : 8 * n + 8, :], axis=0, keepdims=True)
        gdec_ref[n : n + 1, :] = gdec_in[n : n + 1, :] + total
    delta = delta_ref[0]
    drive = gu_ref[0]
    gdelta = gstep[...] * (1.0 / LOG2E) + drive * u_ref[0].astype(F32)
    gu_ref[0] = drive * delta + skip_ref[...] * gin_ref[0]
    small = delta * (1.0 - delta * (0.5 - delta * (1.0 / 6.0)))
    slope = jnp.where(delta < 0.01, small, 1.0 - jnp.exp(-delta))
    gpre = (gdelta * slope).astype(BF16)
    gpre_ref[0] = gpre
    gbias_ref[...] = gbias_in[...] + partial_rows(gpre.astype(F32))
    gnorm = dot_nt(gpre, wdt_ref[...]) + dot(acc[...].astype(BF16), ebt_ref[...])
    gnorm_ref[0] = gnorm.astype(BF16)


def conv_back_kernel(
    end_ref, kept_ref, coming_ref, proj_ref, gain_ref, gu_ref, wxp_ref, xs_ref, edge_ref, cw_ref,
    cb_ref, ggain_in, gcw_in, gproj_ref, gxs_ref, head_ref, ggain_ref, gcw_ref, pad, per, nat,
    *, rank, states,
):
    tok, taps = xs_ref.shape[1], cw_ref.shape[0]
    grad = picked(end_ref, kept_ref, coming_ref)[0]
    value = proj_ref[0]
    scale = lax.rsqrt(segment_rows(value * value, rank, states) + EPS)
    by_gain = gain_ref[...] * grad
    mean = segment_rows(value * by_gain, rank, states)
    gproj = (scale * by_gain - scale * scale * scale * value * mean).astype(BF16)
    gproj_ref[0] = gproj
    ggain_ref[...] = ggain_in[...] + partial_rows(grad * value * scale)
    to_natural_order(gu_ref[0] + dot_nt(gproj, wxp_ref[...]), per, nat)
    load_padded(pad, edge_ref, xs_ref, tok)
    conv = conv_of(pad, cw_ref[...], cb_ref[...], tok, taps)
    sig = sigmoid(conv)
    gconv = nat[...] * sig * (1.0 + conv * (1.0 - sig))
    for k in range(taps):
        start = 8 - (taps - 1) + k
        gcw_ref[8 * k : 8 * k + 8, :] = gcw_in[8 * k : 8 * k + 8, :] + partial_rows(
            gconv * pad[start : start + tok, :]
        )
    gcw_ref[8 * taps :, :] = gcw_in[8 * taps :, :] + partial_rows(gconv)
    head_ref[0] = gconv[0:8, :]
    pad[0:tok, :] = gconv
    pad[tok : tok + 8, :] = jnp.zeros((8, gconv.shape[1]), F32)
    gxs = cw_ref[taps - 1 : taps, :] * gconv
    for k in range(taps - 1):
        ahead = taps - 1 - k
        gxs = gxs + cw_ref[k : k + 1, :] * pad[ahead : ahead + tok, :]
    gxs_ref[0] = gxs


def ffn_kernel(
    end_ref, x_ref, kept_ref, coming_ref, ctl_ref, w_ref, wd_ref,
    mid_ref, low_ref, hid_ref, gffn_ref, gn_ref, down_ref, gn_acc, down_acc,
):
    step = pl.program_id(0)

    @pl.when(step == 0)
    def _():
        mid = x_ref[0].astype(F32) + picked(end_ref, kept_ref, coming_ref)
        mid_ref[0] = mid
        scale = lax.rsqrt(jnp.mean(mid * mid, axis=-1, keepdims=True) + EPS)
        low_ref[0] = (mid * scale).astype(BF16)

    weight = w_ref[...]
    units = weight.shape[1] // 2
    both = dot(low_ref[0], weight)
    back = dot(ctl_ref[0], wd_ref[...])
    gate, up = both[:, :units], both[:, units:]
    sig = sigmoid(gate)
    act = gate * sig
    hid = (act * up).astype(BF16)
    hid_ref[0] = hid
    ggate = (back * up * (sig * (1.0 + gate - act))).astype(BF16)
    gffn = jnp.concatenate([ggate, (back * act).astype(BF16)], axis=1)
    gffn_ref[0] = gffn
    gn = dot_nt(gffn, weight)
    down = dot_nt(hid, wd_ref[...])

    @pl.when(step == 0)
    def _():
        gn_acc[...] = gn
        down_acc[...] = down

    @pl.when(step > 0)
    def _():
        gn_acc[...] += gn
        down_acc[...] += down

    @pl.when(step == pl.num_programs(0) - 1)
    def _():
        gn_ref[...] = gn_acc[...].astype(BF16)
        down_ref[...] = down_acc[...].astype(BF16)


def add_kernel(end_ref, mid_ref, kept_ref, coming_ref, out_ref):
    out_ref[0] = mid_ref[0] + picked(end_ref, kept_ref, coming_ref)


def in_grad_kernel(
    gxs_ref, ahead_ref, cw_ref, gz_ref, wx_ref, wz_ref, x_ref, gain_in,
    low_ref, gn_ref, gain_ref, *, taps,
):
    tok = gxs_ref.shape[1]
    row = lax.broadcasted_iota(jnp.int32, (8, gxs_ref.shape[2]), 0)
    ahead = ahead_ref[0]
    fix = jnp.zeros((8, gxs_ref.shape[2]), F32)
    for k in range(taps - 1):
        start = 8 - (taps - 1 - k)
        moved = pltpu.roll(ahead, start, 0)
        fix = fix + jnp.where(row >= start, cw_ref[k : k + 1, :] * moved, 0.0)
    main = gxs_ref[0]
    low = jnp.concatenate([main[: tok - 8], main[tok - 8 :] + fix], axis=0).astype(BF16)
    low_ref[0] = low
    gn = dot_nt(low, wx_ref[...]) + dot_nt(gz_ref[0], wz_ref[...])
    x = x_ref[0].astype(F32)
    scale = lax.rsqrt(jnp.mean(x * x, axis=-1, keepdims=True) + EPS)
    gain_ref[...] = gain_in[...] + partial_rows(gn * x * scale)
    gn_ref[...] = gn.astype(BF16)


def end_kernel(end_ref, x_ref, kept_ref, coming_ref, gm_ref, out_ref):
    x = x_ref[0].astype(F32)
    grad = picked(end_ref, kept_ref, coming_ref)
    scale = lax.rsqrt(jnp.mean(x * x, axis=-1, keepdims=True) + EPS)
    mean = jnp.mean(x * grad, axis=-1, keepdims=True)
    out_ref[0] = gm_ref[0] + scale * grad - (scale * scale * scale * mean) * x


def weight_kernel(left_ref, right_ref, out_ref):
    out_ref[...] = dot_tn(left_ref[...], right_ref[...]).astype(BF16)


def part(*shape, at=0):
    return pl.BlockSpec((1,) + shape, lambda i: (i + at,) + (0,) * len(shape))


def slot(*shape, at):
    return pl.BlockSpec((1,) + shape, lambda i: (at,) + (0,) * len(shape))


def same(*shape, at=0):
    return pl.BlockSpec(shape, lambda i: (at,) + (0,) * (len(shape) - 1))


def call(body, count, in_specs, outs, scratch, args, into=None, carry=None):
    into, carry = into or {}, carry or {}
    fixed = len(args)
    kept = sorted(k for k in into if into[k] is not None)
    args = tuple(args) + tuple(into[k] for k in kept)
    in_specs = list(in_specs) + [pl.BlockSpec(memory_space=pl.ANY)] * len(kept)
    aliases = {fixed + i: k for i, k in enumerate(kept)}
    aliases.update({arg: out for out, arg in carry.items()})

    def run(*refs):
        body(*refs[:fixed], *refs[fixed + len(kept) :])

    return pl.pallas_call(
        run,
        grid=(count,),
        in_specs=in_specs,
        out_specs=[spec for spec, kind, shape in outs],
        out_shape=[jax.ShapeDtypeStruct(shape, kind) for spec, kind, shape in outs],
        scratch_shapes=scratch,
        input_output_aliases=aliases,
        compiler_params=pltpu.CompilerParams(vmem_limit_bytes=VMEM_LIMIT),
        cost_estimate=pl.CostEstimate(flops=0, bytes_accessed=0, transcendentals=0),
    )(*args)


class Sum:
    def __init__(self, value, axis):
        self.axis, self.hops, self.kept = axis, 0, value
        if lax.axis_size(axis) != 4:
            self.hops, self.kept = 3, lax.psum(value, axis)
            return
        self.coming = lax.ppermute(value, axis, [(0, 1), (3, 2)])

    def advance(self, tie, mark):
        if self.hops >= 2:
            return
        self.kept = self.kept + tie(self.coming)
        mark(self.kept)
        route = [(1, 0), (2, 3)] if self.hops else [(1, 2), (2, 1)]
        self.coming = lax.ppermute(self.kept, self.axis, route)
        self.hops += 1

    def result(self):
        while self.hops < 2:
            self.advance(lambda v: v, lambda v: None)
        if self.hops == 2:
            place = lax.axis_index(self.axis)
            at_end = jnp.logical_or(place == 0, place == 3)
            self.kept, self.hops = jnp.where(at_end, self.coming, self.kept), 3
        return self.kept

    def pair(self):
        while self.hops < 2:
            self.advance(lambda v: v, lambda v: None)
        return (self.kept, self.coming if self.hops == 2 else self.kept)


def shifted(value, distance):
    size = lax.axis_size("seq")
    route = [(i, i + distance) for i in range(size) if 0 <= i + distance < size]
    return lax.ppermute(value, "seq", route)


class Cube:
    def __init__(self, value, axis):
        self.value, self.axis, self.size, self.bit = value, axis, lax.axis_size(axis), 1
        if self.size & (self.size - 1):
            self.value, self.bit = lax.psum(value, axis), self.size
        self.send()

    def send(self):
        if self.bit < self.size:
            route = [(i, i ^ self.bit) for i in range(self.size)]
            self.coming = lax.ppermute(self.value, self.axis, route)

    def advance(self, tie, mark):
        if self.bit < self.size:
            self.value = self.value + tie(self.coming)
            mark(self.value)
            self.bit *= 2
            self.send()

    def result(self):
        while self.bit < self.size:
            self.advance(lambda v: v, lambda v: None)
        return self.value


class Entering:
    def __init__(self, payload, decay, states, sign):
        self.decay, self.states, self.sign = decay, states, sign
        self.size = lax.axis_size("seq")
        self.reach = min(4, self.size - 1)
        packed = self.pack((payload[:, :states], payload[:, states : states + 1]))
        self.parts = [shifted(packed, sign * k) for k in range(1, self.reach + 1)]
        self.total = None

    def pack(self, pair):
        value, length = pair
        high = lax.optimization_barrier(length.astype(BF16))
        low = (length - high.astype(F32)).astype(BF16)
        return jnp.concatenate([value.astype(BF16), high, low], axis=1)

    def unpack(self, packed):
        whole = packed.astype(F32)
        value, high = whole[:, : self.states], whole[:, self.states : self.states + 1]
        return value, high + whole[:, self.states + 1 :]

    def join(self, far, near):
        return jnp.exp2(self.decay[None] * near[1]) * far[0] + near[0], far[1] + near[1]

    def advance(self, tie, mark):
        total = self.unpack(tie(self.parts[-1]))
        for near in self.parts[-2::-1]:
            total = self.join(total, self.unpack(near))
        self.total = total
        mark(total[0])
        if self.reach < self.size - 1:
            self.coming = shifted(self.pack(total), self.sign * self.reach)

    def result(self):
        if self.total is None:
            self.advance(lambda v: v, lambda v: None)
        while self.reach < self.size - 1:
            self.total = self.join(self.unpack(self.coming), self.total)
            self.reach *= 2
            if self.reach < self.size - 1:
                self.coming = shifted(self.pack(self.total), self.sign * self.reach)
        return self.total[0]


def on_device(
    inputs, lengths, norm1_gain, w_in_x, w_in_z, conv_w, conv_b, w_xproj, dt_gain, b_gain, c_gain,
    w_dt, dt_bias, decay_log, skip_d, w_out, norm2_gain, w_gate, w_up, w_down, cotangent,
):
    batch, tok, width = inputs.shape
    chans = conv_w.shape[1]
    taps = conv_w.shape[0]
    rank, states = dt_gain.shape[0], b_gain.shape[0]
    cols = w_xproj.shape[1]
    per = batch // GROUPS
    rows = per * tok
    groups = range(GROUPS)

    def gather(weight):
        return lax.all_gather(weight, "seq", axis=0, tiled=True)

    gain_one = norm1_gain.astype(F32)[:, None]
    gain_two = norm2_gain.astype(F32)[:, None]
    full_in_x = gather((w_in_x.astype(F32) * gain_one).astype(BF16))
    full_in_z = gather((w_in_z.astype(F32) * gain_one).astype(BF16))
    full_out = gather(w_out.T)
    full_down = gather(w_down.T)
    low_gate = (w_gate.astype(F32) * gain_two).astype(BF16)
    low_up = (w_up.astype(F32) * gain_two).astype(BF16)
    units, tile = w_gate.shape[1], w_gate.shape[1]
    own_rows = w_gate.shape[0]
    both_ffn = jnp.stack([low_gate.reshape(own_rows, -1, tile), low_up.reshape(own_rows, -1, tile)], 2)
    full_ffn = gather(both_ffn.reshape(own_rows, 2 * units))

    first_place = lax.axis_index("seq") * tok
    counts = jnp.clip(lengths - first_place, 0, tok)
    live = (jnp.arange(tok, dtype=jnp.int32)[None, :] < counts[:, None])[:, :, None]
    decay = -jnp.exp(decay_log)
    decay2 = decay * LOG2E
    dec8 = jnp.repeat(decay2, 8, axis=0)
    k_of = lax.broadcasted_iota(jnp.int32, (2 * cols, 2 * states * LANE), 0) % cols
    c_of = lax.broadcasted_iota(jnp.int32, (2 * cols, 2 * states * LANE), 1) // LANE
    spread = (k_of == c_of + rank).astype(BF16)
    k_of = lax.broadcasted_iota(jnp.int32, (2 * states * LANE, cols), 1)
    c_of = lax.broadcasted_iota(jnp.int32, (2 * states * LANE, cols), 0) // LANE
    gathering = (k_of == c_of + rank).astype(BF16)
    gains = jnp.concatenate([dt_gain, b_gain, c_gain])[None]
    wdt = jnp.pad(w_dt, ((0, cols - rank), (0, 0)))
    cb_row, bias_row, skip_row = conv_b[None], dt_bias[None], skip_d[None]

    def unit(value):
        return value * lax.rsqrt(jnp.mean(value * value, axis=-1, keepdims=True) + EPS)

    edge_in = shifted(inputs[:, tok - 8 :, :], 1)
    edge_low = unit(edge_in.astype(F32)).astype(BF16)
    edge_xs = dot(edge_low.reshape(batch * 8, width), full_in_x).astype(BF16)
    edge_xs = edge_xs.reshape(batch, 8, chans)

    big = (per, tok, chans)
    f32_blk = lambda *s: pltpu.VMEM(s, F32)
    wide = states * LANE
    tmp_blk = pltpu.VMEM((chans // LANE, tok, LANE), F32)

    state = {"last": None}

    def tie(value):
        if state["last"] is None:
            return value
        return lax.optimization_barrier((value, state["last"]))[0]

    def mark(value):
        state["last"] = value

    low1, xs, z, edges, u, proj = {}, {}, {}, {}, {}, {}
    delta, normed, sn, einc, csd, enter, ctl, own = {}, {}, {}, {}, {}, {}, {}, {}
    live_sums = {}

    def scattered(grad):
        return lax.psum_scatter(grad, "seq", scatter_dimension=0, tiled=True).astype(F32)

    ch_place = lax.axis_index("ch")
    at_end = jnp.logical_or(ch_place == 0, ch_place == lax.axis_size("ch") - 1)
    at_end = at_end.astype(jnp.int32).reshape(1)
    smem = pl.BlockSpec(memory_space=pltpu.SMEM)
    whole = lambda *shape: (batch,) + shape
    acc = lambda rows_, width_: jnp.zeros((rows_, width_), F32)
    buf = dict.fromkeys(
        ("inner", "gated", "mid", "low2", "hidden", "gffn", "gm", "gml", "gin", "gz", "sinc", "pay",
         "gpre", "gu1", "gnorm", "gproj", "gxs", "head", "low_xs", "block", "grad_in")
    )
    buf.update(gskip=acc(8, chans), gain2=acc(8, width), gdec=acc(states, chans),
               gbias=acc(8, chans), ggain=acc(8, cols), gcw=acc(8 * (taps + 1), chans),
               gain1=acc(8, width))

    def at_block(b, *shape):
        return slot(*shape, at=b)

    def run(body, b, specs, args, outs, scratch=(), count=1, carry=()):
        specs, args = list(specs), list(args)
        shapes, into, carried = [], {}, {}
        for i, (name, block, kind) in enumerate(outs):
            if name in buf:
                shapes.append((at_block(b, *block), kind, whole(*block)))
                into[i] = buf[name]
            else:
                shapes.append((same(*block), kind, block))
        for name in carry:
            shape = buf[name].shape
            carried[len(shapes)] = len(args)
            specs.append(same(*shape))
            args.append(buf[name])
            shapes.append((same(*shape), F32, shape))
        out = call(body, count, specs, shapes, list(scratch), args, into, carried)
        names = [name for name, block, kind in outs] + list(carry)
        for name, value in zip(names, out):
            buf[name] = value
        return dict(zip(names, out))

    def stage_a(g):
        x = tie(inputs).astype(F32).reshape(rows, width)
        low1[g] = unit(x).astype(BF16)
        xs[g] = dot(low1[g], full_in_x).astype(BF16).reshape(big)
        edges[g] = edge_xs
        u[g], proj_part = call(
            pre_kernel, per,
            [part(tok, chans), part(8, chans), same(taps, chans), same(1, chans), same(chans, cols)],
            [(part(tok, chans), BF16, big), (part(tok, cols), BF16, whole(tok, cols))],
            [f32_blk(tok + 8, chans), tmp_blk, f32_blk(tok, chans)],
            (xs[g], edges[g], conv_w, cb_row, w_xproj),
        )
        mark(proj_part)
        live_sums["p", g] = Sum(proj_part.reshape(rows, cols), "ch")

    def stage_z(g):
        z[g] = dot(tie(low1[g]), full_in_z).astype(BF16).reshape(big)
        mark(z[g])

    def stage_s(g):
        proj[g] = live_sums["p", g].result().astype(F32).reshape(per, tok, cols)
        out = call(
            functools.partial(state_kernel, rank=rank, states=states), per,
            [smem, part(tok, cols), part(tok, chans),
             same(cols, chans), same(1, chans), same(1, cols), same(8 * states, chans),
             same(2 * cols, wide)],
            [(part(tok, chans), F32, big), (part(tok, cols), F32, whole(tok, cols)),
             (part(tok, cols), BF16, whole(tok, cols)),
             (part(8 * states, chans), F32, whole(8 * states, chans)),
             (part(8, chans), F32, whole(8, chans)),
             (part(states + 8, chans), F32, whole(states + 8, chans))],
            [f32_blk(tok, wide), f32_blk(tok, chans)],
            (counts, proj[g], tie(u[g]), wdt, bias_row, gains, dec8, spread[:, :wide]),
        )
        delta[g], normed[g], sn[g], einc[g], csd[g] = out[:5]
        mark(out[5])
        live_sums["e", g] = Entering(out[5], decay2, states, 1)

    def stage_h(g):
        ctl[0] = jnp.where(live, tie(cotangent), 0)
        mark(ctl[0])

    def stage_o(b):
        if 0 not in enter:
            enter[0] = live_sums["e", 0].result()
        out = run(
            functools.partial(out_kernel, states=states), b,
            [at_block(b, tok, chans), at_block(b, tok, chans), at_block(b, tok, cols),
             same(8 * states, chans), at_block(b, 8 * states, chans), at_block(b, 8, chans),
             at_block(b, states, chans), at_block(b, tok, chans), same(1, chans),
             same(2 * cols, 2 * wide), same(width, chans)],
            (delta[0], u[0], normed[0], dec8, einc[0], csd[0], enter[0], tie(z[0]), skip_row, spread,
             full_out),
            [("inner", (tok, chans), F32), ("gated", (tok, chans), BF16), ("branch", (tok, width), BF16)],
            [f32_blk(tok, 2 * wide), f32_blk(tok, chans), f32_blk(tok, chans), tmp_blk],
        )
        del buf["branch"]
        mark(out["branch"])
        live_sums["o", b] = Sum(out["branch"], "ch")

    def stage_f(b):
        kept, coming = live_sums["o", b].pair()
        deep = lambda *shape: pl.BlockSpec((1,) + shape, lambda i: (b, 0, i))
        outs = [
            (at_block(b, tok, width), F32, whole(tok, width)),
            (at_block(b, tok, width), BF16, whole(tok, width)),
            (deep(tok, tile), BF16, whole(tok, units)),
            (deep(tok, 2 * tile), BF16, whole(tok, 2 * units)),
            (same(tok, width), BF16, (tok, width)),
            (same(tok, width, at=b % 2), BF16, (2 * tok, width)),
        ]
        names = ["mid", "low2", "hidden", "gffn"]
        into = {i: buf[name] for i, name in enumerate(names)}
        if b % 2:
            into[5] = live_sums["down", b // 2]
        out = call(
            ffn_kernel, units // tile,
            [smem, at_block(b, tok, width), same(tok, width), same(tok, width),
             at_block(b, tok, width),
             pl.BlockSpec((width, 2 * tile), lambda i: (0, i)),
             pl.BlockSpec((width, tile), lambda i: (0, i))],
            outs, [f32_blk(tok, width), f32_blk(tok, width)],
            (at_end, tie(inputs), kept, coming, ctl[0], full_ffn, full_down),
            into,
        )
        for name, value in zip(names, out):
            buf[name] = value
        mark(out[4])
        live_sums["f", b] = Sum(out[4], "ch")
        live_sums["down", b // 2] = out[5]

    def stage_d(pair):
        live_sums["d", pair] = Sum(tie(live_sums["down", pair]), "ch")

    def row_part(b):
        return pl.BlockSpec((1, tok // 2, width), lambda i: (b, i, 0))

    def stage_q(b):
        kept, coming = live_sums["d", b // 2].pair()
        moved = pl.BlockSpec((tok // 2, width), lambda i: (2 * (b % 2) + i, 0))
        (buf["block"],) = call(
            add_kernel, 2, [smem, row_part(b), moved, moved],
            [(row_part(b), F32, whole(tok, width))], [],
            (at_end, tie(buf["mid"]), kept, coming), {0: buf["block"]},
        )
        mark(buf["block"])

    def flat(value):
        return value.reshape(-1, value.shape[-1])

    def stage_w(name):
        left, right = dict(
            down=lambda: (ctl[0], buf["hidden"]), ffn=lambda: (buf["low2"], buf["gffn"]),
            out=lambda: (buf["gml"], buf["gated"]), in_z=lambda: (low1[0], buf["gz"]),
            in_x=lambda: (low1[0], buf["low_xs"]),
        )[name]()
        left, right = flat(left), flat(right)
        deep, cut, wide_ = left.shape[0], width // WEIGHT_STEPS, right.shape[1]
        (grad,) = call(
            weight_kernel, WEIGHT_STEPS,
            [pl.BlockSpec((deep, cut), lambda i: (0, i)), same(deep, wide_)],
            [(pl.BlockSpec((cut, wide_), lambda i: (i, 0)), BF16, (width, wide_))], [],
            (left, tie(right)),
        )
        mark(grad)
        own[name] = grad

    def stage_t(name):
        grad = tie(own[name])
        mark(grad)
        own[name] = scattered(grad)

    def stage_r(name):
        own[name] = tie(own[name])
        mark(own[name])

    def stage_b(b):
        kept, coming = live_sums["f", b].pair()
        out = run(
            functools.partial(back_state_kernel, states=states), b,
            [smem, at_block(b, tok, width), same(tok, width), same(tok, width),
             at_block(b, tok, width), same(width, chans)]
            + [at_block(b, tok, chans)] * 4
            + [at_block(b, tok, cols), same(8 * states, chans), same(1, chans), same(2 * cols, wide)],
            (at_end, buf["mid"], kept, coming, ctl[0], full_out, z[0], buf["inner"], delta[0],
             tie(u[0]), normed[0], dec8, skip_row, spread[:, wide:]),
            [("gm", (tok, width), F32), ("gml", (tok, width), BF16), ("gin", (tok, chans), F32),
             ("gz", (tok, chans), BF16), ("sinc", (8 * states, chans), F32),
             ("pay", (states + 8, chans), F32)],
            [f32_blk(tok, wide), tmp_blk],
            carry=("gskip", "gain2"),
        )
        mark(out["pay"])
        if b == batch - 1:
            live_sums["l", 0] = Entering(out["pay"], decay2, states, -1)

    def stage_m(b):
        if b == 0:
            live_sums["leave"] = live_sums["l", 0].result()
        out = run(
            functools.partial(back_kernel, states=states), b,
            [at_block(b, tok, chans), at_block(b, tok, chans), at_block(b, tok, cols),
             same(8 * states, chans), at_block(b, 8 * states, chans), at_block(b, 8, chans),
             at_block(b, states, chans), at_block(b, tok, chans), at_block(b, 8 * states, chans),
             at_block(b, states, chans), same(1, chans),
             same(2 * cols, 2 * wide), same(2 * wide, cols), same(cols, chans)],
            (delta[0], tie(u[0]), normed[0], dec8, einc[0], csd[0], enter[0], buf["gin"],
             buf["sinc"], live_sums["leave"], skip_row, spread, gathering, wdt),
            [("gpre", (tok, chans), BF16), ("gu1", (tok, chans), F32), ("gnorm", (tok, cols), BF16)],
            [f32_blk(tok, 2 * wide), f32_blk(tok, 2 * wide), f32_blk(tok, chans),
             f32_blk(tok, STATE_BLOCK * chans), f32_blk(tok, STATE_BLOCK * chans), f32_blk(tok, chans)]
            + [f32_blk(8 * states, chans)] * 3,
            carry=("gdec", "gbias"),
        )
        mark(out["gnorm"])
        if b % 2 == 1:
            live_sums["m", b // 2] = Sum(out["gnorm"][b - 1 : b + 1].reshape(2 * tok, cols), "ch")

    def stage_c(pair):
        kept, coming = live_sums["m", pair].pair()
        kept, coming = kept.reshape(2, tok, cols), coming.reshape(2, tok, cols)
        for b in (2 * pair, 2 * pair + 1):
            out = run(
                functools.partial(conv_back_kernel, rank=rank, states=states), b,
                [smem, at_block(b % 2, tok, cols), at_block(b % 2, tok, cols),
                 at_block(b, tok, cols), same(1, cols), at_block(b, tok, chans),
                 same(chans, cols), at_block(b, tok, chans), at_block(b, 8, chans),
                 same(taps, chans), same(1, chans)],
                (at_end, kept, coming, proj[0], gains, buf["gu1"], w_xproj, tie(xs[0]), edges[0],
                 conv_w, cb_row),
                [("gproj", (tok, cols), BF16), ("gxs", (tok, chans), F32), ("head", (8, chans), F32)],
                [f32_blk(tok + 8, chans), tmp_blk, f32_blk(tok, chans)],
                carry=("ggain", "gcw"),
            )
            mark(out["head"])
        live_sums["fix", pair] = shifted(out["head"][2 * pair : 2 * pair + 2], -1)

    def stage_x(b):
        out = run(
            functools.partial(in_grad_kernel, taps=taps), b,
            [at_block(b, tok, chans), at_block(b % 2, 8, chans), same(taps, chans),
             at_block(b, tok, chans), same(width, chans), same(width, chans),
             at_block(b, tok, width)],
            (buf["gxs"], live_sums["fix", b // 2], conv_w, buf["gz"], full_in_x, full_in_z,
             tie(inputs)),
            [("low_xs", (tok, chans), BF16), ("gn1", (tok, width), BF16)],
            carry=("gain1",),
        )
        del buf["gn1"]
        mark(out["gn1"])
        live_sums["x", b] = Sum(out["gn1"], "ch")

    def stage_e(b):
        kept, coming = live_sums["x", b].pair()
        moved = pl.BlockSpec((tok // 2, width), lambda i: (i, 0))
        (buf["grad_in"],) = call(
            end_kernel, 2, [smem, row_part(b), moved, moved, row_part(b)],
            [(row_part(b), F32, whole(tok, width))], [],
            (at_end, tie(inputs), kept, coming, buf["gm"]), {0: buf["grad_in"]},
        )
        mark(buf["grad_in"])

    def stage_g(name):
        total = jnp.sum(tie(buf["gain1"]), axis=0).reshape(8, width // 8)
        total = lax.psum(total, "ch")
        mark(total)
        live_sums["g"] = total

    def stage_n(name):
        gxproj = dot_tn(flat(buf["gproj"]), tie(flat(u[0])))
        gwdt = dot_tn(flat(sn[0]), flat(buf["gpre"]))[:rank]
        one = lambda v: jnp.sum(v, axis=0, keepdims=True)
        narrow = [live_sums["g"].reshape(width), one(buf["gain2"])[0], one(buf["ggain"])[0]]
        narrow = jnp.concatenate(narrow)
        narrow = jnp.pad(narrow, (0, -narrow.shape[0] % chans)).reshape(-1, chans)
        gcw = jnp.sum(buf["gcw"].reshape(taps + 1, 8, chans), axis=1)
        rows_of = [gxproj, gwdt, buf["gdec"] * decay, gcw, one(buf["gbias"]), one(buf["gskip"]), narrow]
        stacked = jnp.concatenate(rows_of, axis=0).astype(BF16)
        mark(stacked)
        live_sums["n", 0] = Cube(stacked, "seq")
        own["marks"] = [r.shape[0] for r in rows_of]

    stages = dict(
        A=stage_a, Z=stage_z, S=stage_s, O=stage_o, H=stage_h, F=stage_f, D=stage_d, W=stage_w,
        B=stage_b, M=stage_m, C=stage_c, X=stage_x, E=stage_e, Q=stage_q, R=stage_r, N=stage_n, G=stage_g, T=stage_t,
    )
    for step in ORDER:
        rest = step[1:]
        rest = int(rest) if rest.isdigit() else rest
        if step[0].islower():
            live_sums[step[0], rest].advance(tie, mark)
        else:
            stages[step[0]](rest)

    split_ffn = own["ffn"].reshape(own_rows, units // tile, 2, tile)
    own["stacked"] = live_sums["n", 0].result().astype(F32)
    marks = [0]
    for count in own["marks"]:
        marks.append(marks[-1] + count)
    cut = [own["stacked"][a:b] for a, b in zip(marks[:-1], marks[1:])]
    narrow = cut[6].reshape(-1)
    local = norm1_gain.shape[0]
    at = lax.axis_index("seq") * local
    own_one = lax.dynamic_slice(narrow, (at,), (local,)) / gain_one[:, 0]
    own_two = lax.dynamic_slice(narrow, (width + at,), (local,)) / gain_two[:, 0]
    ggain = narrow[2 * width : 2 * width + cols]
    return (
        buf["block"],
        buf["grad_in"],
        own_one,
        own["in_x"] * gain_one,
        own["in_z"] * gain_one,
        cut[3][:taps],
        cut[3][taps],
        cut[0].T,
        ggain[:rank],
        ggain[rank : rank + states],
        ggain[rank + states :],
        cut[1],
        cut[4][0],
        cut[2],
        cut[5][0],
        own["out"].T,
        own_two,
        split_ffn[:, :, 0].reshape(own_rows, units) * gain_two,
        split_ffn[:, :, 1].reshape(own_rows, units) * gain_two,
        own["down"].T,
    )


def solution(mesh):
    return jax.shard_map(
        on_device,
        mesh=mesh,
        in_specs=(
            P(None, "seq", None),
            P(),
            P("seq"),
            P("seq", "ch"),
            P("seq", "ch"),
            P(None, "ch"),
            P("ch"),
            P("ch", None),
            P(),
            P(),
            P(),
            P(None, "ch"),
            P("ch"),
            P(None, "ch"),
            P("ch"),
            P("ch", "seq"),
            P("seq"),
            P("seq", "ch"),
            P("seq", "ch"),
            P("ch", "seq"),
            P(None, "seq", None),
        ),
        out_specs=(
            P(None, "seq", None),
            P(None, "seq", None),
            P("seq"),
            P("seq", "ch"),
            P("seq", "ch"),
            P(None, "ch"),
            P("ch"),
            P("ch", None),
            P(),
            P(),
            P(),
            P(None, "ch"),
            P("ch"),
            P(None, "ch"),
            P("ch"),
            P("ch", "seq"),
            P("seq"),
            P("seq", "ch"),
            P("seq", "ch"),
            P("ch", "seq"),
        ),
        check_vma=False,
    )
```

```python
import functools

import jax
import jax.numpy as jnp
from jax import lax
from jax.experimental import pallas as pl
from jax.experimental.pallas import tpu as pltpu
from jax.sharding import PartitionSpec as P

EPS = 1e-05
LOG2E = 1.4426950408889634
LANE = 128
CHUNKS = 8
UNROLL = 8
FORWARD_UNROLL = 4
BACK_UNROLL = 4
STATE_BLOCK = 2
WEIGHT_STEPS = 3
GROUPS = 1
ORDER = (
    "A0", "p0", "H0", "p0", "S0", "Z0", "e0", "O0", "O1", "O2", "o0", "O3", "o1", "o0", "o2", "o1",
    "F0", "o3", "o2", "F1", "f0", "o3", "F2", "f1", "f0", "F3", "Wdown", "Tdown", "f2", "f1", "B0",
    "f3", "f2", "D0", "B1", "f3", "B2", "d0", "B3", "D1", "Wffn", "l0", "Wout", "Win_z", "M0",
    "d0", "d1", "Tffn", "Tout", "Tin_z", "M1", "M2", "m0", "M3", "Q0", "Q1", "m0", "Rdown", "C0",
    "m1", "X0", "m1", "C1", "d1", "X1", "x0", "X2", "x1", "x0", "X3", "x2", "x1", "Q2", "Q3", "G0",
    "E0", "Win_x", "Tin_x", "N0", "x3", "x2", "Rffn", "E1", "n0", "x3", "n0", "E2", "Rout",
    "Rin_z", "E3",
)
F32 = jnp.float32
BF16 = jnp.bfloat16
VMEM_LIMIT = 48 * 1024 * 1024


def tree_sum(parts):
    parts = list(parts)
    while len(parts) > 1:
        parts = [
            parts[i] + parts[i + 1] if i + 1 < len(parts) else parts[i]
            for i in range(0, len(parts), 2)
        ]
    return parts[0]


def dot(left, right):
    return jnp.dot(left, right, preferred_element_type=F32)


def dot_nt(left, right):
    return lax.dot_general(left, right, (((1,), (1,)), ((), ())), preferred_element_type=F32)


def dot_tn(left, right):
    return lax.dot_general(left, right, (((0,), (0,)), ((), ())), preferred_element_type=F32)


def sigmoid(value):
    return 1.0 / (1.0 + jnp.exp(-value))


def split_low(value):
    high = value.astype(BF16)
    rest = (value - high.astype(F32)).astype(BF16)
    return jnp.concatenate([high, rest], axis=1)


def segment_rows(value, rank, states):
    lane = lax.broadcasted_iota(jnp.int32, value.shape, 1)
    first = lane < rank
    last = lane >= rank + states
    middle = jnp.logical_not(jnp.logical_or(first, last))
    means = []
    for mask, count in ((first, rank), (middle, states), (last, states)):
        means.append(jnp.sum(jnp.where(mask, value, 0.0), axis=1, keepdims=True) / count)
    return jnp.where(first, means[0], jnp.where(last, means[2], means[1]))


def load_padded(pad_ref, edge_ref, xs_ref, tok):
    pad_ref[0:8, :] = edge_ref[0].astype(F32)
    pad_ref[8 : 8 + tok, :] = xs_ref[0].astype(F32)


def conv_of(pad_ref, conv_w, conv_b, tok, taps):
    out = conv_b
    for k in range(taps):
        start = 8 - (taps - 1) + k
        out = out + conv_w[k : k + 1, :] * pad_ref[start : start + tok, :]
    return out


def picked(end_ref, kept_ref, coming_ref):
    kept, coming = kept_ref[...], coming_ref[...]
    return jnp.where(end_ref[0] == 1, coming, kept).astype(F32)


def partial_rows(value):
    return jnp.sum(value.reshape(value.shape[0] // 8, 8, value.shape[1]), axis=0)


def to_scan_order(value, tmp_ref, dst_ref):
    tok, chans = value.shape
    steps = tok // CHUNKS
    for j in range(chans // LANE):
        tmp_ref[j] = value[:, col(j)]
        for t in range(steps):
            dst_ref[8 * t : 8 * t + 8, col(j)] = tmp_ref[j, pl.ds(t, 8, stride=steps), :]


def to_natural_order(value, tmp_ref, dst_ref):
    tok, chans = value.shape
    steps = tok // CHUNKS
    for j in range(chans // LANE):
        tmp_ref[j] = value[:, col(j)]
        for k in range(CHUNKS):
            for t in range(0, steps, 8):
                dst_ref[k * steps + t : k * steps + t + 8, col(j)] = tmp_ref[
                    j, pl.ds(8 * t + k, 8, stride=8), :
                ]


def pre_kernel(xs_ref, edge_ref, cw_ref, cb_ref, wxp_ref, u_ref, proj_ref, pad, nat, per):
    tok, taps = xs_ref.shape[1], cw_ref.shape[0]
    load_padded(pad, edge_ref, xs_ref, tok)
    conv = conv_of(pad, cw_ref[...], cb_ref[...], tok, taps)
    to_scan_order(conv * sigmoid(conv), nat, per)
    u_low = per[...].astype(BF16)
    u_ref[0] = u_low
    proj_ref[0] = dot(u_low, wxp_ref[...]).astype(BF16)


def lanes_at(j):
    return pl.ds(pl.multiple_of(j * LANE, LANE), LANE)


def rows_at(t):
    return pl.ds(pl.multiple_of(t * 8, 8), 8)


def col(n):
    return slice(n * LANE, (n + 1) * LANE)


def chunk_prefix(prod, value, backwards):
    place = lax.broadcasted_iota(jnp.int32, value.shape, 0)
    for step in (1, 2, 4):
        shift = CHUNKS - step if backwards else step
        keep = place < CHUNKS - step if backwards else place >= step
        prod_far = jnp.where(keep, pltpu.roll(prod, shift, 0), 1.0)
        value_far = jnp.where(keep, pltpu.roll(value, shift, 0), 0.0)
        value = prod * value_far + value
        prod = prod * prod_far
    return value


def sum_prefix(value):
    place = lax.broadcasted_iota(jnp.int32, value.shape, 0)
    for step in (1, 2, 4):
        value = value + jnp.where(place >= step, pltpu.roll(value, step, 0), 0.0)
    return value


def state_kernel(
    cnt_ref, proj_ref, u_ref, wdt_ref, bias_ref, gain_ref, dec_ref, eb_ref,
    delta_ref, normed_ref, sn_ref, einc_ref, csd_ref, pay_ref, bb, du,
    *, rank, states,
):
    tok, chans = u_ref.shape[1], u_ref.shape[2]
    steps = tok // CHUNKS
    value = proj_ref[0]
    scale = lax.rsqrt(segment_rows(value * value, rank, states) + EPS)
    normed = value * scale * gain_ref[...]
    normed_ref[0] = normed
    lane = lax.broadcasted_iota(jnp.int32, value.shape, 1)
    step_low = jnp.where(lane < rank, normed, 0.0).astype(BF16)
    sn_ref[0] = step_low
    pre = dot(step_low, wdt_ref[...]) + bias_ref[...]
    row = lax.broadcasted_iota(jnp.int32, pre.shape, 0)
    place = (row & 7) * steps + (row >> 3)
    live = place < cnt_ref[pl.program_id(0)]
    soft = jnp.maximum(pre, 0.0) + jnp.log(1.0 + jnp.exp(-jnp.abs(pre)))
    delta = jnp.where(live, soft, 0.0)
    delta_ref[0] = delta
    du[...] = delta * u_ref[0].astype(F32)
    bb[...] = dot(split_low(normed), eb_ref[...])

    def tile(j, carry):
        lanes = lanes_at(j)
        dec = [dec_ref[8 * n : 8 * n + 8, lanes] for n in range(states)]

        def step(i, carry):
            ends, total = carry
            for q in range(UNROLL):
                rows = rows_at(i * UNROLL + q)
                d = delta_ref[0, rows, lanes]
                v = du[rows, lanes]
                ends = tuple(
                    jnp.exp2(d * dec[n]) * ends[n] + v * bb[rows, col(n)] for n in range(states)
                )
                total = total + d
            return ends, total

        zero = jnp.zeros((8, LANE), F32)
        ends, total = lax.fori_loop(0, steps // UNROLL, step, ((zero,) * states, zero))
        csd = sum_prefix(total)
        csd_ref[0, :, lanes] = csd
        for n in range(states):
            inc = chunk_prefix(jnp.exp2(dec[n] * total), ends[n], False)
            einc_ref[0, 8 * n : 8 * n + 8, lanes] = inc
            pay_ref[0, n : n + 1, lanes] = inc[7:8, :]
        pay_ref[0, states : states + 8, lanes] = jnp.broadcast_to(csd[7:8, :], (8, LANE))
        return carry

    lax.fori_loop(0, chans // LANE, tile, 0)


def start_states(dec, csd, einc_ref, enter_ref, lanes, states):
    place = lax.broadcasted_iota(jnp.int32, csd.shape, 0)
    before = jnp.where(place >= 1, pltpu.roll(csd, 1, 0), 0.0)
    out = []
    for n in range(states):
        own = jnp.where(place >= 1, pltpu.roll(einc_ref[0, 8 * n : 8 * n + 8, lanes], 1, 0), 0.0)
        out.append(own + jnp.exp2(dec[n] * before) * enter_ref[0, n : n + 1, lanes])
    return tuple(out)


def out_kernel(
    delta_ref, u_ref, normed_ref, dec_ref, einc_ref, csd_ref, enter_ref, z_ref, skip_ref, eb_ref,
    wout_ref, inner_ref, gated_ref, branch_ref, bc, du, per, tmp, *, states,
):
    tok, chans = u_ref.shape[1], u_ref.shape[2]
    steps = tok // CHUNKS
    bc[...] = dot(split_low(normed_ref[0]), eb_ref[...])
    u_val = u_ref[0].astype(F32)
    du[...] = delta_ref[0] * u_val
    per[...] = skip_ref[...] * u_val

    def tile(j, carry):
        lanes = lanes_at(j)
        dec = [dec_ref[8 * n : 8 * n + 8, lanes] for n in range(states)]

        def step(i, hs):
            for q in range(UNROLL):
                rows = rows_at(i * UNROLL + q)
                d = delta_ref[0, rows, lanes]
                v = du[rows, lanes]
                hs = tuple(
                    jnp.exp2(d * dec[n]) * hs[n] + v * bc[rows, col(n)] for n in range(states)
                )
                per[rows, lanes] += tree_sum(
                    hs[n] * bc[rows, col(states + n)] for n in range(states)
                )
            return hs

        first = start_states(dec, csd_ref[0, :, lanes], einc_ref, enter_ref, lanes, states)
        lax.fori_loop(0, steps // UNROLL, step, first)
        return carry

    lax.fori_loop(0, chans // LANE, tile, 0)
    to_natural_order(per[...], tmp, du)
    inner = du[...]
    inner_ref[0] = inner
    z_val = z_ref[0].astype(F32)
    gated = (inner * z_val * sigmoid(z_val)).astype(BF16)
    gated_ref[0] = gated
    branch_ref[...] = dot_nt(gated, wout_ref[...]).astype(BF16)


def back_state_kernel(
    edge_ref, mid_ref, kept_ref, coming_ref, ctl_ref, wout_ref, z_ref, inner_ref, delta_ref, u_ref,
    normed_ref, dec_ref, skip_ref, ec_ref, gskip_in, gain_in,
    gm_ref, gml_ref, gin_ref, gz_ref, sinc_ref, pay_ref, gskip_ref, gain_ref, cb, nat, *, states,
):
    tok, chans = u_ref.shape[1], u_ref.shape[2]
    steps = tok // CHUNKS
    mid = mid_ref[0]
    grad = picked(edge_ref, kept_ref, coming_ref)
    scale = lax.rsqrt(jnp.mean(mid * mid, axis=-1, keepdims=True) + EPS)
    by_mid = mid * grad
    mean = jnp.mean(by_mid, axis=-1, keepdims=True)
    gain_ref[...] = gain_in[...] + partial_rows(by_mid * scale)
    gm = ctl_ref[0].astype(F32) + scale * grad - (scale * scale * scale * mean) * mid
    gm_ref[0] = gm
    gml_ref[0] = gm.astype(BF16)
    gg = dot(gml_ref[0], wout_ref[...])
    cb[...] = dot(split_low(normed_ref[0]), ec_ref[...])
    z_val = z_ref[0].astype(F32)
    sig = sigmoid(z_val)
    gin = gin_ref.at[0]
    to_scan_order(gg * z_val * sig, nat, gin)
    gz_ref[0] = (gg * inner_ref[0] * sig * (1.0 + z_val * (1.0 - sig))).astype(BF16)

    gskip_ref[...] = gskip_in[...] + partial_rows(gin[...] * u_ref[0].astype(F32))

    def tile(j, carry):
        lanes = lanes_at(j)
        dec = [dec_ref[8 * n : 8 * n + 8, lanes] for n in range(states)]

        def step(i, carry):
            flow, total = carry
            for q in range(UNROLL):
                rows = rows_at(steps - 1 - (i * UNROLL + q))
                d = delta_ref[0, rows, lanes]
                g = gin[rows, lanes]
                flow = tuple(
                    jnp.exp2(d * dec[n]) * (flow[n] + g * cb[rows, col(n)]) for n in range(states)
                )
                total = total + d
            return flow, total

        zero = jnp.zeros((8, LANE), F32)
        flow, total = lax.fori_loop(0, steps // UNROLL, step, ((zero,) * states, zero))
        for n in range(states):
            inc = chunk_prefix(jnp.exp2(dec[n] * total), flow[n], True)
            sinc_ref[0, 8 * n : 8 * n + 8, lanes] = inc
            pay_ref[0, n : n + 1, lanes] = inc[0:1, :]
        full = jnp.sum(total, axis=0, keepdims=True)
        pay_ref[0, states : states + 8, lanes] = jnp.broadcast_to(full, (8, LANE))
        return carry

    lax.fori_loop(0, chans // LANE, tile, 0)


def back_kernel(
    delta_ref, u_ref, normed_ref, dec_ref, einc_ref, csd_ref, enter_ref, gin_ref, sinc_ref,
    leave_ref, skip_ref, eb_ref, ebt_ref, wdt_ref, gdec_in, gbias_in,
    gpre_ref, gu_ref, gnorm_ref, gdec_ref, gbias_ref, bc, acc, du, fac, prev, gstep,
    enter8, leave8, logs8,
    *, states,
):
    tok, chans = u_ref.shape[1], u_ref.shape[2]
    steps, tiles = tok // CHUNKS, chans // LANE
    bc[...] = dot(split_low(normed_ref[0]), eb_ref[...])
    du[...] = delta_ref[0] * u_ref[0].astype(F32)
    gu_ref[0] = jnp.zeros((tok, chans), F32)
    gstep[...] = jnp.zeros((tok, chans), F32)
    for n in range(states):
        rows = slice(8 * n, 8 * n + 8)
        enter8[rows, :] = jnp.broadcast_to(enter_ref[0, n : n + 1, :], (8, chans))
        leave8[rows, :] = jnp.broadcast_to(leave_ref[0, n : n + 1, :], (8, chans))
    place = lax.broadcasted_iota(jnp.int32, (8, LANE), 0)
    pairs = [(q, j) for q in range(STATE_BLOCK) for j in range(tiles)]

    def block(i, carry):
        ns = [i * STATE_BLOCK + q for q in range(STATE_BLOCK)]
        rows_of = [rows_at(n) for n in ns]
        at_b = [lanes_at(n) for n in ns]
        at_c = [lanes_at(n + states) for n in ns]
        dec = {(q, j): dec_ref[rows_of[q], col(j)] for q, j in pairs}
        first, last = [], []
        for q, j in pairs:
            csd = csd_ref[0, :, col(j)]
            before = jnp.where(place >= 1, pltpu.roll(csd, 1, 0), 0.0)
            own = jnp.where(place >= 1, pltpu.roll(einc_ref[0, rows_of[q], col(j)], 1, 0), 0.0)
            first.append(own + jnp.exp2(dec[q, j] * before) * enter8[rows_of[q], col(j)])
            after = csd[7:8, :] - csd
            own = jnp.where(place < 7, pltpu.roll(sinc_ref[0, rows_of[q], col(j)], 7, 0), 0.0)
            last.append(own + jnp.exp2(dec[q, j] * after) * leave8[rows_of[q], col(j)])

        def forward(t, hs):
            for r in range(FORWARD_UNROLL):
                rows = rows_at(t * FORWARD_UNROLL + r)
                d = [delta_ref[0, rows, col(j)] for j in range(tiles)]
                v = [du[rows, col(j)] for j in range(tiles)]
                g = [gin_ref[0, rows, col(j)] for j in range(tiles)]
                b = [bc[rows, at] for at in at_b]
                new = []
                for k, (q, j) in enumerate(pairs):
                    a = jnp.exp2(d[j] * dec[q, j])
                    p = a * hs[k]
                    fac[rows, col(k)] = a
                    prev[rows, col(k)] = p
                    new.append(p + v[j] * b[q])
                hs = tuple(new)
                for q in range(STATE_BLOCK):
                    acc[rows, at_c[q]] = tree_sum(hs[q * tiles + j] * g[j] for j in range(tiles))
            return hs

        lax.fori_loop(0, steps // FORWARD_UNROLL, forward, tuple(first))

        def backward(t, carry):
            flow, logs = carry
            for r in range(BACK_UNROLL):
                rows = rows_at(steps - 1 - (t * BACK_UNROLL + r))
                d = [delta_ref[0, rows, col(j)] for j in range(tiles)]
                v = [du[rows, col(j)] for j in range(tiles)]
                g = [gin_ref[0, rows, col(j)] for j in range(tiles)]
                b = [bc[rows, at] for at in at_b]
                c = [bc[rows, at] for at in at_c]
                new_flow, new_logs, grads, scaled = [], [], [], []
                for k, (q, j) in enumerate(pairs):
                    grad = flow[k] + g[j] * c[q]
                    gp = grad * prev[rows, col(k)]
                    new_flow.append(fac[rows, col(k)] * grad)
                    new_logs.append(logs[k] + gp * d[j])
                    scaled.append(gp * dec[q, j])
                    grads.append(grad)
                flow, logs = tuple(new_flow), tuple(new_logs)
                for j in range(tiles):
                    gu_ref[0, rows, col(j)] += tree_sum(
                        grads[q * tiles + j] * b[q] for q in range(STATE_BLOCK)
                    )
                    gstep[rows, col(j)] += tree_sum(
                        scaled[q * tiles + j] for q in range(STATE_BLOCK)
                    )
                for q in range(STATE_BLOCK):
                    acc[rows, at_b[q]] = tree_sum(grads[q * tiles + j] * v[j] for j in range(tiles))
            return flow, logs

        zero = jnp.zeros((8, LANE), F32)
        unused, logs = lax.fori_loop(
            0, steps // BACK_UNROLL, backward, (tuple(last), (zero,) * len(pairs))
        )
        for k, (q, j) in enumerate(pairs):
            logs8[rows_of[q], col(j)] = logs[k]
        return carry

    lax.fori_loop(0, states // STATE_BLOCK, block, 0)
    for n in range(states):
        total = jnp.sum(logs8[8 * n : 8 * n + 8, :], axis=0, keepdims=True)
        gdec_ref[n : n + 1, :] = gdec_in[n : n + 1, :] + total
    delta = delta_ref[0]
    drive = gu_ref[0]
    gdelta = gstep[...] * (1.0 / LOG2E) + drive * u_ref[0].astype(F32)
    gu_ref[0] = drive * delta + skip_ref[...] * gin_ref[0]
    small = delta * (1.0 - delta * (0.5 - delta * (1.0 / 6.0)))
    slope = jnp.where(delta < 0.01, small, 1.0 - jnp.exp(-delta))
    gpre = (gdelta * slope).astype(BF16)
    gpre_ref[0] = gpre
    gbias_ref[...] = gbias_in[...] + partial_rows(gpre.astype(F32))
    gnorm = dot_nt(gpre, wdt_ref[...]) + dot(acc[...].astype(BF16), ebt_ref[...])
    gnorm_ref[0] = gnorm.astype(BF16)


def conv_back_kernel(
    end_ref, kept_ref, coming_ref, proj_ref, gain_ref, gu_ref, wxp_ref, xs_ref, edge_ref, cw_ref,
    cb_ref, ggain_in, gcw_in, gproj_ref, gxs_ref, head_ref, ggain_ref, gcw_ref, pad, per, nat,
    *, rank, states,
):
    tok, taps = xs_ref.shape[1], cw_ref.shape[0]
    grad = picked(end_ref, kept_ref, coming_ref)[0]
    value = proj_ref[0]
    scale = lax.rsqrt(segment_rows(value * value, rank, states) + EPS)
    by_gain = gain_ref[...] * grad
    mean = segment_rows(value * by_gain, rank, states)
    gproj = (scale * by_gain - scale * scale * scale * value * mean).astype(BF16)
    gproj_ref[0] = gproj
    ggain_ref[...] = ggain_in[...] + partial_rows(grad * value * scale)
    to_natural_order(gu_ref[0] + dot_nt(gproj, wxp_ref[...]), per, nat)
    load_padded(pad, edge_ref, xs_ref, tok)
    conv = conv_of(pad, cw_ref[...], cb_ref[...], tok, taps)
    sig = sigmoid(conv)
    gconv = nat[...] * sig * (1.0 + conv * (1.0 - sig))
    for k in range(taps):
        start = 8 - (taps - 1) + k
        gcw_ref[8 * k : 8 * k + 8, :] = gcw_in[8 * k : 8 * k + 8, :] + partial_rows(
            gconv * pad[start : start + tok, :]
        )
    gcw_ref[8 * taps :, :] = gcw_in[8 * taps :, :] + partial_rows(gconv)
    head_ref[0] = gconv[0:8, :]
    pad[0:tok, :] = gconv
    pad[tok : tok + 8, :] = jnp.zeros((8, gconv.shape[1]), F32)
    gxs = cw_ref[taps - 1 : taps, :] * gconv
    for k in range(taps - 1):
        ahead = taps - 1 - k
        gxs = gxs + cw_ref[k : k + 1, :] * pad[ahead : ahead + tok, :]
    gxs_ref[0] = gxs


def ffn_kernel(
    end_ref, x_ref, kept_ref, coming_ref, ctl_ref, w_ref, wd_ref,
    mid_ref, low_ref, hid_ref, gffn_ref, gn_ref, down_ref, gn_acc, down_acc,
):
    step = pl.program_id(0)

    @pl.when(step == 0)
    def _():
        mid = x_ref[0].astype(F32) + picked(end_ref, kept_ref, coming_ref)
        mid_ref[0] = mid
        scale = lax.rsqrt(jnp.mean(mid * mid, axis=-1, keepdims=True) + EPS)
        low_ref[0] = (mid * scale).astype(BF16)

    weight = w_ref[...]
    units = weight.shape[1] // 2
    both = dot(low_ref[0], weight)
    back = dot(ctl_ref[0], wd_ref[...])
    gate, up = both[:, :units], both[:, units:]
    sig = sigmoid(gate)
    act = gate * sig
    hid = (act * up).astype(BF16)
    hid_ref[0] = hid
    ggate = (back * up * (sig * (1.0 + gate - act))).astype(BF16)
    gffn = jnp.concatenate([ggate, (back * act).astype(BF16)], axis=1)
    gffn_ref[0] = gffn
    gn = dot_nt(gffn, weight)
    down = dot_nt(hid, wd_ref[...])

    @pl.when(step == 0)
    def _():
        gn_acc[...] = gn
        down_acc[...] = down

    @pl.when(step > 0)
    def _():
        gn_acc[...] += gn
        down_acc[...] += down

    @pl.when(step == pl.num_programs(0) - 1)
    def _():
        gn_ref[...] = gn_acc[...].astype(BF16)
        down_ref[...] = down_acc[...].astype(BF16)


def add_kernel(end_ref, mid_ref, kept_ref, coming_ref, out_ref):
    out_ref[0] = mid_ref[0] + picked(end_ref, kept_ref, coming_ref)


def in_grad_kernel(
    gxs_ref, ahead_ref, cw_ref, gz_ref, wx_ref, wz_ref, x_ref, gain_in,
    low_ref, gn_ref, gain_ref, *, taps,
):
    tok = gxs_ref.shape[1]
    row = lax.broadcasted_iota(jnp.int32, (8, gxs_ref.shape[2]), 0)
    ahead = ahead_ref[0]
    fix = jnp.zeros((8, gxs_ref.shape[2]), F32)
    for k in range(taps - 1):
        start = 8 - (taps - 1 - k)
        moved = pltpu.roll(ahead, start, 0)
        fix = fix + jnp.where(row >= start, cw_ref[k : k + 1, :] * moved, 0.0)
    main = gxs_ref[0]
    low = jnp.concatenate([main[: tok - 8], main[tok - 8 :] + fix], axis=0).astype(BF16)
    low_ref[0] = low
    gn = dot_nt(low, wx_ref[...]) + dot_nt(gz_ref[0], wz_ref[...])
    x = x_ref[0].astype(F32)
    scale = lax.rsqrt(jnp.mean(x * x, axis=-1, keepdims=True) + EPS)
    gain_ref[...] = gain_in[...] + partial_rows(gn * x * scale)
    gn_ref[...] = gn.astype(BF16)


def end_kernel(end_ref, x_ref, kept_ref, coming_ref, gm_ref, out_ref):
    x = x_ref[0].astype(F32)
    grad = picked(end_ref, kept_ref, coming_ref)
    scale = lax.rsqrt(jnp.mean(x * x, axis=-1, keepdims=True) + EPS)
    mean = jnp.mean(x * grad, axis=-1, keepdims=True)
    out_ref[0] = gm_ref[0] + scale * grad - (scale * scale * scale * mean) * x


def weight_kernel(left_ref, right_ref, out_ref):
    out_ref[...] = dot_tn(left_ref[...], right_ref[...]).astype(BF16)


def part(*shape, at=0):
    return pl.BlockSpec((1,) + shape, lambda i: (i + at,) + (0,) * len(shape))


def slot(*shape, at):
    return pl.BlockSpec((1,) + shape, lambda i: (at,) + (0,) * len(shape))


def same(*shape, at=0):
    return pl.BlockSpec(shape, lambda i: (at,) + (0,) * (len(shape) - 1))


def call(body, count, in_specs, outs, scratch, args, into=None, carry=None):
    into, carry = into or {}, carry or {}
    fixed = len(args)
    kept = sorted(k for k in into if into[k] is not None)
    args = tuple(args) + tuple(into[k] for k in kept)
    in_specs = list(in_specs) + [pl.BlockSpec(memory_space=pl.ANY)] * len(kept)
    aliases = {fixed + i: k for i, k in enumerate(kept)}
    aliases.update({arg: out for out, arg in carry.items()})

    def run(*refs):
        body(*refs[:fixed], *refs[fixed + len(kept) :])

    return pl.pallas_call(
        run,
        grid=(count,),
        in_specs=in_specs,
        out_specs=[spec for spec, kind, shape in outs],
        out_shape=[jax.ShapeDtypeStruct(shape, kind) for spec, kind, shape in outs],
        scratch_shapes=scratch,
        input_output_aliases=aliases,
        compiler_params=pltpu.CompilerParams(vmem_limit_bytes=VMEM_LIMIT),
        cost_estimate=pl.CostEstimate(flops=0, bytes_accessed=0, transcendentals=0),
    )(*args)


class Sum:
    def __init__(self, value, axis):
        self.axis, self.hops, self.kept = axis, 0, value
        if lax.axis_size(axis) != 4:
            self.hops, self.kept = 3, lax.psum(value, axis)
            return
        self.coming = lax.ppermute(value, axis, [(0, 1), (3, 2)])

    def advance(self, tie, mark):
        if self.hops >= 2:
            return
        self.kept = self.kept + tie(self.coming)
        mark(self.kept)
        route = [(1, 0), (2, 3)] if self.hops else [(1, 2), (2, 1)]
        self.coming = lax.ppermute(self.kept, self.axis, route)
        self.hops += 1

    def result(self):
        while self.hops < 2:
            self.advance(lambda v: v, lambda v: None)
        if self.hops == 2:
            place = lax.axis_index(self.axis)
            at_end = jnp.logical_or(place == 0, place == 3)
            self.kept, self.hops = jnp.where(at_end, self.coming, self.kept), 3
        return self.kept

    def pair(self):
        while self.hops < 2:
            self.advance(lambda v: v, lambda v: None)
        return (self.kept, self.coming if self.hops == 2 else self.kept)


def shifted(value, distance):
    size = lax.axis_size("seq")
    route = [(i, i + distance) for i in range(size) if 0 <= i + distance < size]
    return lax.ppermute(value, "seq", route)


class Cube:
    def __init__(self, value, axis):
        self.value, self.axis, self.size, self.bit = value, axis, lax.axis_size(axis), 1
        if self.size & (self.size - 1):
            self.value, self.bit = lax.psum(value, axis), self.size
        self.send()

    def send(self):
        if self.bit < self.size:
            route = [(i, i ^ self.bit) for i in range(self.size)]
            self.coming = lax.ppermute(self.value, self.axis, route)

    def advance(self, tie, mark):
        if self.bit < self.size:
            self.value = self.value + tie(self.coming)
            mark(self.value)
            self.bit *= 2
            self.send()

    def result(self):
        while self.bit < self.size:
            self.advance(lambda v: v, lambda v: None)
        return self.value


class Entering:
    def __init__(self, payload, decay, states, sign):
        self.decay, self.states, self.sign = decay, states, sign
        self.size = lax.axis_size("seq")
        self.reach = min(4, self.size - 1)
        packed = self.pack((payload[:, :states], payload[:, states : states + 1]))
        self.parts = [shifted(packed, sign * k) for k in range(1, self.reach + 1)]
        self.total = None

    def pack(self, pair):
        value, length = pair
        high = lax.optimization_barrier(length.astype(BF16))
        low = (length - high.astype(F32)).astype(BF16)
        return jnp.concatenate([value.astype(BF16), high, low], axis=1)

    def unpack(self, packed):
        whole = packed.astype(F32)
        value, high = whole[:, : self.states], whole[:, self.states : self.states + 1]
        return value, high + whole[:, self.states + 1 :]

    def join(self, far, near):
        return jnp.exp2(self.decay[None] * near[1]) * far[0] + near[0], far[1] + near[1]

    def advance(self, tie, mark):
        total = self.unpack(tie(self.parts[-1]))
        for near in self.parts[-2::-1]:
            total = self.join(total, self.unpack(near))
        self.total = total
        mark(total[0])
        if self.reach < self.size - 1:
            self.coming = shifted(self.pack(total), self.sign * self.reach)

    def result(self):
        if self.total is None:
            self.advance(lambda v: v, lambda v: None)
        while self.reach < self.size - 1:
            self.total = self.join(self.unpack(self.coming), self.total)
            self.reach *= 2
            if self.reach < self.size - 1:
                self.coming = shifted(self.pack(self.total), self.sign * self.reach)
        return self.total[0]


def on_device(
    inputs, lengths, norm1_gain, w_in_x, w_in_z, conv_w, conv_b, w_xproj, dt_gain, b_gain, c_gain,
    w_dt, dt_bias, decay_log, skip_d, w_out, norm2_gain, w_gate, w_up, w_down, cotangent,
):
    batch, tok, width = inputs.shape
    chans = conv_w.shape[1]
    taps = conv_w.shape[0]
    rank, states = dt_gain.shape[0], b_gain.shape[0]
    cols = w_xproj.shape[1]
    per = batch // GROUPS
    rows = per * tok
    groups = range(GROUPS)

    def gather(weight):
        return lax.all_gather(weight, "seq", axis=0, tiled=True)

    gain_one = norm1_gain.astype(F32)[:, None]
    gain_two = norm2_gain.astype(F32)[:, None]
    full_in_x = gather((w_in_x.astype(F32) * gain_one).astype(BF16))
    full_in_z = gather((w_in_z.astype(F32) * gain_one).astype(BF16))
    full_out = gather(w_out.T)
    full_down = gather(w_down.T)
    low_gate = (w_gate.astype(F32) * gain_two).astype(BF16)
    low_up = (w_up.astype(F32) * gain_two).astype(BF16)
    units = tile = w_gate.shape[1]
    full_ffn = gather(jnp.concatenate([low_gate, low_up], axis=1))

    first_place = lax.axis_index("seq") * tok
    counts = jnp.clip(lengths - first_place, 0, tok)
    live = (jnp.arange(tok, dtype=jnp.int32)[None, :] < counts[:, None])[:, :, None]
    decay = -jnp.exp(decay_log)
    decay2 = decay * LOG2E
    dec8 = jnp.repeat(decay2, 8, axis=0)
    k_of = lax.broadcasted_iota(jnp.int32, (2 * cols, 2 * states * LANE), 0) % cols
    c_of = lax.broadcasted_iota(jnp.int32, (2 * cols, 2 * states * LANE), 1) // LANE
    spread = (k_of == c_of + rank).astype(BF16)
    k_of = lax.broadcasted_iota(jnp.int32, (2 * states * LANE, cols), 1)
    c_of = lax.broadcasted_iota(jnp.int32, (2 * states * LANE, cols), 0) // LANE
    gathering = (k_of == c_of + rank).astype(BF16)
    gains = jnp.concatenate([dt_gain, b_gain, c_gain])[None]
    wdt = jnp.pad(w_dt, ((0, cols - rank), (0, 0)))
    cb_row, bias_row, skip_row = conv_b[None], dt_bias[None], skip_d[None]

    def unit(value):
        return value * lax.rsqrt(jnp.mean(value * value, axis=-1, keepdims=True) + EPS)

    edge_in = shifted(inputs[:, tok - 8 :, :], 1)
    edge_low = unit(edge_in.astype(F32)).astype(BF16)
    edge_xs = dot(edge_low.reshape(batch * 8, width), full_in_x).astype(BF16)
    edge_xs = edge_xs.reshape(batch, 8, chans)

    big = (per, tok, chans)
    f32_blk = lambda *s: pltpu.VMEM(s, F32)
    wide = states * LANE
    tmp_blk = pltpu.VMEM((chans // LANE, tok, LANE), F32)

    state = {"last": None}

    def tie(value):
        if state["last"] is None:
            return value
        return lax.optimization_barrier((value, state["last"]))[0]

    def mark(value):
        state["last"] = value

    low1, xs, z, edges, u, proj = {}, {}, {}, {}, {}, {}
    delta, normed, sn, einc, csd, enter, ctl, own = {}, {}, {}, {}, {}, {}, {}, {}
    live_sums = {}

    def scattered(grad):
        return lax.psum_scatter(grad, "seq", scatter_dimension=0, tiled=True)

    ch_place = lax.axis_index("ch")
    at_end = jnp.logical_or(ch_place == 0, ch_place == lax.axis_size("ch") - 1)
    at_end = at_end.astype(jnp.int32).reshape(1)
    smem = pl.BlockSpec(memory_space=pltpu.SMEM)
    whole = lambda *shape: (batch,) + shape
    acc = lambda rows_, width_: jnp.zeros((rows_, width_), F32)
    buf = dict.fromkeys(
        ("inner", "gated", "mid", "low2", "hidden", "gffn", "gm", "gml", "gin", "gz", "sinc", "pay",
         "gpre", "gu1", "gnorm", "gproj", "gxs", "head", "low_xs", "block", "grad_in")
    )
    buf.update(gskip=acc(8, chans), gain2=acc(8, width), gdec=acc(states, chans),
               gbias=acc(8, chans), ggain=acc(8, cols), gcw=acc(8 * (taps + 1), chans),
               gain1=acc(8, width))

    def at_block(b, *shape):
        return slot(*shape, at=b)

    def run(body, b, specs, args, outs, scratch=(), count=1, carry=()):
        specs, args = list(specs), list(args)
        shapes, into, carried = [], {}, {}
        for i, (name, block, kind) in enumerate(outs):
            if name in buf:
                shapes.append((at_block(b, *block), kind, whole(*block)))
                into[i] = buf[name]
            else:
                shapes.append((same(*block), kind, block))
        for name in carry:
            shape = buf[name].shape
            carried[len(shapes)] = len(args)
            specs.append(same(*shape))
            args.append(buf[name])
            shapes.append((same(*shape), F32, shape))
        out = call(body, count, specs, shapes, list(scratch), args, into, carried)
        names = [name for name, block, kind in outs] + list(carry)
        for name, value in zip(names, out):
            buf[name] = value
        return dict(zip(names, out))

    def stage_a(g):
        x = tie(inputs).astype(F32).reshape(rows, width)
        low1[g] = unit(x).astype(BF16)
        xs[g] = dot(low1[g], full_in_x).astype(BF16).reshape(big)
        edges[g] = edge_xs
        u[g], proj_part = call(
            pre_kernel, per,
            [part(tok, chans), part(8, chans), same(taps, chans), same(1, chans), same(chans, cols)],
            [(part(tok, chans), BF16, big), (part(tok, cols), BF16, whole(tok, cols))],
            [f32_blk(tok + 8, chans), tmp_blk, f32_blk(tok, chans)],
            (xs[g], edges[g], conv_w, cb_row, w_xproj),
        )
        mark(proj_part)
        live_sums["p", g] = Sum(proj_part.reshape(rows, cols), "ch")

    def stage_z(g):
        z[g] = dot(tie(low1[g]), full_in_z).astype(BF16).reshape(big)
        mark(z[g])

    def stage_s(g):
        proj[g] = live_sums["p", g].result().astype(F32).reshape(per, tok, cols)
        out = call(
            functools.partial(state_kernel, rank=rank, states=states), per,
            [smem, part(tok, cols), part(tok, chans),
             same(cols, chans), same(1, chans), same(1, cols), same(8 * states, chans),
             same(2 * cols, wide)],
            [(part(tok, chans), F32, big), (part(tok, cols), F32, whole(tok, cols)),
             (part(tok, cols), BF16, whole(tok, cols)),
             (part(8 * states, chans), F32, whole(8 * states, chans)),
             (part(8, chans), F32, whole(8, chans)),
             (part(states + 8, chans), F32, whole(states + 8, chans))],
            [f32_blk(tok, wide), f32_blk(tok, chans)],
            (counts, proj[g], tie(u[g]), wdt, bias_row, gains, dec8, spread[:, :wide]),
        )
        delta[g], normed[g], sn[g], einc[g], csd[g] = out[:5]
        mark(out[5])
        live_sums["e", g] = Entering(out[5], decay2, states, 1)

    def stage_h(g):
        ctl[0] = jnp.where(live, tie(cotangent), 0)
        mark(ctl[0])

    def stage_o(b):
        if 0 not in enter:
            enter[0] = live_sums["e", 0].result()
        out = run(
            functools.partial(out_kernel, states=states), b,
            [at_block(b, tok, chans), at_block(b, tok, chans), at_block(b, tok, cols),
             same(8 * states, chans), at_block(b, 8 * states, chans), at_block(b, 8, chans),
             at_block(b, states, chans), at_block(b, tok, chans), same(1, chans),
             same(2 * cols, 2 * wide), same(width, chans)],
            (delta[0], u[0], normed[0], dec8, einc[0], csd[0], enter[0], tie(z[0]), skip_row, spread,
             full_out),
            [("inner", (tok, chans), F32), ("gated", (tok, chans), BF16), ("branch", (tok, width), BF16)],
            [f32_blk(tok, 2 * wide), f32_blk(tok, chans), f32_blk(tok, chans), tmp_blk],
        )
        del buf["branch"]
        mark(out["branch"])
        live_sums["o", b] = Sum(out["branch"], "ch")

    def stage_f(b):
        kept, coming = live_sums["o", b].pair()
        deep = lambda *shape: pl.BlockSpec((1,) + shape, lambda i: (b, 0, i))
        outs = [
            (at_block(b, tok, width), F32, whole(tok, width)),
            (at_block(b, tok, width), BF16, whole(tok, width)),
            (deep(tok, tile), BF16, whole(tok, units)),
            (deep(tok, 2 * tile), BF16, whole(tok, 2 * units)),
            (same(tok, width), BF16, (tok, width)),
            (same(tok, width, at=b % 2), BF16, (2 * tok, width)),
        ]
        names = ["mid", "low2", "hidden", "gffn"]
        into = {i: buf[name] for i, name in enumerate(names)}
        if b % 2:
            into[5] = live_sums["down", b // 2]
        out = call(
            ffn_kernel, units // tile,
            [smem, at_block(b, tok, width), same(tok, width), same(tok, width),
             at_block(b, tok, width),
             pl.BlockSpec((width, 2 * tile), lambda i: (0, i)),
             pl.BlockSpec((width, tile), lambda i: (0, i))],
            outs, [f32_blk(tok, width), f32_blk(tok, width)],
            (at_end, tie(inputs), kept, coming, ctl[0], full_ffn, full_down),
            into,
        )
        for name, value in zip(names, out):
            buf[name] = value
        mark(out[4])
        live_sums["f", b] = Sum(out[4], "ch")
        live_sums["down", b // 2] = out[5]

    def stage_d(pair):
        live_sums["d", pair] = Sum(tie(live_sums["down", pair]), "ch")

    def row_part(b):
        return pl.BlockSpec((1, tok // 2, width), lambda i: (b, i, 0))

    def stage_q(b):
        kept, coming = live_sums["d", b // 2].pair()
        moved = pl.BlockSpec((tok // 2, width), lambda i: (2 * (b % 2) + i, 0))
        (buf["block"],) = call(
            add_kernel, 2, [smem, row_part(b), moved, moved],
            [(row_part(b), F32, whole(tok, width))], [],
            (at_end, tie(buf["mid"]), kept, coming), {0: buf["block"]},
        )
        mark(buf["block"])

    def flat(value):
        return value.reshape(-1, value.shape[-1])

    def stage_w(name):
        left, right = dict(
            down=lambda: (ctl[0], buf["hidden"]), ffn=lambda: (buf["low2"], buf["gffn"]),
            out=lambda: (buf["gml"], buf["gated"]), in_z=lambda: (low1[0], buf["gz"]),
            in_x=lambda: (low1[0], buf["low_xs"]),
        )[name]()
        left, right = flat(left), flat(right)
        deep, cut, wide_ = left.shape[0], width // WEIGHT_STEPS, right.shape[1]
        (grad,) = call(
            weight_kernel, WEIGHT_STEPS,
            [pl.BlockSpec((deep, cut), lambda i: (0, i)), same(deep, wide_)],
            [(pl.BlockSpec((cut, wide_), lambda i: (i, 0)), BF16, (width, wide_))], [],
            (left, tie(right)),
        )
        mark(grad)
        own[name] = grad

    def stage_t(name):
        grad = tie(own[name])
        mark(grad)
        own[name] = scattered(grad)

    def stage_r(name):
        own[name] = tie(own[name])
        mark(own[name])

    def stage_b(b):
        kept, coming = live_sums["f", b].pair()
        out = run(
            functools.partial(back_state_kernel, states=states), b,
            [smem, at_block(b, tok, width), same(tok, width), same(tok, width),
             at_block(b, tok, width), same(width, chans)]
            + [at_block(b, tok, chans)] * 4
            + [at_block(b, tok, cols), same(8 * states, chans), same(1, chans), same(2 * cols, wide)],
            (at_end, buf["mid"], kept, coming, ctl[0], full_out, z[0], buf["inner"], delta[0],
             tie(u[0]), normed[0], dec8, skip_row, spread[:, wide:]),
            [("gm", (tok, width), F32), ("gml", (tok, width), BF16), ("gin", (tok, chans), F32),
             ("gz", (tok, chans), BF16), ("sinc", (8 * states, chans), F32),
             ("pay", (states + 8, chans), F32)],
            [f32_blk(tok, wide), tmp_blk],
            carry=("gskip", "gain2"),
        )
        mark(out["pay"])
        if b == batch - 1:
            live_sums["l", 0] = Entering(out["pay"], decay2, states, -1)

    def stage_m(b):
        if b == 0:
            live_sums["leave"] = live_sums["l", 0].result()
        out = run(
            functools.partial(back_kernel, states=states), b,
            [at_block(b, tok, chans), at_block(b, tok, chans), at_block(b, tok, cols),
             same(8 * states, chans), at_block(b, 8 * states, chans), at_block(b, 8, chans),
             at_block(b, states, chans), at_block(b, tok, chans), at_block(b, 8 * states, chans),
             at_block(b, states, chans), same(1, chans),
             same(2 * cols, 2 * wide), same(2 * wide, cols), same(cols, chans)],
            (delta[0], tie(u[0]), normed[0], dec8, einc[0], csd[0], enter[0], buf["gin"],
             buf["sinc"], live_sums["leave"], skip_row, spread, gathering, wdt),
            [("gpre", (tok, chans), BF16), ("gu1", (tok, chans), F32), ("gnorm", (tok, cols), BF16)],
            [f32_blk(tok, 2 * wide), f32_blk(tok, 2 * wide), f32_blk(tok, chans),
             f32_blk(tok, STATE_BLOCK * chans), f32_blk(tok, STATE_BLOCK * chans), f32_blk(tok, chans)]
            + [f32_blk(8 * states, chans)] * 3,
            carry=("gdec", "gbias"),
        )
        mark(out["gnorm"])
        if b % 2 == 1:
            live_sums["m", b // 2] = Sum(out["gnorm"][b - 1 : b + 1].reshape(2 * tok, cols), "ch")

    def stage_c(pair):
        kept, coming = live_sums["m", pair].pair()
        kept, coming = kept.reshape(2, tok, cols), coming.reshape(2, tok, cols)
        for b in (2 * pair, 2 * pair + 1):
            out = run(
                functools.partial(conv_back_kernel, rank=rank, states=states), b,
                [smem, at_block(b % 2, tok, cols), at_block(b % 2, tok, cols),
                 at_block(b, tok, cols), same(1, cols), at_block(b, tok, chans),
                 same(chans, cols), at_block(b, tok, chans), at_block(b, 8, chans),
                 same(taps, chans), same(1, chans)],
                (at_end, kept, coming, proj[0], gains, buf["gu1"], w_xproj, tie(xs[0]), edges[0],
                 conv_w, cb_row),
                [("gproj", (tok, cols), BF16), ("gxs", (tok, chans), F32), ("head", (8, chans), F32)],
                [f32_blk(tok + 8, chans), tmp_blk, f32_blk(tok, chans)],
                carry=("ggain", "gcw"),
            )
            mark(out["head"])
        live_sums["fix", pair] = shifted(out["head"][2 * pair : 2 * pair + 2], -1)

    def stage_x(b):
        out = run(
            functools.partial(in_grad_kernel, taps=taps), b,
            [at_block(b, tok, chans), at_block(b % 2, 8, chans), same(taps, chans),
             at_block(b, tok, chans), same(width, chans), same(width, chans),
             at_block(b, tok, width)],
            (buf["gxs"], live_sums["fix", b // 2], conv_w, buf["gz"], full_in_x, full_in_z,
             tie(inputs)),
            [("low_xs", (tok, chans), BF16), ("gn1", (tok, width), BF16)],
            carry=("gain1",),
        )
        del buf["gn1"]
        mark(out["gn1"])
        live_sums["x", b] = Sum(out["gn1"], "ch")

    def stage_e(b):
        kept, coming = live_sums["x", b].pair()
        moved = pl.BlockSpec((tok // 2, width), lambda i: (i, 0))
        (buf["grad_in"],) = call(
            end_kernel, 2, [smem, row_part(b), moved, moved, row_part(b)],
            [(row_part(b), F32, whole(tok, width))], [],
            (at_end, tie(inputs), kept, coming, buf["gm"]), {0: buf["grad_in"]},
        )
        mark(buf["grad_in"])

    def stage_g(name):
        total = jnp.sum(tie(buf["gain1"]), axis=0).reshape(8, width // 8)
        total = lax.psum(total, "ch")
        mark(total)
        live_sums["g"] = total

    def stage_n(name):
        gxproj = dot_tn(flat(buf["gproj"]), tie(flat(u[0])))
        gwdt = dot_tn(flat(sn[0]), flat(buf["gpre"]))[:rank]
        one = lambda v: jnp.sum(v, axis=0, keepdims=True)
        narrow = [live_sums["g"].reshape(width), one(buf["gain2"])[0], one(buf["ggain"])[0]]
        narrow = jnp.concatenate(narrow)
        narrow = jnp.pad(narrow, (0, -narrow.shape[0] % chans)).reshape(-1, chans)
        gcw = jnp.sum(buf["gcw"].reshape(taps + 1, 8, chans), axis=1)
        rows_of = [gxproj, gwdt, buf["gdec"] * decay, gcw, one(buf["gbias"]), one(buf["gskip"]), narrow]
        stacked = jnp.concatenate(rows_of, axis=0).astype(BF16)
        mark(stacked)
        live_sums["n", 0] = Cube(stacked, "seq")
        own["marks"] = [r.shape[0] for r in rows_of]

    stages = dict(
        A=stage_a, Z=stage_z, S=stage_s, O=stage_o, H=stage_h, F=stage_f, D=stage_d, W=stage_w,
        B=stage_b, M=stage_m, C=stage_c, X=stage_x, E=stage_e, Q=stage_q, R=stage_r, N=stage_n, G=stage_g, T=stage_t,
    )
    for step in ORDER:
        rest = step[1:]
        rest = int(rest) if rest.isdigit() else rest
        if step[0].islower():
            live_sums[step[0], rest].advance(tie, mark)
        else:
            stages[step[0]](rest)

    own["stacked"] = live_sums["n", 0].result().astype(F32)
    marks = [0]
    for count in own["marks"]:
        marks.append(marks[-1] + count)
    cut = [own["stacked"][a:b] for a, b in zip(marks[:-1], marks[1:])]
    narrow = cut[6].reshape(-1)
    local = norm1_gain.shape[0]
    at = lax.axis_index("seq") * local
    own_one = lax.dynamic_slice(narrow, (at,), (local,)) / gain_one[:, 0]
    own_two = lax.dynamic_slice(narrow, (width + at,), (local,)) / gain_two[:, 0]
    ggain = narrow[2 * width : 2 * width + cols]
    return (
        buf["block"],
        buf["grad_in"],
        own_one,
        own["in_x"].astype(F32) * gain_one,
        own["in_z"].astype(F32) * gain_one,
        cut[3][:taps],
        cut[3][taps],
        cut[0].T,
        ggain[:rank],
        ggain[rank : rank + states],
        ggain[rank + states :],
        cut[1],
        cut[4][0],
        cut[2],
        cut[5][0],
        own["out"].astype(F32).T,
        own_two,
        own["ffn"][:, :units].astype(F32) * gain_two,
        own["ffn"][:, units:].astype(F32) * gain_two,
        own["down"].astype(F32).T,
    )


def solution(mesh):
    return jax.shard_map(
        on_device,
        mesh=mesh,
        in_specs=(
            P(None, "seq", None),
            P(),
            P("seq"),
            P("seq", "ch"),
            P("seq", "ch"),
            P(None, "ch"),
            P("ch"),
            P("ch", None),
            P(),
            P(),
            P(),
            P(None, "ch"),
            P("ch"),
            P(None, "ch"),
            P("ch"),
            P("ch", "seq"),
            P("seq"),
            P("seq", "ch"),
            P("seq", "ch"),
            P("ch", "seq"),
            P(None, "seq", None),
        ),
        out_specs=(
            P(None, "seq", None),
            P(None, "seq", None),
            P("seq"),
            P("seq", "ch"),
            P("seq", "ch"),
            P(None, "ch"),
            P("ch"),
            P("ch", None),
            P(),
            P(),
            P(),
            P(None, "ch"),
            P("ch"),
            P(None, "ch"),
            P("ch"),
            P("ch", "seq"),
            P("seq"),
            P("seq", "ch"),
            P("seq", "ch"),
            P("ch", "seq"),
        ),
        check_vma=False,
    )
```

```python
import functools

import jax
import jax.numpy as jnp
from jax import lax
from jax.experimental import pallas as pl
from jax.experimental.pallas import tpu as pltpu
from jax.sharding import PartitionSpec as P

EPS = 1e-05
LOG2E = 1.4426950408889634
LANE = 128
CHUNKS = 8
UNROLL = 8
FORWARD_UNROLL = 8
BACK_UNROLL = 4
STATE_BLOCK = 2
WEIGHT_STEPS = 3
GROUPS = 1
ORDER = (
    "A0", "p0", "H0", "p0", "S0", "Z0", "e0", "O0", "O1", "O2", "o0", "O3", "o1", "o0", "o2", "o1",
    "F0", "o3", "o2", "F1", "f0", "o3", "F2", "f1", "f0", "F3", "Wdown", "Tdown", "f2", "f1", "B0",
    "f3", "f2", "D0", "B1", "f3", "B2", "d0", "B3", "D1", "Wffn", "l0", "Wout", "Win_z", "M0",
    "d0", "d1", "Tffn", "Tout", "Tin_z", "M1", "M2", "m0", "M3", "Q0", "Q1", "m0", "Rdown", "C0",
    "m1", "X0", "m1", "C1", "d1", "X1", "x0", "X2", "x1", "x0", "X3", "x2", "x1", "Q2", "Q3", "G0",
    "E0", "Win_x", "Tin_x", "N0", "x3", "x2", "Rffn", "E1", "n0", "x3", "n0", "E2", "Rout",
    "Rin_z", "E3",
)
F32 = jnp.float32
BF16 = jnp.bfloat16
VMEM_LIMIT = 48 * 1024 * 1024


def tree_sum(parts):
    parts = list(parts)
    while len(parts) > 1:
        parts = [
            parts[i] + parts[i + 1] if i + 1 < len(parts) else parts[i]
            for i in range(0, len(parts), 2)
        ]
    return parts[0]


def dot(left, right):
    return jnp.dot(left, right, preferred_element_type=F32)


def dot_nt(left, right):
    return lax.dot_general(left, right, (((1,), (1,)), ((), ())), preferred_element_type=F32)


def dot_tn(left, right):
    return lax.dot_general(left, right, (((0,), (0,)), ((), ())), preferred_element_type=F32)


def sigmoid(value):
    return 1.0 / (1.0 + jnp.exp(-value))


def split_low(value):
    high = value.astype(BF16)
    rest = (value - high.astype(F32)).astype(BF16)
    return jnp.concatenate([high, rest], axis=1)


def segment_rows(value, rank, states):
    lane = lax.broadcasted_iota(jnp.int32, value.shape, 1)
    first = lane < rank
    last = lane >= rank + states
    middle = jnp.logical_not(jnp.logical_or(first, last))
    means = []
    for mask, count in ((first, rank), (middle, states), (last, states)):
        means.append(jnp.sum(jnp.where(mask, value, 0.0), axis=1, keepdims=True) / count)
    return jnp.where(first, means[0], jnp.where(last, means[2], means[1]))


def load_padded(pad_ref, edge_ref, xs_ref, tok):
    pad_ref[0:8, :] = edge_ref[0].astype(F32)
    pad_ref[8 : 8 + tok, :] = xs_ref[0].astype(F32)


def conv_of(pad_ref, conv_w, conv_b, tok, taps):
    out = conv_b
    for k in range(taps):
        start = 8 - (taps - 1) + k
        out = out + conv_w[k : k + 1, :] * pad_ref[start : start + tok, :]
    return out


def picked(end_ref, kept_ref, coming_ref):
    kept, coming = kept_ref[...], coming_ref[...]
    return jnp.where(end_ref[0] == 1, coming, kept).astype(F32)


def partial_rows(value):
    return jnp.sum(value.reshape(value.shape[0] // 8, 8, value.shape[1]), axis=0)


def to_scan_order(value, tmp_ref, dst_ref):
    tok, chans = value.shape
    steps = tok // CHUNKS
    for j in range(chans // LANE):
        tmp_ref[j] = value[:, col(j)]
        for t in range(steps):
            dst_ref[8 * t : 8 * t + 8, col(j)] = tmp_ref[j, pl.ds(t, 8, stride=steps), :]


def to_natural_order(value, tmp_ref, dst_ref):
    tok, chans = value.shape
    steps = tok // CHUNKS
    for j in range(chans // LANE):
        tmp_ref[j] = value[:, col(j)]
        for k in range(CHUNKS):
            for t in range(0, steps, 8):
                dst_ref[k * steps + t : k * steps + t + 8, col(j)] = tmp_ref[
                    j, pl.ds(8 * t + k, 8, stride=8), :
                ]


def pre_kernel(xs_ref, edge_ref, cw_ref, cb_ref, wxp_ref, u_ref, proj_ref, pad, nat, per):
    tok, taps = xs_ref.shape[1], cw_ref.shape[0]
    load_padded(pad, edge_ref, xs_ref, tok)
    conv = conv_of(pad, cw_ref[...], cb_ref[...], tok, taps)
    to_scan_order(conv * sigmoid(conv), nat, per)
    u_low = per[...].astype(BF16)
    u_ref[0] = u_low
    proj_ref[0] = dot(u_low, wxp_ref[...]).astype(BF16)


def lanes_at(j):
    return pl.ds(pl.multiple_of(j * LANE, LANE), LANE)


def rows_at(t):
    return pl.ds(pl.multiple_of(t * 8, 8), 8)


def col(n):
    return slice(n * LANE, (n + 1) * LANE)


def chunk_prefix(prod, value, backwards):
    place = lax.broadcasted_iota(jnp.int32, value.shape, 0)
    for step in (1, 2, 4):
        shift = CHUNKS - step if backwards else step
        keep = place < CHUNKS - step if backwards else place >= step
        prod_far = jnp.where(keep, pltpu.roll(prod, shift, 0), 1.0)
        value_far = jnp.where(keep, pltpu.roll(value, shift, 0), 0.0)
        value = prod * value_far + value
        prod = prod * prod_far
    return value


def sum_prefix(value):
    place = lax.broadcasted_iota(jnp.int32, value.shape, 0)
    for step in (1, 2, 4):
        value = value + jnp.where(place >= step, pltpu.roll(value, step, 0), 0.0)
    return value


def state_kernel(
    cnt_ref, proj_ref, u_ref, wdt_ref, bias_ref, gain_ref, dec_ref, eb_ref,
    delta_ref, normed_ref, sn_ref, einc_ref, csd_ref, pay_ref, bb, du,
    *, rank, states,
):
    tok, chans = u_ref.shape[1], u_ref.shape[2]
    steps = tok // CHUNKS
    value = proj_ref[0]
    scale = lax.rsqrt(segment_rows(value * value, rank, states) + EPS)
    normed = value * scale * gain_ref[...]
    normed_ref[0] = normed
    lane = lax.broadcasted_iota(jnp.int32, value.shape, 1)
    step_low = jnp.where(lane < rank, normed, 0.0).astype(BF16)
    sn_ref[0] = step_low
    pre = dot(step_low, wdt_ref[...]) + bias_ref[...]
    row = lax.broadcasted_iota(jnp.int32, pre.shape, 0)
    place = (row & 7) * steps + (row >> 3)
    live = place < cnt_ref[pl.program_id(0)]
    soft = jnp.maximum(pre, 0.0) + jnp.log(1.0 + jnp.exp(-jnp.abs(pre)))
    delta = jnp.where(live, soft, 0.0)
    delta_ref[0] = delta
    du[...] = delta * u_ref[0].astype(F32)
    bb[...] = dot(split_low(normed), eb_ref[...])

    def tile(j, carry):
        lanes = lanes_at(j)
        dec = [dec_ref[8 * n : 8 * n + 8, lanes] for n in range(states)]

        def step(i, carry):
            ends, total = carry
            for q in range(UNROLL):
                rows = rows_at(i * UNROLL + q)
                d = delta_ref[0, rows, lanes]
                v = du[rows, lanes]
                ends = tuple(
                    jnp.exp2(d * dec[n]) * ends[n] + v * bb[rows, col(n)] for n in range(states)
                )
                total = total + d
            return ends, total

        zero = jnp.zeros((8, LANE), F32)
        ends, total = lax.fori_loop(0, steps // UNROLL, step, ((zero,) * states, zero))
        csd = sum_prefix(total)
        csd_ref[0, :, lanes] = csd
        for n in range(states):
            inc = chunk_prefix(jnp.exp2(dec[n] * total), ends[n], False)
            einc_ref[0, 8 * n : 8 * n + 8, lanes] = inc
            pay_ref[0, n : n + 1, lanes] = inc[7:8, :]
        pay_ref[0, states : states + 8, lanes] = jnp.broadcast_to(csd[7:8, :], (8, LANE))
        return carry

    lax.fori_loop(0, chans // LANE, tile, 0)


def start_states(dec, csd, einc_ref, enter_ref, lanes, states):
    place = lax.broadcasted_iota(jnp.int32, csd.shape, 0)
    before = jnp.where(place >= 1, pltpu.roll(csd, 1, 0), 0.0)
    out = []
    for n in range(states):
        own = jnp.where(place >= 1, pltpu.roll(einc_ref[0, 8 * n : 8 * n + 8, lanes], 1, 0), 0.0)
        out.append(own + jnp.exp2(dec[n] * before) * enter_ref[0, n : n + 1, lanes])
    return tuple(out)


def out_kernel(
    delta_ref, u_ref, normed_ref, dec_ref, einc_ref, csd_ref, enter_ref, z_ref, skip_ref, eb_ref,
    wout_ref, inner_ref, gated_ref, branch_ref, bc, du, per, tmp, *, states,
):
    tok, chans = u_ref.shape[1], u_ref.shape[2]
    steps = tok // CHUNKS
    bc[...] = dot(split_low(normed_ref[0]), eb_ref[...])
    u_val = u_ref[0].astype(F32)
    du[...] = delta_ref[0] * u_val
    per[...] = skip_ref[...] * u_val

    def tile(j, carry):
        lanes = lanes_at(j)
        dec = [dec_ref[8 * n : 8 * n + 8, lanes] for n in range(states)]

        def step(i, hs):
            for q in range(UNROLL):
                rows = rows_at(i * UNROLL + q)
                d = delta_ref[0, rows, lanes]
                v = du[rows, lanes]
                hs = tuple(
                    jnp.exp2(d * dec[n]) * hs[n] + v * bc[rows, col(n)] for n in range(states)
                )
                per[rows, lanes] += tree_sum(
                    hs[n] * bc[rows, col(states + n)] for n in range(states)
                )
            return hs

        first = start_states(dec, csd_ref[0, :, lanes], einc_ref, enter_ref, lanes, states)
        lax.fori_loop(0, steps // UNROLL, step, first)
        return carry

    lax.fori_loop(0, chans // LANE, tile, 0)
    to_natural_order(per[...], tmp, du)
    inner = du[...]
    inner_ref[0] = inner
    z_val = z_ref[0].astype(F32)
    gated = (inner * z_val * sigmoid(z_val)).astype(BF16)
    gated_ref[0] = gated
    branch_ref[...] = dot_nt(gated, wout_ref[...]).astype(BF16)


def back_state_kernel(
    edge_ref, mid_ref, kept_ref, coming_ref, ctl_ref, wout_ref, z_ref, inner_ref, delta_ref, u_ref,
    normed_ref, dec_ref, skip_ref, ec_ref, gskip_in, gain_in,
    gm_ref, gml_ref, gin_ref, gz_ref, sinc_ref, pay_ref, gskip_ref, gain_ref, cb, nat, *, states,
):
    tok, chans = u_ref.shape[1], u_ref.shape[2]
    steps = tok // CHUNKS
    mid = mid_ref[0]
    grad = picked(edge_ref, kept_ref, coming_ref)
    scale = lax.rsqrt(jnp.mean(mid * mid, axis=-1, keepdims=True) + EPS)
    by_mid = mid * grad
    mean = jnp.mean(by_mid, axis=-1, keepdims=True)
    gain_ref[...] = gain_in[...] + partial_rows(by_mid * scale)
    gm = ctl_ref[0].astype(F32) + scale * grad - (scale * scale * scale * mean) * mid
    gm_ref[0] = gm
    gml_ref[0] = gm.astype(BF16)
    gg = dot(gml_ref[0], wout_ref[...])
    cb[...] = dot(split_low(normed_ref[0]), ec_ref[...])
    z_val = z_ref[0].astype(F32)
    sig = sigmoid(z_val)
    gin = gin_ref.at[0]
    to_scan_order(gg * z_val * sig, nat, gin)
    gz_ref[0] = (gg * inner_ref[0] * sig * (1.0 + z_val * (1.0 - sig))).astype(BF16)

    gskip_ref[...] = gskip_in[...] + partial_rows(gin[...] * u_ref[0].astype(F32))

    def tile(j, carry):
        lanes = lanes_at(j)
        dec = [dec_ref[8 * n : 8 * n + 8, lanes] for n in range(states)]

        def step(i, carry):
            flow, total = carry
            for q in range(UNROLL):
                rows = rows_at(steps - 1 - (i * UNROLL + q))
                d = delta_ref[0, rows, lanes]
                g = gin[rows, lanes]
                flow = tuple(
                    jnp.exp2(d * dec[n]) * (flow[n] + g * cb[rows, col(n)]) for n in range(states)
                )
                total = total + d
            return flow, total

        zero = jnp.zeros((8, LANE), F32)
        flow, total = lax.fori_loop(0, steps // UNROLL, step, ((zero,) * states, zero))
        for n in range(states):
            inc = chunk_prefix(jnp.exp2(dec[n] * total), flow[n], True)
            sinc_ref[0, 8 * n : 8 * n + 8, lanes] = inc
            pay_ref[0, n : n + 1, lanes] = inc[0:1, :]
        full = jnp.sum(total, axis=0, keepdims=True)
        pay_ref[0, states : states + 8, lanes] = jnp.broadcast_to(full, (8, LANE))
        return carry

    lax.fori_loop(0, chans // LANE, tile, 0)


def back_kernel(
    delta_ref, u_ref, normed_ref, dec_ref, einc_ref, csd_ref, enter_ref, gin_ref, sinc_ref,
    leave_ref, skip_ref, eb_ref, ebt_ref, wdt_ref, gdec_in, gbias_in,
    gpre_ref, gu_ref, gnorm_ref, gdec_ref, gbias_ref, bc, acc, du, fac, prev, gstep,
    enter8, leave8, logs8,
    *, states,
):
    tok, chans = u_ref.shape[1], u_ref.shape[2]
    steps, tiles = tok // CHUNKS, chans // LANE
    bc[...] = dot(split_low(normed_ref[0]), eb_ref[...])
    du[...] = delta_ref[0] * u_ref[0].astype(F32)
    gu_ref[0] = jnp.zeros((tok, chans), F32)
    gstep[...] = jnp.zeros((tok, chans), F32)
    for n in range(states):
        rows = slice(8 * n, 8 * n + 8)
        enter8[rows, :] = jnp.broadcast_to(enter_ref[0, n : n + 1, :], (8, chans))
        leave8[rows, :] = jnp.broadcast_to(leave_ref[0, n : n + 1, :], (8, chans))
    place = lax.broadcasted_iota(jnp.int32, (8, LANE), 0)
    pairs = [(q, j) for q in range(STATE_BLOCK) for j in range(tiles)]

    def block(i, carry):
        ns = [i * STATE_BLOCK + q for q in range(STATE_BLOCK)]
        rows_of = [rows_at(n) for n in ns]
        at_b = [lanes_at(n) for n in ns]
        at_c = [lanes_at(n + states) for n in ns]
        dec = {(q, j): dec_ref[rows_of[q], col(j)] for q, j in pairs}
        first, last = [], []
        for q, j in pairs:
            csd = csd_ref[0, :, col(j)]
            before = jnp.where(place >= 1, pltpu.roll(csd, 1, 0), 0.0)
            own = jnp.where(place >= 1, pltpu.roll(einc_ref[0, rows_of[q], col(j)], 1, 0), 0.0)
            first.append(own + jnp.exp2(dec[q, j] * before) * enter8[rows_of[q], col(j)])
            after = csd[7:8, :] - csd
            own = jnp.where(place < 7, pltpu.roll(sinc_ref[0, rows_of[q], col(j)], 7, 0), 0.0)
            last.append(own + jnp.exp2(dec[q, j] * after) * leave8[rows_of[q], col(j)])

        def forward(t, hs):
            for r in range(FORWARD_UNROLL):
                rows = rows_at(t * FORWARD_UNROLL + r)
                d = [delta_ref[0, rows, col(j)] for j in range(tiles)]
                v = [du[rows, col(j)] for j in range(tiles)]
                g = [gin_ref[0, rows, col(j)] for j in range(tiles)]
                b = [bc[rows, at] for at in at_b]
                new = []
                for k, (q, j) in enumerate(pairs):
                    a = jnp.exp2(d[j] * dec[q, j])
                    p = a * hs[k]
                    fac[rows, col(k)] = a
                    prev[rows, col(k)] = p
                    new.append(p + v[j] * b[q])
                hs = tuple(new)
                for q in range(STATE_BLOCK):
                    acc[rows, at_c[q]] = tree_sum(hs[q * tiles + j] * g[j] for j in range(tiles))
            return hs

        lax.fori_loop(0, steps // FORWARD_UNROLL, forward, tuple(first))

        def backward(t, carry):
            flow, logs = carry
            for r in range(BACK_UNROLL):
                rows = rows_at(steps - 1 - (t * BACK_UNROLL + r))
                d = [delta_ref[0, rows, col(j)] for j in range(tiles)]
                v = [du[rows, col(j)] for j in range(tiles)]
                g = [gin_ref[0, rows, col(j)] for j in range(tiles)]
                b = [bc[rows, at] for at in at_b]
                c = [bc[rows, at] for at in at_c]
                new_flow, new_logs, grads, scaled = [], [], [], []
                for k, (q, j) in enumerate(pairs):
                    grad = flow[k] + g[j] * c[q]
                    gp = grad * prev[rows, col(k)]
                    new_flow.append(fac[rows, col(k)] * grad)
                    new_logs.append(logs[k] + gp * d[j])
                    scaled.append(gp * dec[q, j])
                    grads.append(grad)
                flow, logs = tuple(new_flow), tuple(new_logs)
                for j in range(tiles):
                    gu_ref[0, rows, col(j)] += tree_sum(
                        grads[q * tiles + j] * b[q] for q in range(STATE_BLOCK)
                    )
                    gstep[rows, col(j)] += tree_sum(
                        scaled[q * tiles + j] for q in range(STATE_BLOCK)
                    )
                for q in range(STATE_BLOCK):
                    acc[rows, at_b[q]] = tree_sum(grads[q * tiles + j] * v[j] for j in range(tiles))
            return flow, logs

        zero = jnp.zeros((8, LANE), F32)
        unused, logs = lax.fori_loop(
            0, steps // BACK_UNROLL, backward, (tuple(last), (zero,) * len(pairs))
        )
        for k, (q, j) in enumerate(pairs):
            logs8[rows_of[q], col(j)] = logs[k]
        return carry

    lax.fori_loop(0, states // STATE_BLOCK, block, 0)
    for n in range(states):
        total = jnp.sum(logs8[8 * n : 8 * n + 8, :], axis=0, keepdims=True)
        gdec_ref[n : n + 1, :] = gdec_in[n : n + 1, :] + total
    delta = delta_ref[0]
    drive = gu_ref[0]
    gdelta = gstep[...] * (1.0 / LOG2E) + drive * u_ref[0].astype(F32)
    gu_ref[0] = drive * delta + skip_ref[...] * gin_ref[0]
    small = delta * (1.0 - delta * (0.5 - delta * (1.0 / 6.0)))
    slope = jnp.where(delta < 0.01, small, 1.0 - jnp.exp(-delta))
    gpre = (gdelta * slope).astype(BF16)
    gpre_ref[0] = gpre
    gbias_ref[...] = gbias_in[...] + partial_rows(gpre.astype(F32))
    gnorm = dot_nt(gpre, wdt_ref[...]) + dot(acc[...].astype(BF16), ebt_ref[...])
    gnorm_ref[0] = gnorm.astype(BF16)


def conv_back_kernel(
    end_ref, kept_ref, coming_ref, proj_ref, gain_ref, gu_ref, wxp_ref, xs_ref, edge_ref, cw_ref,
    cb_ref, ggain_in, gcw_in, gproj_ref, gxs_ref, head_ref, ggain_ref, gcw_ref, pad, per, nat,
    *, rank, states,
):
    tok, taps = xs_ref.shape[1], cw_ref.shape[0]
    grad = picked(end_ref, kept_ref, coming_ref)[0]
    value = proj_ref[0]
    scale = lax.rsqrt(segment_rows(value * value, rank, states) + EPS)
    by_gain = gain_ref[...] * grad
    mean = segment_rows(value * by_gain, rank, states)
    gproj = (scale * by_gain - scale * scale * scale * value * mean).astype(BF16)
    gproj_ref[0] = gproj
    ggain_ref[...] = ggain_in[...] + partial_rows(grad * value * scale)
    to_natural_order(gu_ref[0] + dot_nt(gproj, wxp_ref[...]), per, nat)
    load_padded(pad, edge_ref, xs_ref, tok)
    conv = conv_of(pad, cw_ref[...], cb_ref[...], tok, taps)
    sig = sigmoid(conv)
    gconv = nat[...] * sig * (1.0 + conv * (1.0 - sig))
    for k in range(taps):
        start = 8 - (taps - 1) + k
        gcw_ref[8 * k : 8 * k + 8, :] = gcw_in[8 * k : 8 * k + 8, :] + partial_rows(
            gconv * pad[start : start + tok, :]
        )
    gcw_ref[8 * taps :, :] = gcw_in[8 * taps :, :] + partial_rows(gconv)
    head_ref[0] = gconv[0:8, :]
    pad[0:tok, :] = gconv
    pad[tok : tok + 8, :] = jnp.zeros((8, gconv.shape[1]), F32)
    gxs = cw_ref[taps - 1 : taps, :] * gconv
    for k in range(taps - 1):
        ahead = taps - 1 - k
        gxs = gxs + cw_ref[k : k + 1, :] * pad[ahead : ahead + tok, :]
    gxs_ref[0] = gxs


def ffn_kernel(
    end_ref, x_ref, kept_ref, coming_ref, ctl_ref, w_ref, wd_ref,
    mid_ref, low_ref, hid_ref, gffn_ref, gn_ref, down_ref, gn_acc, down_acc,
):
    step = pl.program_id(0)

    @pl.when(step == 0)
    def _():
        mid = x_ref[0].astype(F32) + picked(end_ref, kept_ref, coming_ref)
        mid_ref[0] = mid
        scale = lax.rsqrt(jnp.mean(mid * mid, axis=-1, keepdims=True) + EPS)
        low_ref[0] = (mid * scale).astype(BF16)

    weight = w_ref[...]
    units = weight.shape[1] // 2
    both = dot(low_ref[0], weight)
    back = dot(ctl_ref[0], wd_ref[...])
    gate, up = both[:, :units], both[:, units:]
    sig = sigmoid(gate)
    act = gate * sig
    hid = (act * up).astype(BF16)
    hid_ref[0] = hid
    ggate = (back * up * (sig * (1.0 + gate - act))).astype(BF16)
    gffn = jnp.concatenate([ggate, (back * act).astype(BF16)], axis=1)
    gffn_ref[0] = gffn
    gn = dot_nt(gffn, weight)
    down = dot_nt(hid, wd_ref[...])

    @pl.when(step == 0)
    def _():
        gn_acc[...] = gn
        down_acc[...] = down

    @pl.when(step > 0)
    def _():
        gn_acc[...] += gn
        down_acc[...] += down

    @pl.when(step == pl.num_programs(0) - 1)
    def _():
        gn_ref[...] = gn_acc[...].astype(BF16)
        down_ref[...] = down_acc[...].astype(BF16)


def add_kernel(end_ref, mid_ref, kept_ref, coming_ref, out_ref):
    out_ref[0] = mid_ref[0] + picked(end_ref, kept_ref, coming_ref)


def in_grad_kernel(
    gxs_ref, ahead_ref, cw_ref, gz_ref, wx_ref, wz_ref, x_ref, gain_in,
    low_ref, gn_ref, gain_ref, *, taps,
):
    tok = gxs_ref.shape[1]
    row = lax.broadcasted_iota(jnp.int32, (8, gxs_ref.shape[2]), 0)
    ahead = ahead_ref[0]
    fix = jnp.zeros((8, gxs_ref.shape[2]), F32)
    for k in range(taps - 1):
        start = 8 - (taps - 1 - k)
        moved = pltpu.roll(ahead, start, 0)
        fix = fix + jnp.where(row >= start, cw_ref[k : k + 1, :] * moved, 0.0)
    main = gxs_ref[0]
    low = jnp.concatenate([main[: tok - 8], main[tok - 8 :] + fix], axis=0).astype(BF16)
    low_ref[0] = low
    gn = dot_nt(low, wx_ref[...]) + dot_nt(gz_ref[0], wz_ref[...])
    x = x_ref[0].astype(F32)
    scale = lax.rsqrt(jnp.mean(x * x, axis=-1, keepdims=True) + EPS)
    gain_ref[...] = gain_in[...] + partial_rows(gn * x * scale)
    gn_ref[...] = gn.astype(BF16)


def end_kernel(end_ref, x_ref, kept_ref, coming_ref, gm_ref, out_ref):
    x = x_ref[0].astype(F32)
    grad = picked(end_ref, kept_ref, coming_ref)
    scale = lax.rsqrt(jnp.mean(x * x, axis=-1, keepdims=True) + EPS)
    mean = jnp.mean(x * grad, axis=-1, keepdims=True)
    out_ref[0] = gm_ref[0] + scale * grad - (scale * scale * scale * mean) * x


def weight_kernel(left_ref, right_ref, out_ref):
    out_ref[...] = dot_tn(left_ref[...], right_ref[...]).astype(BF16)


def part(*shape, at=0):
    return pl.BlockSpec((1,) + shape, lambda i: (i + at,) + (0,) * len(shape))


def slot(*shape, at):
    return pl.BlockSpec((1,) + shape, lambda i: (at,) + (0,) * len(shape))


def same(*shape, at=0):
    return pl.BlockSpec(shape, lambda i: (at,) + (0,) * (len(shape) - 1))


def call(body, count, in_specs, outs, scratch, args, into=None, carry=None):
    into, carry = into or {}, carry or {}
    fixed = len(args)
    kept = sorted(k for k in into if into[k] is not None)
    args = tuple(args) + tuple(into[k] for k in kept)
    in_specs = list(in_specs) + [pl.BlockSpec(memory_space=pl.ANY)] * len(kept)
    aliases = {fixed + i: k for i, k in enumerate(kept)}
    aliases.update({arg: out for out, arg in carry.items()})

    def run(*refs):
        body(*refs[:fixed], *refs[fixed + len(kept) :])

    return pl.pallas_call(
        run,
        grid=(count,),
        in_specs=in_specs,
        out_specs=[spec for spec, kind, shape in outs],
        out_shape=[jax.ShapeDtypeStruct(shape, kind) for spec, kind, shape in outs],
        scratch_shapes=scratch,
        input_output_aliases=aliases,
        compiler_params=pltpu.CompilerParams(vmem_limit_bytes=VMEM_LIMIT),
        cost_estimate=pl.CostEstimate(flops=0, bytes_accessed=0, transcendentals=0),
    )(*args)


class Sum:
    def __init__(self, value, axis):
        self.axis, self.hops, self.kept = axis, 0, value
        if lax.axis_size(axis) != 4:
            self.hops, self.kept = 3, lax.psum(value, axis)
            return
        self.coming = lax.ppermute(value, axis, [(0, 1), (3, 2)])

    def advance(self, tie, mark):
        if self.hops >= 2:
            return
        self.kept = self.kept + tie(self.coming)
        mark(self.kept)
        route = [(1, 0), (2, 3)] if self.hops else [(1, 2), (2, 1)]
        self.coming = lax.ppermute(self.kept, self.axis, route)
        self.hops += 1

    def result(self):
        while self.hops < 2:
            self.advance(lambda v: v, lambda v: None)
        if self.hops == 2:
            place = lax.axis_index(self.axis)
            at_end = jnp.logical_or(place == 0, place == 3)
            self.kept, self.hops = jnp.where(at_end, self.coming, self.kept), 3
        return self.kept

    def pair(self):
        while self.hops < 2:
            self.advance(lambda v: v, lambda v: None)
        return (self.kept, self.coming if self.hops == 2 else self.kept)


def shifted(value, distance):
    size = lax.axis_size("seq")
    route = [(i, i + distance) for i in range(size) if 0 <= i + distance < size]
    return lax.ppermute(value, "seq", route)


class Cube:
    def __init__(self, value, axis):
        self.value, self.axis, self.size, self.bit = value, axis, lax.axis_size(axis), 1
        if self.size & (self.size - 1):
            self.value, self.bit = lax.psum(value, axis), self.size
        self.send()

    def send(self):
        if self.bit < self.size:
            route = [(i, i ^ self.bit) for i in range(self.size)]
            self.coming = lax.ppermute(self.value, self.axis, route)

    def advance(self, tie, mark):
        if self.bit < self.size:
            self.value = self.value + tie(self.coming)
            mark(self.value)
            self.bit *= 2
            self.send()

    def result(self):
        while self.bit < self.size:
            self.advance(lambda v: v, lambda v: None)
        return self.value


class Entering:
    def __init__(self, payload, decay, states, sign):
        self.decay, self.states, self.sign = decay, states, sign
        self.size = lax.axis_size("seq")
        self.reach = min(4, self.size - 1)
        packed = self.pack((payload[:, :states], payload[:, states : states + 1]))
        self.parts = [shifted(packed, sign * k) for k in range(1, self.reach + 1)]
        self.total = None

    def pack(self, pair):
        value, length = pair
        high = lax.optimization_barrier(length.astype(BF16))
        low = (length - high.astype(F32)).astype(BF16)
        return jnp.concatenate([value.astype(BF16), high, low], axis=1)

    def unpack(self, packed):
        whole = packed.astype(F32)
        value, high = whole[:, : self.states], whole[:, self.states : self.states + 1]
        return value, high + whole[:, self.states + 1 :]

    def join(self, far, near):
        return jnp.exp2(self.decay[None] * near[1]) * far[0] + near[0], far[1] + near[1]

    def advance(self, tie, mark):
        total = self.unpack(tie(self.parts[-1]))
        for near in self.parts[-2::-1]:
            total = self.join(total, self.unpack(near))
        self.total = total
        mark(total[0])
        if self.reach < self.size - 1:
            self.coming = shifted(self.pack(total), self.sign * self.reach)

    def result(self):
        if self.total is None:
            self.advance(lambda v: v, lambda v: None)
        while self.reach < self.size - 1:
            self.total = self.join(self.unpack(self.coming), self.total)
            self.reach *= 2
            if self.reach < self.size - 1:
                self.coming = shifted(self.pack(self.total), self.sign * self.reach)
        return self.total[0]


def on_device(
    inputs, lengths, norm1_gain, w_in_x, w_in_z, conv_w, conv_b, w_xproj, dt_gain, b_gain, c_gain,
    w_dt, dt_bias, decay_log, skip_d, w_out, norm2_gain, w_gate, w_up, w_down, cotangent,
):
    batch, tok, width = inputs.shape
    chans = conv_w.shape[1]
    taps = conv_w.shape[0]
    rank, states = dt_gain.shape[0], b_gain.shape[0]
    cols = w_xproj.shape[1]
    per = batch // GROUPS
    rows = per * tok
    groups = range(GROUPS)

    def gather(weight):
        return lax.all_gather(weight, "seq", axis=0, tiled=True)

    gain_one = norm1_gain.astype(F32)[:, None]
    gain_two = norm2_gain.astype(F32)[:, None]
    full_in_x = gather((w_in_x.astype(F32) * gain_one).astype(BF16))
    full_in_z = gather((w_in_z.astype(F32) * gain_one).astype(BF16))
    full_out = gather(w_out.T)
    full_down = gather(w_down.T)
    low_gate = (w_gate.astype(F32) * gain_two).astype(BF16)
    low_up = (w_up.astype(F32) * gain_two).astype(BF16)
    units = tile = w_gate.shape[1]
    full_ffn = gather(jnp.concatenate([low_gate, low_up], axis=1))

    first_place = lax.axis_index("seq") * tok
    counts = jnp.clip(lengths - first_place, 0, tok)
    live = (jnp.arange(tok, dtype=jnp.int32)[None, :] < counts[:, None])[:, :, None]
    decay = -jnp.exp(decay_log)
    decay2 = decay * LOG2E
    dec8 = jnp.repeat(decay2, 8, axis=0)
    k_of = lax.broadcasted_iota(jnp.int32, (2 * cols, 2 * states * LANE), 0) % cols
    c_of = lax.broadcasted_iota(jnp.int32, (2 * cols, 2 * states * LANE), 1) // LANE
    spread = (k_of == c_of + rank).astype(BF16)
    k_of = lax.broadcasted_iota(jnp.int32, (2 * states * LANE, cols), 1)
    c_of = lax.broadcasted_iota(jnp.int32, (2 * states * LANE, cols), 0) // LANE
    gathering = (k_of == c_of + rank).astype(BF16)
    gains = jnp.concatenate([dt_gain, b_gain, c_gain])[None]
    wdt = jnp.pad(w_dt, ((0, cols - rank), (0, 0)))
    cb_row, bias_row, skip_row = conv_b[None], dt_bias[None], skip_d[None]

    def unit(value):
        return value * lax.rsqrt(jnp.mean(value * value, axis=-1, keepdims=True) + EPS)

    edge_in = shifted(inputs[:, tok - 8 :, :], 1)
    edge_low = unit(edge_in.astype(F32)).astype(BF16)
    edge_xs = dot(edge_low.reshape(batch * 8, width), full_in_x).astype(BF16)
    edge_xs = edge_xs.reshape(batch, 8, chans)

    big = (per, tok, chans)
    f32_blk = lambda *s: pltpu.VMEM(s, F32)
    wide = states * LANE
    tmp_blk = pltpu.VMEM((chans // LANE, tok, LANE), F32)

    state = {"last": None}

    def tie(value):
        if state["last"] is None:
            return value
        return lax.optimization_barrier((value, state["last"]))[0]

    def mark(value):
        state["last"] = value

    low1, xs, z, edges, u, proj = {}, {}, {}, {}, {}, {}
    delta, normed, sn, einc, csd, enter, ctl, own = {}, {}, {}, {}, {}, {}, {}, {}
    live_sums = {}

    def scattered(grad):
        return lax.psum_scatter(grad, "seq", scatter_dimension=0, tiled=True)

    ch_place = lax.axis_index("ch")
    at_end = jnp.logical_or(ch_place == 0, ch_place == lax.axis_size("ch") - 1)
    at_end = at_end.astype(jnp.int32).reshape(1)
    smem = pl.BlockSpec(memory_space=pltpu.SMEM)
    whole = lambda *shape: (batch,) + shape
    acc = lambda rows_, width_: jnp.zeros((rows_, width_), F32)
    buf = dict.fromkeys(
        ("inner", "gated", "mid", "low2", "hidden", "gffn", "gm", "gml", "gin", "gz", "sinc", "pay",
         "gpre", "gu1", "gnorm", "gproj", "gxs", "head", "low_xs", "block", "grad_in")
    )
    buf.update(gskip=acc(8, chans), gain2=acc(8, width), gdec=acc(states, chans),
               gbias=acc(8, chans), ggain=acc(8, cols), gcw=acc(8 * (taps + 1), chans),
               gain1=acc(8, width))

    def at_block(b, *shape):
        return slot(*shape, at=b)

    def run(body, b, specs, args, outs, scratch=(), count=1, carry=()):
        specs, args = list(specs), list(args)
        shapes, into, carried = [], {}, {}
        for i, (name, block, kind) in enumerate(outs):
            if name in buf:
                shapes.append((at_block(b, *block), kind, whole(*block)))
                into[i] = buf[name]
            else:
                shapes.append((same(*block), kind, block))
        for name in carry:
            shape = buf[name].shape
            carried[len(shapes)] = len(args)
            specs.append(same(*shape))
            args.append(buf[name])
            shapes.append((same(*shape), F32, shape))
        out = call(body, count, specs, shapes, list(scratch), args, into, carried)
        names = [name for name, block, kind in outs] + list(carry)
        for name, value in zip(names, out):
            buf[name] = value
        return dict(zip(names, out))

    def stage_a(g):
        x = tie(inputs).astype(F32).reshape(rows, width)
        low1[g] = unit(x).astype(BF16)
        xs[g] = dot(low1[g], full_in_x).astype(BF16).reshape(big)
        edges[g] = edge_xs
        u[g], proj_part = call(
            pre_kernel, per,
            [part(tok, chans), part(8, chans), same(taps, chans), same(1, chans), same(chans, cols)],
            [(part(tok, chans), BF16, big), (part(tok, cols), BF16, whole(tok, cols))],
            [f32_blk(tok + 8, chans), tmp_blk, f32_blk(tok, chans)],
            (xs[g], edges[g], conv_w, cb_row, w_xproj),
        )
        mark(proj_part)
        live_sums["p", g] = Sum(proj_part.reshape(rows, cols), "ch")

    def stage_z(g):
        z[g] = dot(tie(low1[g]), full_in_z).astype(BF16).reshape(big)
        mark(z[g])

    def stage_s(g):
        proj[g] = live_sums["p", g].result().astype(F32).reshape(per, tok, cols)
        out = call(
            functools.partial(state_kernel, rank=rank, states=states), per,
            [smem, part(tok, cols), part(tok, chans),
             same(cols, chans), same(1, chans), same(1, cols), same(8 * states, chans),
             same(2 * cols, wide)],
            [(part(tok, chans), F32, big), (part(tok, cols), F32, whole(tok, cols)),
             (part(tok, cols), BF16, whole(tok, cols)),
             (part(8 * states, chans), F32, whole(8 * states, chans)),
             (part(8, chans), F32, whole(8, chans)),
             (part(states + 8, chans), F32, whole(states + 8, chans))],
            [f32_blk(tok, wide), f32_blk(tok, chans)],
            (counts, proj[g], tie(u[g]), wdt, bias_row, gains, dec8, spread[:, :wide]),
        )
        delta[g], normed[g], sn[g], einc[g], csd[g] = out[:5]
        mark(out[5])
        live_sums["e", g] = Entering(out[5], decay2, states, 1)

    def stage_h(g):
        ctl[0] = jnp.where(live, tie(cotangent), 0)
        mark(ctl[0])

    def stage_o(b):
        if 0 not in enter:
            enter[0] = live_sums["e", 0].result()
        out = run(
            functools.partial(out_kernel, states=states), b,
            [at_block(b, tok, chans), at_block(b, tok, chans), at_block(b, tok, cols),
             same(8 * states, chans), at_block(b, 8 * states, chans), at_block(b, 8, chans),
             at_block(b, states, chans), at_block(b, tok, chans), same(1, chans),
             same(2 * cols, 2 * wide), same(width, chans)],
            (delta[0], u[0], normed[0], dec8, einc[0], csd[0], enter[0], tie(z[0]), skip_row, spread,
             full_out),
            [("inner", (tok, chans), F32), ("gated", (tok, chans), BF16), ("branch", (tok, width), BF16)],
            [f32_blk(tok, 2 * wide), f32_blk(tok, chans), f32_blk(tok, chans), tmp_blk],
        )
        del buf["branch"]
        mark(out["branch"])
        live_sums["o", b] = Sum(out["branch"], "ch")

    def stage_f(b):
        kept, coming = live_sums["o", b].pair()
        deep = lambda *shape: pl.BlockSpec((1,) + shape, lambda i: (b, 0, i))
        outs = [
            (at_block(b, tok, width), F32, whole(tok, width)),
            (at_block(b, tok, width), BF16, whole(tok, width)),
            (deep(tok, tile), BF16, whole(tok, units)),
            (deep(tok, 2 * tile), BF16, whole(tok, 2 * units)),
            (same(tok, width), BF16, (tok, width)),
            (same(tok, width, at=b % 2), BF16, (2 * tok, width)),
        ]
        names = ["mid", "low2", "hidden", "gffn"]
        into = {i: buf[name] for i, name in enumerate(names)}
        if b % 2:
            into[5] = live_sums["down", b // 2]
        out = call(
            ffn_kernel, units // tile,
            [smem, at_block(b, tok, width), same(tok, width), same(tok, width),
             at_block(b, tok, width),
             pl.BlockSpec((width, 2 * tile), lambda i: (0, i)),
             pl.BlockSpec((width, tile), lambda i: (0, i))],
            outs, [f32_blk(tok, width), f32_blk(tok, width)],
            (at_end, tie(inputs), kept, coming, ctl[0], full_ffn, full_down),
            into,
        )
        for name, value in zip(names, out):
            buf[name] = value
        mark(out[4])
        live_sums["f", b] = Sum(out[4], "ch")
        live_sums["down", b // 2] = out[5]

    def stage_d(pair):
        live_sums["d", pair] = Sum(tie(live_sums["down", pair]), "ch")

    def row_part(b):
        return pl.BlockSpec((1, tok // 2, width), lambda i: (b, i, 0))

    def stage_q(b):
        kept, coming = live_sums["d", b // 2].pair()
        moved = pl.BlockSpec((tok // 2, width), lambda i: (2 * (b % 2) + i, 0))
        (buf["block"],) = call(
            add_kernel, 2, [smem, row_part(b), moved, moved],
            [(row_part(b), F32, whole(tok, width))], [],
            (at_end, tie(buf["mid"]), kept, coming), {0: buf["block"]},
        )
        mark(buf["block"])

    def flat(value):
        return value.reshape(-1, value.shape[-1])

    def stage_w(name):
        left, right = dict(
            down=lambda: (ctl[0], buf["hidden"]), ffn=lambda: (buf["low2"], buf["gffn"]),
            out=lambda: (buf["gml"], buf["gated"]), in_z=lambda: (low1[0], buf["gz"]),
            in_x=lambda: (low1[0], buf["low_xs"]),
        )[name]()
        left, right = flat(left), flat(right)
        deep, cut, wide_ = left.shape[0], width // WEIGHT_STEPS, right.shape[1]
        (grad,) = call(
            weight_kernel, WEIGHT_STEPS,
            [pl.BlockSpec((deep, cut), lambda i: (0, i)), same(deep, wide_)],
            [(pl.BlockSpec((cut, wide_), lambda i: (i, 0)), BF16, (width, wide_))], [],
            (left, tie(right)),
        )
        mark(grad)
        own[name] = grad

    def stage_t(name):
        grad = tie(own[name])
        mark(grad)
        own[name] = scattered(grad)

    def stage_r(name):
        own[name] = tie(own[name])
        mark(own[name])

    def stage_b(b):
        kept, coming = live_sums["f", b].pair()
        out = run(
            functools.partial(back_state_kernel, states=states), b,
            [smem, at_block(b, tok, width), same(tok, width), same(tok, width),
             at_block(b, tok, width), same(width, chans)]
            + [at_block(b, tok, chans)] * 4
            + [at_block(b, tok, cols), same(8 * states, chans), same(1, chans), same(2 * cols, wide)],
            (at_end, buf["mid"], kept, coming, ctl[0], full_out, z[0], buf["inner"], delta[0],
             tie(u[0]), normed[0], dec8, skip_row, spread[:, wide:]),
            [("gm", (tok, width), F32), ("gml", (tok, width), BF16), ("gin", (tok, chans), F32),
             ("gz", (tok, chans), BF16), ("sinc", (8 * states, chans), F32),
             ("pay", (states + 8, chans), F32)],
            [f32_blk(tok, wide), tmp_blk],
            carry=("gskip", "gain2"),
        )
        mark(out["pay"])
        if b == batch - 1:
            live_sums["l", 0] = Entering(out["pay"], decay2, states, -1)

    def stage_m(b):
        if b == 0:
            live_sums["leave"] = live_sums["l", 0].result()
        out = run(
            functools.partial(back_kernel, states=states), b,
            [at_block(b, tok, chans), at_block(b, tok, chans), at_block(b, tok, cols),
             same(8 * states, chans), at_block(b, 8 * states, chans), at_block(b, 8, chans),
             at_block(b, states, chans), at_block(b, tok, chans), at_block(b, 8 * states, chans),
             at_block(b, states, chans), same(1, chans),
             same(2 * cols, 2 * wide), same(2 * wide, cols), same(cols, chans)],
            (delta[0], tie(u[0]), normed[0], dec8, einc[0], csd[0], enter[0], buf["gin"],
             buf["sinc"], live_sums["leave"], skip_row, spread, gathering, wdt),
            [("gpre", (tok, chans), BF16), ("gu1", (tok, chans), F32), ("gnorm", (tok, cols), BF16)],
            [f32_blk(tok, 2 * wide), f32_blk(tok, 2 * wide), f32_blk(tok, chans),
             f32_blk(tok, STATE_BLOCK * chans), f32_blk(tok, STATE_BLOCK * chans), f32_blk(tok, chans)]
            + [f32_blk(8 * states, chans)] * 3,
            carry=("gdec", "gbias"),
        )
        mark(out["gnorm"])
        if b % 2 == 1:
            live_sums["m", b // 2] = Sum(out["gnorm"][b - 1 : b + 1].reshape(2 * tok, cols), "ch")

    def stage_c(pair):
        kept, coming = live_sums["m", pair].pair()
        kept, coming = kept.reshape(2, tok, cols), coming.reshape(2, tok, cols)
        for b in (2 * pair, 2 * pair + 1):
            out = run(
                functools.partial(conv_back_kernel, rank=rank, states=states), b,
                [smem, at_block(b % 2, tok, cols), at_block(b % 2, tok, cols),
                 at_block(b, tok, cols), same(1, cols), at_block(b, tok, chans),
                 same(chans, cols), at_block(b, tok, chans), at_block(b, 8, chans),
                 same(taps, chans), same(1, chans)],
                (at_end, kept, coming, proj[0], gains, buf["gu1"], w_xproj, tie(xs[0]), edges[0],
                 conv_w, cb_row),
                [("gproj", (tok, cols), BF16), ("gxs", (tok, chans), F32), ("head", (8, chans), F32)],
                [f32_blk(tok + 8, chans), tmp_blk, f32_blk(tok, chans)],
                carry=("ggain", "gcw"),
            )
            mark(out["head"])
        live_sums["fix", pair] = shifted(out["head"][2 * pair : 2 * pair + 2], -1)

    def stage_x(b):
        out = run(
            functools.partial(in_grad_kernel, taps=taps), b,
            [at_block(b, tok, chans), at_block(b % 2, 8, chans), same(taps, chans),
             at_block(b, tok, chans), same(width, chans), same(width, chans),
             at_block(b, tok, width)],
            (buf["gxs"], live_sums["fix", b // 2], conv_w, buf["gz"], full_in_x, full_in_z,
             tie(inputs)),
            [("low_xs", (tok, chans), BF16), ("gn1", (tok, width), BF16)],
            carry=("gain1",),
        )
        del buf["gn1"]
        mark(out["gn1"])
        live_sums["x", b] = Sum(out["gn1"], "ch")

    def stage_e(b):
        kept, coming = live_sums["x", b].pair()
        moved = pl.BlockSpec((tok // 2, width), lambda i: (i, 0))
        (buf["grad_in"],) = call(
            end_kernel, 2, [smem, row_part(b), moved, moved, row_part(b)],
            [(row_part(b), F32, whole(tok, width))], [],
            (at_end, tie(inputs), kept, coming, buf["gm"]), {0: buf["grad_in"]},
        )
        mark(buf["grad_in"])

    def stage_g(name):
        total = jnp.sum(tie(buf["gain1"]), axis=0).reshape(8, width // 8)
        total = lax.psum(total, "ch")
        mark(total)
        live_sums["g"] = total

    def stage_n(name):
        gxproj = dot_tn(flat(buf["gproj"]), tie(flat(u[0])))
        gwdt = dot_tn(flat(sn[0]), flat(buf["gpre"]))[:rank]
        one = lambda v: jnp.sum(v, axis=0, keepdims=True)
        narrow = [live_sums["g"].reshape(width), one(buf["gain2"])[0], one(buf["ggain"])[0]]
        narrow = jnp.concatenate(narrow)
        narrow = jnp.pad(narrow, (0, -narrow.shape[0] % chans)).reshape(-1, chans)
        gcw = jnp.sum(buf["gcw"].reshape(taps + 1, 8, chans), axis=1)
        rows_of = [gxproj, gwdt, buf["gdec"] * decay, gcw, one(buf["gbias"]), one(buf["gskip"]), narrow]
        stacked = jnp.concatenate(rows_of, axis=0).astype(BF16)
        mark(stacked)
        live_sums["n", 0] = Cube(stacked, "seq")
        own["marks"] = [r.shape[0] for r in rows_of]

    stages = dict(
        A=stage_a, Z=stage_z, S=stage_s, O=stage_o, H=stage_h, F=stage_f, D=stage_d, W=stage_w,
        B=stage_b, M=stage_m, C=stage_c, X=stage_x, E=stage_e, Q=stage_q, R=stage_r, N=stage_n, G=stage_g, T=stage_t,
    )
    for step in ORDER:
        rest = step[1:]
        rest = int(rest) if rest.isdigit() else rest
        if step[0].islower():
            live_sums[step[0], rest].advance(tie, mark)
        else:
            stages[step[0]](rest)

    own["stacked"] = live_sums["n", 0].result().astype(F32)
    marks = [0]
    for count in own["marks"]:
        marks.append(marks[-1] + count)
    cut = [own["stacked"][a:b] for a, b in zip(marks[:-1], marks[1:])]
    narrow = cut[6].reshape(-1)
    local = norm1_gain.shape[0]
    at = lax.axis_index("seq") * local
    own_one = lax.dynamic_slice(narrow, (at,), (local,)) / gain_one[:, 0]
    own_two = lax.dynamic_slice(narrow, (width + at,), (local,)) / gain_two[:, 0]
    ggain = narrow[2 * width : 2 * width + cols]
    return (
        buf["block"],
        buf["grad_in"],
        own_one,
        own["in_x"].astype(F32) * gain_one,
        own["in_z"].astype(F32) * gain_one,
        cut[3][:taps],
        cut[3][taps],
        cut[0].T,
        ggain[:rank],
        ggain[rank : rank + states],
        ggain[rank + states :],
        cut[1],
        cut[4][0],
        cut[2],
        cut[5][0],
        own["out"].astype(F32).T,
        own_two,
        own["ffn"][:, :units].astype(F32) * gain_two,
        own["ffn"][:, units:].astype(F32) * gain_two,
        own["down"].astype(F32).T,
    )


def solution(mesh):
    return jax.shard_map(
        on_device,
        mesh=mesh,
        in_specs=(
            P(None, "seq", None),
            P(),
            P("seq"),
            P("seq", "ch"),
            P("seq", "ch"),
            P(None, "ch"),
            P("ch"),
            P("ch", None),
            P(),
            P(),
            P(),
            P(None, "ch"),
            P("ch"),
            P(None, "ch"),
            P("ch"),
            P("ch", "seq"),
            P("seq"),
            P("seq", "ch"),
            P("seq", "ch"),
            P("ch", "seq"),
            P(None, "seq", None),
        ),
        out_specs=(
            P(None, "seq", None),
            P(None, "seq", None),
            P("seq"),
            P("seq", "ch"),
            P("seq", "ch"),
            P(None, "ch"),
            P("ch"),
            P("ch", None),
            P(),
            P(),
            P(),
            P(None, "ch"),
            P("ch"),
            P(None, "ch"),
            P("ch"),
            P("ch", "seq"),
            P("seq"),
            P("seq", "ch"),
            P("seq", "ch"),
            P("ch", "seq"),
        ),
        check_vma=False,
    )
```
